256 devices in a mesh: tile: 64 (over x, z, core), lev: 4 (over y).
Axes of the slice: x: 4, y: 4, z: 8, core: 2. Of those that a mesh axis runs over, the one named last changes fastest.
Arguments:
- cube_field: bfloat16 [128, 294912], P('lev', 'tile'), may hold values from -6 to 6
- margin: bfloat16 [9216, 64, 128], P('tile'), may hold values from -0.75 to 0.75
- pair_owner: int32 [9216], P('tile'), may hold values from 0 to 63, as said below
- pair_block: int32 [9216], P('tile'), may hold values from 0 to 143
- cube_area: float32 [294912], P('tile'), may hold values from 0.5 to 2
- band_area: float32 [768, 1536], P('tile'), may hold values from 0.5 to 2
- wave_order: int32 [768], replicated, may hold values from 0 to 767, each once
- legendre: bfloat16 [768, 2, 384, 384], P(('tile', 'lev')), may hold values from -0.3125 to 0.3125
- gauss_weight: float32 [384], replicated, may hold values from 0.3 to 1.5
- diffusion: float32 [128], replicated, may hold values from 0.3 to 30
Outputs:
- regridded: bfloat16 [128, 294912], P('lev', 'tile')
The draws below stay inside these ranges and needn't reach their ends.
Inputs may be any that keep to these rules, and one draw needn't show every extreme that they name: `pair_owner`: among the pairs of one index of tile, one owner appears at most 6 times; one owner, drawn from the seed, appears exactly 6 times among the pairs of every index of tile. `wave_order`: each wavenumber 0 to 767 stands in exactly one slot.
All inputs are finite; a program needn't handle non-finite values.
Results may differ from the reference program's by a relative error of at most 0.013.
Values may be sent and summed in bfloat16 or wider, within the bound.
A program may use at most 128 MiB of HBM per device.

```python
import math
import jax
import jax.numpy as jnp
from jax import lax

NLAT = 768
NLON = 1536
TRUNC = 766
GB = 128
CB = 64
WAVES = 768
NDEG = 768
LAT_HALF = 384
PAIRS_DEV = 144
PAIRS = 9216
CUBE_CELLS = 294912
FIELDS = 128
CAP = 6
BLK_DEV = 144


def draw_pair_owner(key, part):
    key = jax.random.fold_in(key, 7)
    tile_count = PAIRS // PAIRS_DEV
    hot_owner = jax.random.randint(jax.random.fold_in(key, 1), (), 0, tile_count, dtype=jnp.int32)

    def one_device(target_processor):
        device_key = jax.random.fold_in(key, target_processor + 2)
        first_key, second_key = jax.random.split(device_key)
        chosen = jax.random.permutation(first_key, (tile_count - 1) * CAP)[:PAIRS_DEV - CAP].astype(jnp.int32)
        others = (hot_owner + 1 + chosen // CAP) % tile_count
        owners = jnp.concatenate([jnp.full((CAP,), hot_owner, jnp.int32), others.astype(jnp.int32)])
        shuffle = jax.random.permutation(second_key, PAIRS_DEV)
        return owners[shuffle]
    return jax.vmap(one_device)(jnp.arange(tile_count, dtype=jnp.int32)).reshape(PAIRS).astype(jnp.int32)


def place_ends(values, key, least, top_value):
    place = [jax.random.randint(jax.random.fold_in(key, axis), (), 0, length) for axis, length in enumerate(values.shape)]
    widest = values.shape.index(max(values.shape))
    next_to = place[:widest] + [(place[widest] + 1) % values.shape[widest]] + place[widest + 1:]
    return values.at[tuple(place)].set(least).at[tuple(next_to)].set(top_value)


def levels(key, dims, pieces, low, high):
    factor_of, own = 1.0, jax.random.fold_in(key, 6)
    for axis_at, parts in pieces:
        steps = jnp.exp(jax.random.uniform(jax.random.fold_in(own, axis_at), (parts,), jnp.float32, low / len(pieces), high / len(pieces)))
        factor_of = factor_of * jnp.repeat(steps, dims[axis_at] // parts).reshape([-1 if axis == axis_at else 1 for axis in range(len(dims))])
    return factor_of


def noise(key, shape, spread, most, cuts=(), kind=jnp.bfloat16):
    result = jax.random.normal(key, shape, jnp.float32) * spread
    if len(cuts) > 0:
        result = levels(key, shape, cuts, -0.22, 0.18) * result
    return jnp.clip(result, min=-most, max=most).astype(kind)


def setup_inputs(seed: int = 0) -> dict:
    splits = jax.random.split(jax.random.key(seed), 11)
    cube_field = noise(splits[0], (FIELDS, CUBE_CELLS), 1.0, 6.0, ((0, 4), (1, 64)))
    margin = noise(splits[1], (PAIRS, CB, GB), CB ** -0.5, 0.75, ((0, 64),))
    pair_owner = draw_pair_owner(jax.random.fold_in(splits[10], 71), 0)
    pair_block = place_ends(jax.random.randint(splits[3], (PAIRS,), 0, BLK_DEV), jax.random.fold_in(splits[3], 1), 0, BLK_DEV - 1).astype(jnp.int32)
    cube_area = jnp.clip(jnp.exp(math.log(2.0) - 1.3862944 * jax.random.uniform(splits[4], (CUBE_CELLS,), jnp.float32) ** levels(splits[4], (CUBE_CELLS,), ((0, 64),), -0.2, 0.2)), 0.5, 2.0)
    band_area = jnp.clip(jnp.exp(math.log(2.0) - 1.3862944 * jax.random.uniform(splits[5], (NLAT, NLON), jnp.float32) ** levels(splits[5], (NLAT, NLON), ((0, 64),), -0.2, 0.2)), 0.5, 2.0)
    wave_order = jax.random.permutation(splits[6], WAVES).astype(jnp.int32)
    legendre = noise(splits[7], (WAVES, 2, NDEG // 2, LAT_HALF), LAT_HALF ** -0.5, 0.3125, ((0, 256),))
    gauss_weight = jnp.clip(jnp.exp(jax.random.uniform(splits[8], (LAT_HALF,), jnp.float32, math.log(0.3), math.log(1.5))), 0.3, 1.5)
    diffusion = jnp.clip(jnp.exp(jax.random.uniform(splits[9], (FIELDS,), jnp.float32, math.log(0.3), math.log(30.0))), 0.3, 30.0)
    return dict(cube_field=cube_field, margin=margin, pair_owner=pair_owner, pair_block=pair_block, cube_area=cube_area, band_area=band_area, wave_order=wave_order, legendre=legendre, gauss_weight=gauss_weight, diffusion=diffusion)


def wavenumber_lookup(points, wavenumbers, doubled):
    longitude = jnp.arange(points, dtype=jnp.int32)
    phases = longitude[:, None] * wavenumbers[None, :] % points
    angles = phases.astype(jnp.float32) * (2.0 * math.pi / points)
    norm_scale = 1.0 / math.sqrt(points)
    if doubled:
        weighting = jnp.where(wavenumbers == 0, 1.0, 2.0).astype(jnp.float32) * norm_scale
    else:
        weighting = jnp.full(wavenumbers.shape, norm_scale, jnp.float32)
    return jnp.stack([jnp.cos(angles) * weighting[None, :], -jnp.sin(angles) * weighting[None, :]], axis=-1)

def filter_for(degree, columns_damp, largest):
    inside = degree <= largest
    growth = (degree * (degree + 1)).astype(jnp.float32) / float(largest * (largest + 1))
    return jnp.where(inside[..., None], 1.0 / (1.0 + columns_damp * growth[..., None]), 0.0)

def legendre_pass(spectra, tables, orders, damping, overlay_weight_set, largest):
    half_lat = spectra.shape[0] // 2
    northern = spectra[:half_lat].astype(jnp.float32)
    southern = spectra[half_lat:][::-1].astype(jnp.float32)
    lat_weight = overlay_weight_set[:, None, None]
    symmetric = (lat_weight * (northern + southern)).astype(jnp.bfloat16)
    antisymmetric = (lat_weight * (northern - southern)).astype(jnp.bfloat16)
    even_table = tables[:, 0].astype(jnp.float32)
    odd_table = tables[:, 1].astype(jnp.float32)
    even_coef = jnp.einsum('skj,jsc->skc', even_table, symmetric.astype(jnp.float32), precision=lax.Precision.HIGHEST)
    odd_coef = jnp.einsum('skj,jsc->skc', odd_table, antisymmetric.astype(jnp.float32), precision=lax.Precision.HIGHEST)
    degrees = tables.shape[2]
    degree_even = orders[:, None] + 2 * jnp.arange(degrees, dtype=jnp.int32)[None, :]
    columns_damp = jnp.repeat(damping, 2)
    spec_even = (even_coef * filter_for(degree_even, columns_damp, largest)).astype(jnp.bfloat16)
    spec_odd = (odd_coef * filter_for(degree_even + 1, columns_damp, largest)).astype(jnp.bfloat16)
    even_part = jnp.einsum('skj,skc->jsc', even_table, spec_even.astype(jnp.float32), precision=lax.Precision.HIGHEST)
    odd_part = jnp.einsum('skj,skc->jsc', odd_table, spec_odd.astype(jnp.float32), precision=lax.Precision.HIGHEST)
    upper_half = even_part + odd_part
    lower_half = (even_part - odd_part)[::-1]
    return jnp.concatenate([upper_half, lower_half], axis=0).astype(jnp.bfloat16)

def reference(cube_field, margin, pair_owner, pair_block, cube_area, band_area, wave_order, legendre, gauss_weight, diffusion):
    field_count = cube_field.shape[0]
    per_row = NLON // GB
    block_count = PAIRS // 2
    blocks = cube_field.reshape(field_count, block_count, CB).astype(jnp.float32)
    overlay_weight_set = margin.reshape(block_count, 2, CB, GB).astype(jnp.float32)
    contribution = jnp.einsum('fbc,bkcg->bkfg', blocks, overlay_weight_set, precision=lax.Precision.HIGHEST)
    contribution = contribution.reshape(PAIRS, field_count, GB).astype(jnp.bfloat16)
    target = (pair_owner * BLK_DEV + pair_block).astype(jnp.int32)
    totals = jnp.zeros((NLAT * per_row, field_count, GB), jnp.float32).at[target].add(contribution.astype(jnp.float32))
    band_grid = totals / band_area.reshape(NLAT * per_row, GB)[:, None, :]
    band_grid = band_grid.reshape(NLAT, per_row, field_count, GB).transpose(2, 0, 1, 3).reshape(field_count, NLAT, NLON)
    forward = wavenumber_lookup(NLON, wave_order, False)
    fourier = jnp.einsum('fjx,xsr->sjfr', band_grid, forward, precision=lax.Precision.HIGHEST)
    fourier = fourier.reshape(WAVES, NLAT, field_count * 2).astype(jnp.bfloat16)

    def one_slot(inputs):
        rows_slot, table_slot, order_slot = inputs
        return legendre_pass(rows_slot[:, None], table_slot[None], order_slot[None], diffusion, gauss_weight, TRUNC)[:, 0]
    spectral = lax.map(one_slot, (fourier, legendre, wave_order))
    inverse = wavenumber_lookup(NLON, wave_order, True)
    band_new = jnp.einsum('sjfr,xsr->fjx', spectral.reshape(WAVES, NLAT, field_count, 2).astype(jnp.float32), inverse, precision=lax.Precision.HIGHEST)
    band_new = band_new.astype(jnp.bfloat16)
    band_blocks = band_new.reshape(field_count, NLAT * per_row, GB)
    selected_entries = jnp.take(band_blocks, target, axis=1).astype(jnp.float32)
    return_term_list = jnp.einsum('vqt,qst->qvs', selected_entries, margin.astype(jnp.float32), precision=lax.Precision.HIGHEST)
    summed = return_term_list.reshape(block_count, 2, field_count, CB).sum(axis=1)
    cube_grid = summed / cube_area.reshape(block_count, CB)[:, None, :]
    return cube_grid.transpose(1, 0, 2).reshape(field_count, CUBE_CELLS).astype(jnp.bfloat16)
```

```python
import math

import jax
import jax.numpy as jnp
from jax import lax
from jax.sharding import PartitionSpec as P

TRUNC = 766


def wave_table(points, block, waves):
    def angles(steps):
        phases = waves[:, None] * steps[None, :] % points
        return phases.astype(jnp.float32) * (2.0 * math.pi / points)

    coarse = angles(jnp.arange(points // block, dtype=jnp.int32) * block)
    fine = angles(jnp.arange(block, dtype=jnp.int32))
    scale = 1.0 / math.sqrt(points)
    cos_a, sin_a = jnp.cos(coarse)[:, :, None] * scale, jnp.sin(coarse)[:, :, None] * scale
    cos_b, sin_b = jnp.cos(fine)[:, None, :], jnp.sin(fine)[:, None, :]
    real = (cos_a * cos_b - sin_a * sin_b).astype(jnp.bfloat16)
    imag = -(sin_a * cos_b + cos_a * sin_b).astype(jnp.bfloat16)
    return real.reshape(-1, points), imag.reshape(-1, points)


def shards(
    cube_field,
    margin,
    pair_owner,
    pair_block,
    cube_area,
    band_area,
    wave_order,
    legendre,
    gauss_weight,
    diffusion,
):
    tiles = lax.axis_size("tile")
    levs = lax.axis_size("lev")
    chips = tiles // 2
    tile = lax.axis_index("tile")
    lev = lax.axis_index("lev")
    core = tile % 2
    fields, cell_count = cube_field.shape
    pairs, cells, points = margin.shape
    blocks = pairs // 2
    lat_dev, lons = band_area.shape
    per_row = lons // points
    lats = lat_dev * tiles
    half = lats // 2
    slots = wave_order.shape[0] // tiles
    own_slots = legendre.shape[0]
    same_core = [list(range(c, tiles, 2)) for c in range(2)]
    other_core = [(t, t ^ 1) for t in range(tiles)]

    labels = lax.all_gather(jnp.stack([pair_owner, pair_block]), "tile")
    lat_share = lat_dev // levs
    area_part = lax.dynamic_slice_in_dim(band_area, lev * lat_share, lat_share)
    area = lax.all_gather(area_part, ("tile", "lev"), axis=0, tiled=True)
    tables = lax.all_gather(
        legendre.reshape(own_slots * 2 * half, half), "lev", axis=0, tiled=True
    ).reshape(slots, 2, half, half)

    margin_q = margin.reshape(blocks, 2, cells, points)
    contribution = jnp.einsum(
        "fbc,bkcg->fbkg",
        cube_field.reshape(fields, blocks, cells),
        margin_q,
        preferred_element_type=jnp.float32,
    )
    contribution = contribution.astype(jnp.bfloat16).reshape(fields, pairs, points)
    arrived = lax.all_to_all(
        contribution, "tile", 0, 0, axis_index_groups=same_core, tiled=True
    ).reshape(chips * pairs, points)

    labels = lax.dynamic_index_in_dim(labels.reshape(chips, 2, 2, pairs), core, 1, False)
    owner, block = labels[:, 0].reshape(-1), labels[:, 1].reshape(-1)
    lat = owner * lat_dev + block // per_row
    row = jnp.where(lat < half, lat, lats + half - 1 - lat)
    column = block % per_row
    one_hot = (jnp.arange(lats, dtype=jnp.int32)[:, None] == row[None, :]).astype(jnp.bfloat16)
    in_column = column[:, None, None] == jnp.arange(per_row, dtype=jnp.int32)[None, :, None]
    spread = jnp.where(in_column, arrived[:, None, :], 0).reshape(chips * pairs, lons)
    totals = jnp.dot(one_hot, spread, preferred_element_type=jnp.float32)
    weight = gauss_weight[:, None]
    north = weight * (totals[:half] / area[:half])
    south = weight * (totals[half:] / area[half:][::-1])
    symmetric, antisymmetric = north + south, north - south
    kept = jnp.where(core == 0, symmetric, antisymmetric)
    given = jnp.where(core == 0, antisymmetric, symmetric).astype(jnp.bfloat16)
    folded = (kept + lax.ppermute(given, "tile", other_core).astype(jnp.float32)).astype(
        jnp.bfloat16
    )

    real, imag = wave_table(lons, points, wave_order)
    table = jnp.stack(
        [real.reshape(tiles, slots, lons), imag.reshape(tiles, slots, lons)], axis=1
    ).reshape(tiles * 2 * slots, lons)
    fourier = lax.dot_general(
        table, folded, (((1,), (1,)), ((), ())), preferred_element_type=jnp.float32
    )
    fourier = fourier.astype(jnp.bfloat16).reshape(tiles, 2 * slots, half)
    spectra = lax.all_to_all(fourier, "tile", 0, 0, tiled=True)
    spectra = spectra.reshape(chips, 2, 2, slots, half).transpose(3, 1, 2, 0, 4)
    spectra = spectra.reshape(slots, 2, 2 * fields, half)
    coefficient = jnp.einsum(
        "spmj,spkj->spmk", spectra, tables, preferred_element_type=jnp.float32
    )
    waves = lax.dynamic_slice_in_dim(wave_order, tile * slots, slots)
    damping = lax.dynamic_slice_in_dim(diffusion, lev * fields, fields)
    degree = (
        waves[:, None, None]
        + 2 * jnp.arange(half, dtype=jnp.int32)[None, None, :]
        + jnp.arange(2, dtype=jnp.int32)[None, :, None]
    )
    growth = (degree * (degree + 1)).astype(jnp.float32) / float(TRUNC * (TRUNC + 1))
    response = jnp.where(
        (degree <= TRUNC)[:, :, None, :],
        1.0 / (1.0 + damping[None, None, :, None] * growth[:, :, None, :]),
        0.0,
    )
    spectrum = coefficient.reshape(slots, 2, 2, fields, half) * response[:, :, None]
    spectrum = spectrum.astype(jnp.bfloat16).reshape(slots, 2, 2 * fields, half)
    parts = jnp.einsum("spmk,spkj->spmj", spectrum, tables, preferred_element_type=jnp.float32)
    doubled = jnp.where(waves == 0, 1.0, 2.0).astype(jnp.float32)
    parts = (parts * doubled[:, None, None, None]).astype(jnp.bfloat16)
    parts = parts.reshape(slots, 2, 2, chips, half).transpose(3, 1, 2, 0, 4)
    returned = lax.all_to_all(parts.reshape(tiles, 2 * slots, half), "tile", 0, 0, tiled=True)
    mine = lax.dot_general(
        returned.reshape(tiles * 2 * slots, half),
        table,
        (((0,), (0,)), ((), ())),
        preferred_element_type=jnp.float32,
    )
    theirs = lax.ppermute(mine.astype(jnp.bfloat16), "tile", other_core).astype(jnp.float32)
    even = jnp.where(core == 0, mine, theirs)
    odd = jnp.where(core == 0, theirs, mine)
    band_new = jnp.concatenate([even + odd, even - odd], axis=0).astype(jnp.bfloat16)

    rows = lax.dot_general(
        one_hot, band_new, (((0,), (0,)), ((), ())), preferred_element_type=jnp.float32
    ).reshape(chips * pairs, per_row, points)
    picked = jnp.sum(jnp.where(in_column, rows, 0.0), axis=1).astype(jnp.bfloat16)
    replies = lax.all_to_all(
        picked.reshape(chips, pairs, points), "tile", 0, 0, axis_index_groups=same_core, tiled=True
    )
    cube = jnp.einsum(
        "fbkg,bkcg->fbc",
        replies.reshape(fields, blocks, 2, points),
        margin_q,
        preferred_element_type=jnp.float32,
    )
    cube = cube / cube_area.reshape(blocks, cells)[None]
    return cube.astype(jnp.bfloat16).reshape(fields, cell_count)


def solution(mesh):
    in_specs = (
        P("lev", "tile"),
        P("tile", None, None),
        P("tile"),
        P("tile"),
        P("tile"),
        P("tile", None),
        P(),
        P(("tile", "lev"), None, None, None),
        P(),
        P(),
    )
    out_specs = P("lev", "tile")
    return jax.shard_map(shards, mesh=mesh, in_specs=in_specs, out_specs=out_specs, check_vma=False)
```

```python
import functools
import math

import jax
import jax.numpy as jnp
import numpy as np
from jax import lax
from jax.experimental import pallas as pl
from jax.experimental.pallas import tpu as pltpu
from jax.sharding import PartitionSpec as P

TRUNC = 766
MESH = pl.DeviceIdType.MESH
BF = jnp.bfloat16
F32 = jnp.float32
GROUP = 4
PAD_LAT = 16
VMEM_LIMIT = 56 * 2**20
NT = (((1,), (1,)), ((), ()))
TN = (((0,), (0,)), ((), ()))

XS, ZS, LEVS = 4, 8, 4
CHIPS = XS * ZS
TILES = 2 * CHIPS


def place():
    tile = lax.axis_index("tile")
    return tile, tile // (2 * ZS), (tile // 2) % ZS, tile % 2


def chip_at(x, z):
    return ((x + XS) % XS) * ZS + (z + ZS) % ZS


def greet():
    tile, _, _, _ = place()
    lev = lax.axis_index("lev")
    barrier = pltpu.get_barrier_semaphore()

    def one(step, carry):
        peer = (tile + step) % TILES
        pl.semaphore_signal(barrier, inc=1, device_id=(peer, lev), device_id_type=MESH)
        return carry

    lax.fori_loop(1, TILES, one, 0)
    for step in range(1, LEVS):
        peer = (tile, (lev + step) % LEVS)
        pl.semaphore_signal(barrier, inc=1, device_id=peer, device_id_type=MESH)
    pl.semaphore_wait(barrier, TILES - 1 + LEVS - 1)


def remote(src, dst, send, recv, peer, lev=None):
    return pltpu.make_async_remote_copy(
        src_ref=src,
        dst_ref=dst,
        send_sem=send,
        recv_sem=recv,
        device_id=(peer, lax.axis_index("lev") if lev is None else lev),
        device_id_type=MESH,
    )


def slot_of(tile):
    return (tile % 2) * CHIPS + tile // 2


def cos_sin(phase, turn):
    eighth = turn // 8
    octant = ((phase + eighth).astype(F32) * (4.0 / turn) + 0.5 / turn).astype(jnp.int32)
    angle = (phase - octant * (turn // 4)).astype(F32) * (2.0 * math.pi / turn)
    square = angle * angle
    cos = 1.0 + square * (
        -1 / 2 + square * (1 / 24 + square * (-1 / 720 + square * (1 / 40320)))
    )
    sin = angle * (
        1.0 + square * (-1 / 6 + square * (1 / 120 + square * (-1 / 5040 + square * (1 / 362880))))
    )
    odd = octant % 2 == 1
    base_c, base_s = jnp.where(odd, sin, cos), jnp.where(odd, cos, sin)
    flip_c = (octant == 1) | (octant == 2)
    flip_s = (octant == 2) | (octant == 3)
    return jnp.where(flip_c, -base_c, base_c), jnp.where(flip_s, -base_s, base_s)


def wrap(count, turn):
    return count - ((count.astype(F32) + 0.5) * (1.0 / turn)).astype(jnp.int32) * turn


def down_rows(row, width):
    first = lax.broadcasted_iota(jnp.int32, (16, row.shape[1]), 0) == 0
    spread = jnp.where(first, row.astype(F32), 0.0).astype(BF)
    return lax.dot_general(spread, jnp.ones((16, width), BF), TN, preferred_element_type=F32)


def to_spectra(
    chunks,
    codes,
    area_part,
    pick_rows,
    wave_rows,
    spectra,
    table_any,
    code_rows,
    arrived,
    code_in,
    totals,
    area,
    table,
    given,
    taken,
    folded,
    fourier,
    pair_send,
    pair_recv,
    swap_send,
    swap_recv,
    wave_send,
    wave_recv,
    code_send,
    code_recv,
    area_send,
    area_recv,
    local_sem,
):
    tile, x, z, core = place()
    lev = lax.axis_index("lev")
    chip = tile // 2
    partner = tile + 1 - 2 * core
    lats, lons = totals.shape
    half = lats // 2
    pairs, points = arrived.shape[1:]
    rows = GROUP * pairs
    per_row = lons // points
    greet()

    area[lev, core, chip] = area_part[...]

    def area_z(step):
        there = chip_at(x, z + step)
        here = area.at[lev, core, chip]
        sems = area_send.at[step], area_recv.at[step]
        return remote(here, here, *sems, 2 * there + core)

    def area_x(step):
        there = chip_at(x + step, z)
        here = area.at[lev, core, pl.ds(pl.multiple_of(x * ZS, ZS), ZS)]
        sems = area_send.at[ZS + step], area_recv.at[ZS + step]
        return remote(here, here, *sems, 2 * there + core)

    def area_y(step):
        here = area.at[lev, core]
        sems = area_send.at[ZS + XS + step], area_recv.at[ZS + XS + step]
        return remote(here, here, *sems, tile, (lev + step) % LEVS)

    def area_core(q):
        here = area.at[q, core]
        at = ZS + XS + LEVS + q
        return remote(here, here, area_send.at[at], area_recv.at[at], partner)

    for step in range(1, ZS):
        area_z(step).start()

    def code_copy(slot):
        there = chip_at(x + slot // ZS, z + slot % ZS)
        return remote(
            codes.at[slot % GROUP],
            code_in.at[slot],
            code_send.at[slot],
            code_recv.at[slot],
            2 * there + core,
        )

    def start_code(slot, carry):
        code_copy(slot).start()
        return carry

    lax.fori_loop(1, CHIPS, start_code, 0)
    code_in[0] = codes[0]

    def pair_copy(slot):
        there = chip_at(x + slot // ZS, z + slot % ZS)
        return remote(
            chunks.at[there],
            arrived.at[slot],
            pair_send.at[slot],
            pair_recv.at[slot],
            2 * there + core,
        )

    def start_pair(slot, carry):
        pair_copy(slot).start()
        return carry

    lax.fori_loop(1, CHIPS, start_pair, 0)
    arrived[0] = chunks[chip]

    strip = 64
    longitude = lax.broadcasted_iota(jnp.int32, (strip, points), 1)
    norm = 1.0 / math.sqrt(lons)

    def make_rows(step, carry):
        at = pl.ds(pl.multiple_of(step * strip, strip), strip)
        code = wave_rows[at, :]
        wave, part = code % 1024, code // 1024
        cos, sin = cos_sin(wrap(wave * longitude + part * (lons // 4), lons), lons)
        cos, sin = cos * norm, sin * norm
        turn_c, turn_s = cos_sin(wrap(wave * points, lons), lons)
        for block in range(per_row):
            table[at, block * points : (block + 1) * points] = cos.astype(BF)
            cos, sin = cos * turn_c - sin * turn_s, sin * turn_c + cos * turn_s
        return carry

    lax.fori_loop(0, table.shape[0] // strip, make_rows, 0)
    table_copy = pltpu.make_async_copy(table, table_any, local_sem.at[1])
    table_copy.start()

    for step in range(1, ZS):
        area_z(step).wait_recv()
    for step in range(1, XS):
        area_x(step).start()

    lat_index = lax.broadcasted_iota(jnp.int32, (lats, rows), 0)

    def add_group(group, first):
        for j in range(GROUP):
            if not (first and j == 0):
                code_copy(group * GROUP + j).wait_recv()
                pair_copy(group * GROUP + j).wait_recv()
        code = code_in[group * GROUP]
        for j in range(1, GROUP):
            code = code + code_in[group * GROUP + j]
        code_rows[group] = code
        code = code[:, :rows]
        one_hot = jnp.where(lat_index == code // 16, 1.0, 0.0).astype(BF)
        values = arrived[pl.ds(group * GROUP, GROUP)].reshape(rows, points)
        where = down_rows(code % 16, points).astype(BF)
        for b in range(0, per_row, 2):
            spread = jnp.concatenate(
                [jnp.where(where == float(b + i), values, jnp.zeros_like(values)) for i in range(2)],
                axis=1,
            )
            term = jnp.dot(one_hot, spread, preferred_element_type=F32)
            at = slice(b * points, (b + 2) * points)
            if first:
                totals[:, at] = term
            else:
                totals[:, at] += term

    def later_group(group, carry):
        add_group(group, False)
        return carry

    add_group(0, True)
    for step in range(1, XS):
        area_x(step).wait_recv()
    for step in range(1, LEVS):
        area_y(step).start()
    lax.fori_loop(1, 4, later_group, 0)
    for step in range(1, LEVS):
        area_y(step).wait_recv()
    for q in range(LEVS):
        area_core(q).start()
    lax.fori_loop(4, CHIPS // GROUP, later_group, 0)
    for q in range(LEVS):
        area_core(q).wait_recv()

    sign = (1 - 2 * core).astype(F32)
    quarters = LEVS
    width = lons // LEVS

    def weights(q, side):
        found = []
        for c in range(2):
            part = area[q, c, side * (CHIPS // 2) : (side + 1) * (CHIPS // 2)]
            part = part.reshape(-1, width)
            found.append(jnp.dot(pick_rows[side, c], part, preferred_element_type=F32))
        return found[0] + found[1]

    def swap_copy(q):
        return remote(
            given.at[q], taken.at[q], swap_send.at[q], swap_recv.at[q], partner
        )

    for q in range(quarters):
        at = slice(q * width, (q + 1) * width)
        north = totals[:half, at] * weights(q, 0)
        south = totals[half:, at] * weights(q, 1) * sign
        totals[:half, at] = north + south
        given[q] = (north - south).astype(BF)
        swap_copy(q).start()
    for q in range(quarters):
        at = slice(q * width, (q + 1) * width)
        swap_copy(q).wait_recv()
        folded[:, at] = (totals[:half, at] + taken[q].astype(F32)).astype(BF)

    share = fourier.shape[1]
    batch = ZS

    def wave_copy(peer):
        return remote(
            fourier.at[peer],
            spectra.at[slot_of(tile)],
            wave_send.at[peer],
            wave_recv.at[tile],
            peer,
        )

    def transform(step, carry):
        first = ((x + step // 2) % XS) * (2 * ZS) + ((z // (ZS // 2) + step) % 2) * batch
        at = pl.ds(pl.multiple_of(first * share, batch * share), batch * share)
        part = lax.dot_general(table[at, :], folded[...], NT, preferred_element_type=F32)
        fourier[pl.ds(first, batch)] = part.astype(BF).reshape(batch, share, half)
        for j in range(batch):
            peer = first + j

            @pl.when(peer != tile)
            def _():
                wave_copy(peer).start()

        return carry

    lax.fori_loop(0, TILES // batch, transform, 0)
    spectra[slot_of(tile)] = fourier[tile]

    def finish_wave(step, carry):
        peer = (tile + step) % TILES
        wave_copy(peer).wait_send()
        remote(
            fourier.at[peer],
            spectra.at[slot_of(peer)],
            wave_send.at[peer],
            wave_recv.at[peer],
            peer,
        ).wait_recv()
        return carry

    lax.fori_loop(1, TILES, finish_wave, 0)

    def finish_pair(slot, carry):
        pair_copy(slot).wait_send()
        return carry

    lax.fori_loop(1, CHIPS, finish_pair, 0)
    def finish_code(slot, carry):
        code_copy(slot).wait_send()
        return carry

    lax.fori_loop(1, CHIPS, finish_code, 0)
    for q in range(quarters):
        swap_copy(q).wait_send()
        area_core(q).wait_send()
    for step in range(1, ZS):
        area_z(step).wait_send()
    for step in range(1, XS):
        area_x(step).wait_send()
    for step in range(1, LEVS):
        area_y(step).wait_send()
    table_copy.wait()


def from_spectra(
    spectra,
    order,
    back_order,
    tables_any,
    response,
    table_any,
    code_rows,
    replies,
    tables,
    table,
    sorted_in,
    sorted_out,
    parts,
    returned,
    wide,
    given,
    taken,
    band,
    picked,
    wave_send,
    wave_recv,
    swap_send,
    swap_recv,
    pair_send,
    pair_recv,
    local_sem,
):
    tile, x, z, core = place()
    chip = tile // 2
    slots = tables.shape[0]
    half, lons = wide.shape
    pairs, points = picked.shape[1:]
    rows = GROUP * pairs
    per_row = lons // points
    share = parts.shape[1]
    mixed = 2 * CHIPS
    locals_in = [
        pltpu.make_async_copy(tables_any, tables, local_sem.at[0]),
        pltpu.make_async_copy(table_any, table, local_sem.at[1]),
    ]
    for copy in locals_in:
        copy.start()
    greet()

    for p in range(2):
        sorted_in[p] = jnp.dot(order[...], spectra[p], preferred_element_type=F32).astype(BF)
    locals_in[0].wait()

    def one_slot(slot, carry):
        at = pl.ds(pl.multiple_of(slot * mixed, mixed), mixed)
        for p in range(2):
            legendre = tables[slot, p]
            coefficient = lax.dot_general(
                sorted_in[p, at, :], legendre, NT, preferred_element_type=F32
            )
            scale = response[slot, p]
            spectrum = jnp.concatenate(
                [coefficient[:CHIPS] * scale, coefficient[CHIPS:] * scale], axis=0
            ).astype(BF)
            sorted_out[p, at, :] = jnp.dot(
                spectrum, legendre, preferred_element_type=F32
            ).astype(BF)
        return carry

    lax.fori_loop(0, slots, one_slot, 0)

    def wave_copy(peer):
        return remote(
            parts.at[peer], returned.at[tile], wave_send.at[peer], wave_recv.at[tile], peer
        )

    def send_back(step, carry):
        first = ((x + step) % XS) * ZS
        at = pl.ds(pl.multiple_of(first * share, ZS * share), ZS * share)
        for p in range(2):
            part = jnp.dot(back_order[at, :], sorted_out[p], preferred_element_type=F32)
            part = part.astype(BF).reshape(ZS, share, half)
            for j in range(ZS):
                peer = 2 * (first + j) + p
                parts[peer] = part[j]

                @pl.when(peer != tile)
                def _():
                    wave_copy(peer).start()

        return carry

    lax.fori_loop(0, XS, send_back, 0)
    returned[tile] = parts[tile]
    locals_in[1].wait()

    def wave_arrival(peer):
        return remote(
            parts.at[peer], returned.at[peer], wave_send.at[peer], wave_recv.at[peer], peer
        )

    def inverse(step):
        first = ((x + XS - step) % XS) * (2 * ZS)

        def wait_one(j, carry):
            @pl.when(first + j != tile)
            def _():
                wave_arrival(first + j).wait_recv()

            return carry

        lax.fori_loop(0, 2 * ZS, wait_one, 0)
        values = returned[pl.ds(first, 2 * ZS)].reshape(2 * ZS * share, half)
        at = pl.ds(pl.multiple_of(first * share, 2 * ZS * share), 2 * ZS * share)
        for c in range(0, lons, 512):
            term = lax.dot_general(
                values, table[at, c : c + 512], TN, preferred_element_type=F32
            )
            if step == 0:
                wide[:, c : c + 512] = term
            else:
                wide[:, c : c + 512] += term

    for step in range(XS):
        inverse(step)

    partner = tile + 1 - 2 * core
    sign = (1 - 2 * core).astype(F32)
    quarters = given.shape[0]
    width = given.shape[2]

    def swap_copy(q):
        return remote(
            given.at[q], taken.at[q], swap_send.at[q], swap_recv.at[q], partner
        )

    for q in range(quarters):
        given[q] = wide[:, q * width : (q + 1) * width].astype(BF)
        swap_copy(q).start()
    for q in range(quarters):
        at = slice(q * width, (q + 1) * width)
        swap_copy(q).wait_recv()
        mine, theirs = wide[:, at], taken[q].astype(F32)
        band[:half, at] = (mine + theirs).astype(BF)
        band[half:, at] = ((mine - theirs) * sign).astype(BF)

    def pair_copy(slot):
        there = chip_at(x - slot // ZS, z - slot % ZS)
        return remote(
            picked.at[slot],
            replies.at[chip],
            pair_send.at[slot],
            pair_recv.at[chip],
            2 * there + core,
        )

    lat_index = lax.broadcasted_iota(jnp.int32, (rows, points), 1).astype(F32)

    def answer(group, carry):
        code = code_rows[group][:, :rows]
        lat = code // 16
        lat = down_rows(lat // points, points) * points + down_rows(lat % points, points)
        one_hot = jnp.concatenate(
            [
                jnp.where(lat == lat_index + float(c), 1.0, 0.0).astype(BF)
                for c in range(0, 2 * half, points)
            ],
            axis=1,
        )
        where = down_rows(code % 16, points).astype(BF)
        chosen = jnp.zeros((rows, points), BF)
        for b in range(0, per_row, 2):
            found = jnp.dot(
                one_hot, band[:, b * points : (b + 2) * points], preferred_element_type=F32
            ).astype(BF)
            for i in range(2):
                chosen = jnp.where(
                    where == float(b + i), found[:, i * points : (i + 1) * points], chosen
                )
        picked[pl.ds(group * GROUP, GROUP)] = chosen.reshape(GROUP, pairs, points)
        for j in range(GROUP):
            slot = group * GROUP + j

            @pl.when(slot != 0)
            def _():
                pair_copy(slot).start()

        return carry

    lax.fori_loop(0, CHIPS // GROUP, answer, 0)
    replies[chip] = picked[0]

    def finish_pair(slot, carry):
        pair_copy(slot).wait_send()
        here = chip_at(x - slot // ZS, z - slot % ZS)
        remote(
            picked.at[slot],
            replies.at[here],
            pair_send.at[slot],
            pair_recv.at[here],
            2 * here + core,
        ).wait_recv()
        return carry

    lax.fori_loop(1, CHIPS, finish_pair, 0)

    def finish_wave(step, carry):
        wave_copy((tile + step) % TILES).wait_send()
        return carry

    lax.fori_loop(1, TILES, finish_wave, 0)
    for q in range(quarters):
        swap_copy(q).wait_send()


def slot_orders(slots):
    chip, part, slot = np.meshgrid(
        np.arange(CHIPS), np.arange(2), np.arange(slots), indexing="ij"
    )
    source = ((chip * 2 + part) * slots + slot).reshape(-1)
    target = ((slot * 2 + part) * CHIPS + chip).reshape(-1)
    order = np.zeros((source.size, source.size), np.float32)
    order[target, source] = 1.0
    return jnp.asarray(order, BF), jnp.asarray(order.T.copy(), BF)


def lat_picks(lat_dev, half):
    picks = np.zeros((2, 2, half, CHIPS // 2 * PAD_LAT), np.float32)
    for tile in range(TILES):
        for i in range(lat_dev):
            lat = tile * lat_dev + i
            side = int(lat >= half)
            to = lat if side == 0 else 2 * half - 1 - lat
            picks[side, tile % 2, to, (tile // 2) % (CHIPS // 2) * PAD_LAT + i] = 1.0
    return jnp.asarray(picks, BF)


def shards(
    cube_field,
    margin,
    pair_owner,
    pair_block,
    cube_area,
    band_area,
    wave_order,
    legendre,
    gauss_weight,
    diffusion,
):
    levs = lax.axis_size("lev")
    tile, x, z, core = place()
    lev = lax.axis_index("lev")
    fields, cell_count = cube_field.shape
    pairs, cells, points = margin.shape
    blocks = pairs // 2
    lat_dev, lons = band_area.shape
    per_row = lons // points
    lats = lat_dev * TILES
    half = lats // 2
    slots = wave_order.shape[0] // TILES
    own_slots = legendre.shape[0]
    share = 2 * slots
    width = lons // levs
    groups = CHIPS // GROUP

    lat = pair_owner * lat_dev + pair_block // per_row
    row = jnp.where(lat < half, lat, lats + half - 1 - lat)
    code = row * 16 + pair_block % per_row
    room = -(-GROUP * pairs // points) * points
    codes = jnp.stack(
        [jnp.pad(code, (j * pairs, room - (j + 1) * pairs))[None] for j in range(GROUP)]
    )

    own_lat = tile * lat_dev + jnp.arange(lat_dev, dtype=jnp.int32)
    own_weight = gauss_weight[jnp.where(own_lat < half, own_lat, lats - 1 - own_lat)]
    part = lax.dynamic_slice_in_dim(band_area, lev * width, width, axis=1)
    part = (own_weight[:, None] / part).astype(BF)
    area_part = jnp.pad(part, ((0, PAD_LAT - lat_dev), (0, 0)))
    tables = lax.all_gather(
        legendre.reshape(own_slots * 2 * half, half), "lev", axis=0, tiled=True
    ).reshape(slots, 2, half, half)

    margin_q = margin.reshape(blocks, 2, cells, points)
    chunks = jnp.einsum(
        "fbc,bkcg->fbkg",
        cube_field.reshape(fields, blocks, cells),
        margin_q,
        preferred_element_type=F32,
    )
    chunks = chunks.astype(BF).reshape(fields, pairs, points)

    parts = jnp.arange(2, dtype=jnp.int32)[None, :, None] * 1024
    wave_rows = (wave_order.reshape(TILES, 1, slots) + parts).reshape(-1, 1)
    wave_rows = jnp.broadcast_to(wave_rows, (TILES * share, points))

    waves = lax.dynamic_slice_in_dim(wave_order, tile * slots, slots)
    damping = lax.dynamic_slice_in_dim(diffusion, lev * fields, fields)
    degree = (
        waves[:, None, None]
        + 2 * jnp.arange(half, dtype=jnp.int32)[None, None, :]
        + jnp.arange(2, dtype=jnp.int32)[None, :, None]
    )
    growth = (degree * (degree + 1)).astype(F32) / float(TRUNC * (TRUNC + 1))
    doubled = jnp.where(waves == 0, 1.0, 2.0).astype(F32)[:, None, None, None]
    response = jnp.where(
        (degree <= TRUNC)[:, :, None, :],
        doubled / (1.0 + damping[None, None, :, None] * growth[:, :, None, :]),
        0.0,
    )

    vmem = pl.BlockSpec(memory_space=pltpu.VMEM)
    anywhere = pl.BlockSpec(memory_space=pl.ANY)
    dma = pltpu.SemaphoreType.DMA
    spectra, table, code_rows = pl.pallas_call(
        to_spectra,
        out_shape=(
            jax.ShapeDtypeStruct((TILES, share, half), BF),
            jax.ShapeDtypeStruct((TILES * share, lons), BF),
            jax.ShapeDtypeStruct((groups, 1, room), jnp.int32),
        ),
        in_specs=[vmem] * 5,
        out_specs=(vmem, anywhere, vmem),
        scratch_shapes=[
            pltpu.VMEM((CHIPS, pairs, points), BF),
            pltpu.VMEM((CHIPS, 1, room), jnp.int32),
            pltpu.VMEM((lats, lons), F32),
            pltpu.VMEM((levs, 2, CHIPS, PAD_LAT, width), BF),
            pltpu.VMEM((TILES * share, lons), BF),
            pltpu.VMEM((levs, half, width), BF),
            pltpu.VMEM((levs, half, width), BF),
            pltpu.VMEM((half, lons), BF),
            pltpu.VMEM((TILES, share, half), BF),
            dma((CHIPS,)),
            dma((CHIPS,)),
            dma((levs,)),
            dma((levs,)),
            dma((TILES,)),
            dma((TILES,)),
            dma((CHIPS,)),
            dma((CHIPS,)),
            dma((ZS + XS + 2 * LEVS,)),
            dma((ZS + XS + 2 * LEVS,)),
            dma((2,)),
        ],
        compiler_params=pltpu.CompilerParams(
            collective_id=0, has_side_effects=True, vmem_limit_bytes=VMEM_LIMIT
        ),
    )(chunks, codes, area_part, lat_picks(lat_dev, half), wave_rows)

    order, back_order = slot_orders(slots)
    mixed = CHIPS * share
    replies = pl.pallas_call(
        from_spectra,
        out_shape=jax.ShapeDtypeStruct((CHIPS, pairs, points), BF),
        in_specs=[vmem, vmem, vmem, anywhere, vmem, anywhere, vmem],
        out_specs=vmem,
        scratch_shapes=[
            pltpu.VMEM((slots, 2, half, half), BF),
            pltpu.VMEM((TILES * share, lons), BF),
            pltpu.VMEM((2, mixed, half), BF),
            pltpu.VMEM((2, mixed, half), BF),
            pltpu.VMEM((TILES, share, half), BF),
            pltpu.VMEM((TILES, share, half), BF),
            pltpu.VMEM((half, lons), F32),
            pltpu.VMEM((levs, half, width), BF),
            pltpu.VMEM((levs, half, width), BF),
            pltpu.VMEM((lats, lons), BF),
            pltpu.VMEM((CHIPS, pairs, points), BF),
            dma((TILES,)),
            dma((TILES,)),
            dma((levs,)),
            dma((levs,)),
            dma((CHIPS,)),
            dma((CHIPS,)),
            dma((2,)),
        ],
        compiler_params=pltpu.CompilerParams(
            collective_id=1, has_side_effects=True, vmem_limit_bytes=VMEM_LIMIT
        ),
    )(
        spectra.reshape(2, mixed, half),
        order,
        back_order,
        tables,
        response,
        table,
        code_rows,
    )

    cube = jnp.einsum(
        "fbkg,bkcg->fbc",
        replies.reshape(fields, blocks, 2, points),
        margin_q,
        preferred_element_type=F32,
    )
    cube = cube / cube_area.reshape(blocks, cells)[None]
    return cube.astype(BF).reshape(fields, cell_count)


def solution(mesh):
    in_specs = (
        P("lev", "tile"),
        P("tile", None, None),
        P("tile"),
        P("tile"),
        P("tile"),
        P("tile", None),
        P(),
        P(("tile", "lev"), None, None, None),
        P(),
        P(),
    )
    out_specs = P("lev", "tile")
    return jax.shard_map(shards, mesh=mesh, in_specs=in_specs, out_specs=out_specs, check_vma=False)
```

```python
import functools
import math

import jax
import jax.numpy as jnp
import numpy as np
from jax import lax
from jax.experimental import pallas as pl
from jax.experimental.pallas import tpu as pltpu
from jax.sharding import PartitionSpec as P

TRUNC = 766
MESH = pl.DeviceIdType.MESH
BF = jnp.bfloat16
F32 = jnp.float32
GROUP = 4
PAD_LAT = 16
VMEM_LIMIT = 56 * 2**20
NT = (((1,), (1,)), ((), ()))
TN = (((0,), (0,)), ((), ()))

XS, ZS, LEVS = 4, 8, 4
CHIPS = XS * ZS
TILES = 2 * CHIPS


def place():
    tile = lax.axis_index("tile")
    return tile, tile // (2 * ZS), (tile // 2) % ZS, tile % 2


def chip_at(x, z):
    return ((x + XS) % XS) * ZS + (z + ZS) % ZS


def greet():
    tile, _, _, _ = place()
    lev = lax.axis_index("lev")
    barrier = pltpu.get_barrier_semaphore()

    def one(step, carry):
        peer = (tile + step) % TILES
        pl.semaphore_signal(barrier, inc=1, device_id=(peer, lev), device_id_type=MESH)
        return carry

    lax.fori_loop(1, TILES, one, 0)
    for step in range(1, LEVS):
        peer = (tile, (lev + step) % LEVS)
        pl.semaphore_signal(barrier, inc=1, device_id=peer, device_id_type=MESH)
    pl.semaphore_wait(barrier, TILES - 1 + LEVS - 1)


def remote(src, dst, send, recv, peer, lev=None):
    return pltpu.make_async_remote_copy(
        src_ref=src,
        dst_ref=dst,
        send_sem=send,
        recv_sem=recv,
        device_id=(peer, lax.axis_index("lev") if lev is None else lev),
        device_id_type=MESH,
    )


def slot_of(tile):
    return (tile % 2) * CHIPS + tile // 2


def cos_sin(phase, turn):
    eighth = turn // 8
    octant = ((phase + eighth).astype(F32) * (4.0 / turn) + 0.5 / turn).astype(jnp.int32)
    angle = (phase - octant * (turn // 4)).astype(F32) * (2.0 * math.pi / turn)
    square = angle * angle
    cos = 1.0 + square * (
        -1 / 2 + square * (1 / 24 + square * (-1 / 720 + square * (1 / 40320)))
    )
    sin = angle * (
        1.0 + square * (-1 / 6 + square * (1 / 120 + square * (-1 / 5040 + square * (1 / 362880))))
    )
    odd = octant % 2 == 1
    base_c, base_s = jnp.where(odd, sin, cos), jnp.where(odd, cos, sin)
    flip_c = (octant == 1) | (octant == 2)
    flip_s = (octant == 2) | (octant == 3)
    return jnp.where(flip_c, -base_c, base_c), jnp.where(flip_s, -base_s, base_s)


def wrap(count, turn):
    return count - ((count.astype(F32) + 0.5) * (1.0 / turn)).astype(jnp.int32) * turn


def down_rows(row, width):
    first = lax.broadcasted_iota(jnp.int32, (16, row.shape[1]), 0) == 0
    spread = jnp.where(first, row.astype(F32), 0.0).astype(BF)
    return lax.dot_general(spread, jnp.ones((16, width), BF), TN, preferred_element_type=F32)


def regrid(
    chunks,
    codes,
    area_part,
    pick_rows,
    wave_codes,
    wave_order,
    damping,
    legendre,
    order,
    back_order,
    replies,
    arrived,
    code_in,
    code_rows,
    totals,
    area,
    table,
    tables,
    response,
    given,
    taken,
    folded,
    fourier,
    spectra,
    sorted_in,
    sorted_out,
    parts,
    returned,
    wide,
    sent_back,
    got_back,
    band,
    picked,
    chunk_send,
    chunk_recv,
    code_send,
    code_recv,
    area_send,
    area_recv,
    table_send,
    table_recv,
    swap_send,
    swap_recv,
    fourier_send,
    fourier_recv,
    wave_send,
    wave_recv,
    return_send,
    return_recv,
    pair_send,
    pair_recv,
    local_sem,
):
    tile, x, z, core = place()
    lev = lax.axis_index("lev")
    chip = tile // 2
    partner = tile + 1 - 2 * core
    lats, lons = totals.shape
    half = lats // 2
    pairs, points = arrived.shape[1:]
    rows = GROUP * pairs
    per_row = lons // points
    greet()

    area[lev, core, chip] = area_part[...]

    def area_z(step):
        there = chip_at(x, z + step)
        here = area.at[lev, core, chip]
        sems = area_send.at[step], area_recv.at[step]
        return remote(here, here, *sems, 2 * there + core)

    def area_x(step):
        there = chip_at(x + step, z)
        here = area.at[lev, core, pl.ds(pl.multiple_of(x * ZS, ZS), ZS)]
        sems = area_send.at[ZS + step], area_recv.at[ZS + step]
        return remote(here, here, *sems, 2 * there + core)

    def area_y(step):
        here = area.at[lev, core]
        sems = area_send.at[ZS + XS + step], area_recv.at[ZS + XS + step]
        return remote(here, here, *sems, tile, (lev + step) % LEVS)

    def area_core(q):
        here = area.at[q, core]
        at = ZS + XS + LEVS + q
        return remote(here, here, area_send.at[at], area_recv.at[at], partner)

    for step in range(1, ZS):
        area_z(step).start()

    own = legendre.shape[0]

    def own_tables(first, count):
        return tables.at[pl.ds(own * lev + first, count)]

    keep_tables = pltpu.make_async_copy(legendre, own_tables(0, own), local_sem.at[0])
    keep_tables.start()

    def give_tables(piece, way):
        first, count = ((0, own // 3), (own // 3, own - own // 3))[piece]
        at = 2 * piece + way
        return remote(
            legendre.at[pl.ds(first, count)],
            own_tables(first, count),
            table_send.at[at],
            table_recv.at[at],
            tile,
            (lev + (1, LEVS - 1)[way]) % LEVS,
        )

    def pass_tables(way):
        from_lev = (lev + (LEVS - 1, 1)[way]) % LEVS
        here = tables.at[pl.ds(own * from_lev + way * (own // 2), own // 2)]
        return remote(
            here,
            here,
            table_send.at[4 + way],
            table_recv.at[4 + way],
            tile,
            (lev + (1, LEVS - 1)[way]) % LEVS,
        )

    for way in range(2):
        give_tables(0, way).start()

    def code_copy(slot):
        there = chip_at(x + slot // ZS, z + slot % ZS)
        return remote(
            codes.at[slot % GROUP],
            code_in.at[slot],
            code_send.at[slot],
            code_recv.at[slot],
            2 * there + core,
        )

    def start_code(slot, carry):
        code_copy(slot).start()
        return carry

    lax.fori_loop(1, CHIPS, start_code, 0)
    code_in[0] = codes[0]

    def chunk_copy(slot):
        there = chip_at(x + slot // ZS, z + slot % ZS)
        return remote(
            chunks.at[there],
            arrived.at[slot],
            chunk_send.at[slot],
            chunk_recv.at[slot],
            2 * there + core,
        )

    def start_chunk(slot, carry):
        chunk_copy(slot).start()
        return carry

    lax.fori_loop(1, CHIPS, start_chunk, 0)
    arrived[0] = chunks[chip]

    strip = points
    longitude = lax.broadcasted_iota(jnp.int32, (strip, points), 1)
    norm = 1.0 / math.sqrt(lons)

    def make_rows(step, carry):
        at = pl.ds(pl.multiple_of(step * strip, strip), strip)
        code = wave_codes[:, at]
        code = down_rows(code // 64, points) * 64.0 + down_rows(code % 64, points)
        code = code.astype(jnp.int32)
        wave, part = code % 1024, code // 1024
        cos, sin = cos_sin(wrap(wave * longitude + part * (lons // 4), lons), lons)
        cos, sin = cos * norm, sin * norm
        turn_c, turn_s = cos_sin(wrap(wave * points, lons), lons)
        for block in range(per_row):
            table[at, block * points : (block + 1) * points] = cos.astype(BF)
            cos, sin = cos * turn_c - sin * turn_s, sin * turn_c + cos * turn_s
        return carry

    lax.fori_loop(0, table.shape[0] // strip, make_rows, 0)

    for step in range(1, ZS):
        area_z(step).wait_recv()
    for step in range(1, XS):
        area_x(step).start()

    slots = response.shape[0]

    def make_response(slot, carry):
        wave = wave_order[tile * slots + slot]
        doubled = jnp.where(wave == 0, 1.0, 2.0).astype(F32)
        for p in range(2):
            degree = wave + p + 2 * lax.broadcasted_iota(jnp.int32, (1, half), 1)
            growth = (degree * (degree + 1)).astype(F32) * (1.0 / (TRUNC * (TRUNC + 1)))
            value = doubled / (1.0 + damping[...] * growth)
            response[slot, p] = jnp.where(degree <= TRUNC, value, 0.0)
        return carry

    lax.fori_loop(0, slots, make_response, 0)

    lat_index = lax.broadcasted_iota(jnp.int32, (lats, rows), 0)

    def add_group(group, first):
        for j in range(GROUP):
            if not (first and j == 0):
                code_copy(group * GROUP + j).wait_recv()
                chunk_copy(group * GROUP + j).wait_recv()
        code = code_in[group * GROUP]
        for j in range(1, GROUP):
            code = code + code_in[group * GROUP + j]
        code_rows[group] = code
        code = code[:, :rows]
        one_hot = jnp.where(lat_index == code // 16, 1.0, 0.0).astype(BF)
        values = arrived[pl.ds(group * GROUP, GROUP)].reshape(rows, points)
        where = down_rows(code % 16, points).astype(BF)
        for b in range(0, per_row, 2):
            spread = jnp.concatenate(
                [jnp.where(where == float(b + i), values, jnp.zeros_like(values)) for i in range(2)],
                axis=1,
            )
            term = jnp.dot(one_hot, spread, preferred_element_type=F32)
            at = slice(b * points, (b + 2) * points)
            if first:
                totals[:, at] = term
            else:
                totals[:, at] += term

    def later_group(group, carry):
        add_group(group, False)
        return carry

    add_group(0, True)
    for step in range(1, XS):
        area_x(step).wait_recv()
    for step in range(1, LEVS):
        area_y(step).start()
    for way in range(2):
        give_tables(1, way).start()
    lax.fori_loop(1, 4, later_group, 0)
    for step in range(1, LEVS):
        area_y(step).wait_recv()
    for q in range(LEVS):
        area_core(q).start()
    lax.fori_loop(4, CHIPS // GROUP, later_group, 0)
    for q in range(LEVS):
        area_core(q).wait_recv()

    sign = (1 - 2 * core).astype(F32)
    quarters = LEVS
    width = lons // LEVS

    def weights(q, side):
        found = []
        for c in range(2):
            part = area[q, c, side * (CHIPS // 2) : (side + 1) * (CHIPS // 2)]
            part = part.reshape(-1, width)
            found.append(jnp.dot(pick_rows[side, c], part, preferred_element_type=F32))
        return found[0] + found[1]

    def swap_copy(q):
        return remote(
            given.at[q], taken.at[q], swap_send.at[q], swap_recv.at[q], partner
        )

    for q in range(quarters):
        at = slice(q * width, (q + 1) * width)
        north = totals[:half, at] * weights(q, 0)
        south = totals[half:, at] * weights(q, 1) * sign
        totals[:half, at] = north + south
        given[q] = (north - south).astype(BF)
        swap_copy(q).start()
    for q in range(quarters):
        at = slice(q * width, (q + 1) * width)
        swap_copy(q).wait_recv()
        folded[:, at] = (totals[:half, at] + taken[q].astype(F32)).astype(BF)

    share = fourier.shape[1]
    batch = ZS

    def fourier_copy(peer):
        return remote(
            fourier.at[peer],
            spectra.at[slot_of(tile)],
            fourier_send.at[peer],
            fourier_recv.at[tile],
            peer,
        )

    def transform(step, carry):
        first = ((x + step // 2) % XS) * (2 * ZS) + ((z // (ZS // 2) + step) % 2) * batch
        at = pl.ds(pl.multiple_of(first * share, batch * share), batch * share)
        part = lax.dot_general(table[at, :], folded[...], NT, preferred_element_type=F32)
        fourier[pl.ds(first, batch)] = part.astype(BF).reshape(batch, share, half)
        for j in range(batch):
            peer = first + j

            @pl.when(peer != tile)
            def _():
                fourier_copy(peer).start()

        return carry

    lax.fori_loop(0, TILES // batch, transform, 0)
    spectra[slot_of(tile)] = fourier[tile]
    for way in range(2):
        for piece in range(2):
            give_tables(piece, way).wait_recv()
        pass_tables(way).start()

    def finish_fourier(step, carry):
        peer = (tile + step) % TILES
        fourier_copy(peer).wait_send()
        remote(
            fourier.at[peer],
            spectra.at[slot_of(peer)],
            fourier_send.at[peer],
            fourier_recv.at[peer],
            peer,
        ).wait_recv()
        return carry

    lax.fori_loop(1, TILES, finish_fourier, 0)

    def wave_copy(peer):
        return remote(
            parts.at[peer], returned.at[tile], wave_send.at[peer], wave_recv.at[tile], peer
        )

    mixed = 2 * CHIPS
    for way in range(2):
        pass_tables(way).wait_recv()
    keep_tables.wait()
    for p in range(2):
        rows_in = spectra[p * CHIPS : (p + 1) * CHIPS].reshape(CHIPS * share, half)
        sorted_in[...] = jnp.dot(order[...], rows_in, preferred_element_type=F32).astype(BF)

        def one_slot(slot, carry):
            at = pl.ds(pl.multiple_of(slot * mixed, mixed), mixed)
            legendre_at = tables[2 * slot + p]
            coefficient = lax.dot_general(
                sorted_in[at, :], legendre_at, NT, preferred_element_type=F32
            )
            scale = response[slot, p]
            spectrum = jnp.concatenate(
                [coefficient[:CHIPS] * scale, coefficient[CHIPS:] * scale], axis=0
            ).astype(BF)
            sorted_out[at, :] = jnp.dot(
                spectrum, legendre_at, preferred_element_type=F32
            ).astype(BF)
            return carry

        lax.fori_loop(0, slots, one_slot, 0)

        def send_back(step, carry):
            first = ((x + step) % XS) * ZS
            at = pl.ds(pl.multiple_of(first * share, ZS * share), ZS * share)
            part = jnp.dot(back_order[at, :], sorted_out[...], preferred_element_type=F32)
            part = part.astype(BF).reshape(ZS, share, half)
            for j in range(ZS):
                peer = 2 * (first + j) + p
                parts[peer] = part[j]

                @pl.when(peer != tile)
                def _():
                    wave_copy(peer).start()

            return carry

        lax.fori_loop(0, XS, send_back, 0)
    returned[tile] = parts[tile]

    def wave_arrival(peer):
        return remote(
            parts.at[peer], returned.at[peer], wave_send.at[peer], wave_recv.at[peer], peer
        )

    def inverse(step):
        first = ((x + XS - step) % XS) * (2 * ZS)

        def wait_one(j, carry):
            @pl.when(first + j != tile)
            def _():
                wave_arrival(first + j).wait_recv()

            return carry

        lax.fori_loop(0, 2 * ZS, wait_one, 0)
        values = returned[pl.ds(first, 2 * ZS)].reshape(2 * ZS * share, half)
        at = pl.ds(pl.multiple_of(first * share, 2 * ZS * share), 2 * ZS * share)
        for c in range(0, lons, 512):
            term = lax.dot_general(
                values, table[at, c : c + 512], TN, preferred_element_type=F32
            )
            if step == 0:
                wide[:, c : c + 512] = term
            else:
                wide[:, c : c + 512] += term

    for step in range(XS):
        inverse(step)

    def return_copy(q):
        return remote(
            sent_back.at[q], got_back.at[q], return_send.at[q], return_recv.at[q], partner
        )

    for q in range(quarters):
        sent_back[q] = wide[:, q * width : (q + 1) * width].astype(BF)
        return_copy(q).start()
    for q in range(quarters):
        at = slice(q * width, (q + 1) * width)
        return_copy(q).wait_recv()
        mine, theirs = wide[:, at], got_back[q].astype(F32)
        band[:half, at] = (mine + theirs).astype(BF)
        band[half:, at] = ((mine - theirs) * sign).astype(BF)

    def pair_copy(slot):
        there = chip_at(x - slot // ZS, z - slot % ZS)
        return remote(
            picked.at[slot],
            replies.at[chip],
            pair_send.at[slot],
            pair_recv.at[chip],
            2 * there + core,
        )

    lat_lane = lax.broadcasted_iota(jnp.int32, (rows, points), 1).astype(F32)

    def answer(group, carry):
        code = code_rows[group][:, :rows]
        lat = code // 16
        lat = down_rows(lat // points, points) * points + down_rows(lat % points, points)
        one_hot = jnp.concatenate(
            [
                jnp.where(lat == lat_lane + float(c), 1.0, 0.0).astype(BF)
                for c in range(0, 2 * half, points)
            ],
            axis=1,
        )
        where = down_rows(code % 16, points).astype(BF)
        chosen = jnp.zeros((rows, points), BF)
        for b in range(0, per_row, 2):
            found = jnp.dot(
                one_hot, band[:, b * points : (b + 2) * points], preferred_element_type=F32
            ).astype(BF)
            for i in range(2):
                chosen = jnp.where(
                    where == float(b + i), found[:, i * points : (i + 1) * points], chosen
                )
        picked[pl.ds(group * GROUP, GROUP)] = chosen.reshape(GROUP, pairs, points)
        for j in range(GROUP):
            slot = group * GROUP + j

            @pl.when(slot != 0)
            def _():
                pair_copy(slot).start()

        return carry

    lax.fori_loop(0, CHIPS // GROUP, answer, 0)
    replies[chip] = picked[0]

    def finish_pair(slot, carry):
        pair_copy(slot).wait_send()
        here = chip_at(x - slot // ZS, z - slot % ZS)
        remote(
            picked.at[slot],
            replies.at[here],
            pair_send.at[slot],
            pair_recv.at[here],
            2 * here + core,
        ).wait_recv()
        return carry

    lax.fori_loop(1, CHIPS, finish_pair, 0)

    def finish_wave(step, carry):
        wave_copy((tile + step) % TILES).wait_send()
        return carry

    lax.fori_loop(1, TILES, finish_wave, 0)
    for q in range(quarters):
        return_copy(q).wait_send()
    def finish_chunk(slot, carry):
        chunk_copy(slot).wait_send()
        return carry

    lax.fori_loop(1, CHIPS, finish_chunk, 0)
    def finish_code(slot, carry):
        code_copy(slot).wait_send()
        return carry

    lax.fori_loop(1, CHIPS, finish_code, 0)
    for q in range(quarters):
        swap_copy(q).wait_send()
        area_core(q).wait_send()
    for step in range(1, ZS):
        area_z(step).wait_send()
    for step in range(1, XS):
        area_x(step).wait_send()
    for step in range(1, LEVS):
        area_y(step).wait_send()


    for way in range(2):
        for piece in range(2):
            give_tables(piece, way).wait_send()
        pass_tables(way).wait_send()


def regrid_call(chunks, codes, area_part, picks, wave_codes, wave_order, damping, legendre):
    pairs, points = chunks.shape[1:]
    room, width = codes.shape[2], area_part.shape[1]
    lons, lats = LEVS * width, 2 * picks.shape[2]
    half, share, groups = lats // 2, wave_codes.shape[1] // TILES, CHIPS // GROUP
    slots, mixed = share // 2, CHIPS * share
    order, back_order = slot_orders(slots)
    vmem = pl.BlockSpec(memory_space=pltpu.VMEM)
    smem = pl.BlockSpec(memory_space=pltpu.SMEM)
    anywhere = pl.BlockSpec(memory_space=pl.ANY)
    dma = pltpu.SemaphoreType.DMA
    return pl.pallas_call(
        regrid,
        out_shape=jax.ShapeDtypeStruct((CHIPS, pairs, points), BF),
        in_specs=[vmem] * 5 + [smem, vmem, anywhere, vmem, vmem],
        out_specs=vmem,
        scratch_shapes=[
            pltpu.VMEM((CHIPS, pairs, points), BF),
            pltpu.VMEM((CHIPS, 1, room), jnp.int32),
            pltpu.VMEM((groups, 1, room), jnp.int32),
            pltpu.VMEM((lats, lons), F32),
            pltpu.VMEM((LEVS, 2, CHIPS, PAD_LAT, width), BF),
            pltpu.VMEM((TILES * share, lons), BF),
            pltpu.VMEM((2 * slots, half, half), BF),
            pltpu.VMEM((slots, 2, CHIPS, half), F32),
            pltpu.VMEM((LEVS, half, width), BF),
            pltpu.VMEM((LEVS, half, width), BF),
            pltpu.VMEM((half, lons), BF),
            pltpu.VMEM((TILES, share, half), BF),
            pltpu.VMEM((TILES, share, half), BF),
            pltpu.VMEM((mixed, half), BF),
            pltpu.VMEM((mixed, half), BF),
            pltpu.VMEM((TILES, share, half), BF),
            pltpu.VMEM((TILES, share, half), BF),
            pltpu.VMEM((half, lons), F32),
            pltpu.VMEM((LEVS, half, width), BF),
            pltpu.VMEM((LEVS, half, width), BF),
            pltpu.VMEM((lats, lons), BF),
            pltpu.VMEM((CHIPS, pairs, points), BF),
            dma((CHIPS,)),
            dma((CHIPS,)),
            dma((CHIPS,)),
            dma((CHIPS,)),
            dma((ZS + XS + 2 * LEVS,)),
            dma((ZS + XS + 2 * LEVS,)),
            dma((6,)),
            dma((6,)),
            dma((LEVS,)),
            dma((LEVS,)),
            dma((TILES,)),
            dma((TILES,)),
            dma((TILES,)),
            dma((TILES,)),
            dma((LEVS,)),
            dma((LEVS,)),
            dma((CHIPS,)),
            dma((CHIPS,)),
            dma((1,)),
        ],
        compiler_params=pltpu.CompilerParams(
            collective_id=0, has_side_effects=True, vmem_limit_bytes=VMEM_LIMIT
        ),
    )(
        chunks,
        codes,
        area_part,
        picks,
        wave_codes,
        wave_order,
        damping,
        legendre,
        order,
        back_order,
    )


def slot_orders(slots):
    chip, part, slot = np.meshgrid(
        np.arange(CHIPS), np.arange(2), np.arange(slots), indexing="ij"
    )
    source = ((chip * 2 + part) * slots + slot).reshape(-1)
    target = ((slot * 2 + part) * CHIPS + chip).reshape(-1)
    order = np.zeros((source.size, source.size), np.float32)
    order[target, source] = 1.0
    return jnp.asarray(order, BF), jnp.asarray(order.T.copy(), BF)


def lat_picks(lat_dev, half):
    picks = np.zeros((2, 2, half, CHIPS // 2 * PAD_LAT), np.float32)
    for tile in range(TILES):
        for i in range(lat_dev):
            lat = tile * lat_dev + i
            side = int(lat >= half)
            to = lat if side == 0 else 2 * half - 1 - lat
            picks[side, tile % 2, to, (tile // 2) % (CHIPS // 2) * PAD_LAT + i] = 1.0
    return jnp.asarray(picks, BF)


def shards(
    cube_field,
    margin,
    pair_owner,
    pair_block,
    cube_area,
    band_area,
    wave_order,
    legendre,
    gauss_weight,
    diffusion,
):
    levs = lax.axis_size("lev")
    tile, x, z, core = place()
    lev = lax.axis_index("lev")
    fields, cell_count = cube_field.shape
    pairs, cells, points = margin.shape
    blocks = pairs // 2
    lat_dev, lons = band_area.shape
    per_row = lons // points
    lats = lat_dev * TILES
    half = lats // 2
    slots = wave_order.shape[0] // TILES
    width = lons // levs

    lat = pair_owner * lat_dev + pair_block // per_row
    row = jnp.where(lat < half, lat, lats + half - 1 - lat)
    code = row * 16 + pair_block % per_row
    room = -(-GROUP * pairs // points) * points
    codes = jnp.stack(
        [jnp.pad(code, (j * pairs, room - (j + 1) * pairs))[None] for j in range(GROUP)]
    )

    own_lat = tile * lat_dev + jnp.arange(lat_dev, dtype=jnp.int32)
    own_weight = gauss_weight[jnp.where(own_lat < half, own_lat, lats - 1 - own_lat)]
    part = lax.dynamic_slice_in_dim(band_area, lev * width, width, axis=1)
    part = (own_weight[:, None] / part).astype(BF)
    area_part = jnp.pad(part, ((0, PAD_LAT - lat_dev), (0, 0)))
    margin_q = margin.reshape(blocks, 2, cells, points)
    chunks = jnp.einsum(
        "fbc,bkcg->fbkg",
        cube_field.reshape(fields, blocks, cells),
        margin_q,
        preferred_element_type=F32,
    )
    chunks = chunks.astype(BF).reshape(fields, pairs, points)

    part_codes = jnp.arange(2, dtype=jnp.int32)[None, :, None] * 1024
    wave_codes = (wave_order.reshape(TILES, 1, slots) + part_codes).reshape(1, -1)
    damping = lax.dynamic_slice_in_dim(diffusion, lev * fields, fields)[:, None]
    replies = regrid_call(
        chunks,
        codes,
        area_part,
        lat_picks(lat_dev, half),
        wave_codes,
        wave_order,
        damping,
        legendre.reshape(-1, half, half),
    )

    cube = jnp.einsum(
        "fbkg,bkcg->fbc",
        replies.reshape(fields, blocks, 2, points),
        margin_q,
        preferred_element_type=F32,
    )
    cube = cube / cube_area.reshape(blocks, cells)[None]
    return cube.astype(BF).reshape(fields, cell_count)


def solution(mesh):
    in_specs = (
        P("lev", "tile"),
        P("tile", None, None),
        P("tile"),
        P("tile"),
        P("tile"),
        P("tile", None),
        P(),
        P(("tile", "lev"), None, None, None),
        P(),
        P(),
    )
    out_specs = P("lev", "tile")
    return jax.shard_map(shards, mesh=mesh, in_specs=in_specs, out_specs=out_specs, check_vma=False)
```

```python
import functools
import math

import jax
import jax.numpy as jnp
import numpy as np
from jax import lax
from jax.experimental import pallas as pl
from jax.experimental.pallas import tpu as pltpu
from jax.sharding import PartitionSpec as P

TRUNC = 766
MESH = pl.DeviceIdType.MESH
BF = jnp.bfloat16
F32 = jnp.float32
GROUP = 4
WINDOW = 3
PAD_LAT = 16
VMEM_LIMIT = 56 * 2**20
NT = (((1,), (1,)), ((), ()))
TN = (((0,), (0,)), ((), ()))

XS, ZS, LEVS = 4, 8, 4
CHIPS = XS * ZS
TILES = 2 * CHIPS


def place():
    tile = lax.axis_index("tile")
    return tile, tile // (2 * ZS), (tile // 2) % ZS, tile % 2


def chip_at(x, z):
    return ((x + XS) % XS) * ZS + (z + ZS) % ZS


def greet():
    tile, _, _, _ = place()
    lev = lax.axis_index("lev")
    barrier = pltpu.get_barrier_semaphore()

    def one(step, carry):
        peer = (tile + step) % TILES
        pl.semaphore_signal(barrier, inc=1, device_id=(peer, lev), device_id_type=MESH)
        return carry

    lax.fori_loop(1, TILES, one, 0)
    for step in range(1, LEVS):
        peer = (tile, (lev + step) % LEVS)
        pl.semaphore_signal(barrier, inc=1, device_id=peer, device_id_type=MESH)
    pl.semaphore_wait(barrier, TILES - 1 + LEVS - 1)


def remote(src, dst, send, recv, peer, lev=None):
    return pltpu.make_async_remote_copy(
        src_ref=src,
        dst_ref=dst,
        send_sem=send,
        recv_sem=recv,
        device_id=(peer, lax.axis_index("lev") if lev is None else lev),
        device_id_type=MESH,
    )


def drain(ref, sem):
    pltpu.make_async_copy(ref, ref, sem).wait()


def offset(slot):
    k = slot % ZS
    return slot // ZS, (k + 1) // 2 * (2 * (k % 2) - 1)


def slot_of(tile):
    return (tile % 2) * CHIPS + tile // 2


def cos_sin(phase, turn):
    eighth = turn // 8
    octant = ((phase + eighth).astype(F32) * (4.0 / turn) + 0.5 / turn).astype(jnp.int32)
    angle = (phase - octant * (turn // 4)).astype(F32) * (2.0 * math.pi / turn)
    square = angle * angle
    cos = 1.0 + square * (
        -1 / 2 + square * (1 / 24 + square * (-1 / 720 + square * (1 / 40320)))
    )
    sin = angle * (
        1.0 + square * (-1 / 6 + square * (1 / 120 + square * (-1 / 5040 + square * (1 / 362880))))
    )
    odd = octant % 2 == 1
    base_c, base_s = jnp.where(odd, sin, cos), jnp.where(odd, cos, sin)
    flip_c = (octant == 1) | (octant == 2)
    flip_s = (octant == 2) | (octant == 3)
    return jnp.where(flip_c, -base_c, base_c), jnp.where(flip_s, -base_s, base_s)


def wrap(count, turn):
    return count - ((count.astype(F32) + 0.5) * (1.0 / turn)).astype(jnp.int32) * turn


def down_rows(row, width):
    first = lax.broadcasted_iota(jnp.int32, (16, row.shape[1]), 0) == 0
    spread = jnp.where(first, row.astype(F32), 0.0).astype(BF)
    return lax.dot_general(spread, jnp.ones((16, width), BF), TN, preferred_element_type=F32)


def regrid(
    chunks,
    codes,
    area_part,
    pack_rows,
    unmix,
    wave_codes,
    wave_order,
    damping,
    legendre,
    order,
    back_order,
    replies,
    arrived,
    code_in,
    code_rows,
    totals,
    area_in,
    area,
    table,
    tables,
    response,
    given,
    taken,
    turned,
    fourier,
    spectra,
    sorted_in,
    sorted_out,
    parts,
    returned,
    wide,
    sent_back,
    got_back,
    band,
    picked,
    chunk_send,
    chunk_recv,
    code_send,
    code_recv,
    area_send,
    area_recv,
    table_send,
    table_recv,
    swap_send,
    swap_recv,
    fourier_send,
    fourier_recv,
    wave_send,
    wave_recv,
    return_send,
    return_recv,
    pair_send,
    pair_recv,
    local_sem,
):
    tile, x, z, core = place()
    lev = lax.axis_index("lev")
    chip = tile // 2
    partner = tile + 1 - 2 * core
    lats, lons = totals.shape
    half = lats // 2
    pairs, points = arrived.shape[1:]
    rows = GROUP * pairs
    per_row = lons // points
    greet()

    area_in[chip] = area_part[...]

    def area_z(step):
        there = chip_at(x, z + step)
        here = area_in.at[chip]
        sems = area_send.at[0], area_recv.at[0]
        return remote(here, here, *sems, 2 * there + core)

    def area_x(step):
        there = chip_at(x + step, z)
        here = area_in.at[pl.ds(pl.multiple_of(x * ZS, ZS), ZS)]
        sems = area_send.at[1], area_recv.at[1]
        return remote(here, here, *sems, 2 * there + core)

    def area_y(step):
        here = area.at[lev, core]
        sems = area_send.at[2], area_recv.at[2]
        return remote(here, here, *sems, tile, (lev + step) % LEVS)

    def area_core(q):
        here = area.at[q, core]
        return remote(here, here, area_send.at[3], area_recv.at[3], partner)

    for step in range(1, ZS):
        area_z(step).start()

    own = legendre.shape[0]

    def own_tables(first, count):
        return tables.at[pl.ds(own * lev + first, count)]

    keep_tables = pltpu.make_async_copy(legendre, own_tables(0, own), local_sem.at[0])
    keep_tables.start()

    def give_tables(piece, way):
        first, count = ((0, own // 6), (own // 6, own - own // 6))[piece]
        return remote(
            legendre.at[pl.ds(first, count)],
            own_tables(first, count),
            table_send.at[0],
            table_recv.at[way],
            tile,
            (lev + (1, LEVS - 1)[way]) % LEVS,
        )

    def pass_tables(way):
        from_lev = (lev + (LEVS - 1, 1)[way]) % LEVS
        here = tables.at[pl.ds(own * from_lev + way * (own // 2), own // 2)]
        return remote(
            here,
            here,
            table_send.at[0],
            table_recv.at[2],
            tile,
            (lev + (1, LEVS - 1)[way]) % LEVS,
        )

    for way in range(2):
        give_tables(0, way).start()

    def code_copy(slot):
        dx, dz = offset(slot)
        there = chip_at(x + dx, z + dz)
        return remote(
            codes.at[slot % GROUP],
            code_in.at[slot],
            code_send.at[0],
            code_recv.at[slot // GROUP],
            2 * there + core,
        )

    def start_code(slot, carry):
        code_copy(slot).start()
        return carry

    lax.fori_loop(1, CHIPS, start_code, 0)
    code_in[0] = codes[0]

    def chunk_copy(slot):
        dx, dz = offset(slot)
        there = chip_at(x + dx, z + dz)
        return remote(
            chunks.at[there],
            arrived.at[slot],
            chunk_send.at[0],
            chunk_recv.at[slot // GROUP],
            2 * there + core,
        )

    def start_chunk(slot, carry):
        chunk_copy(slot).start()
        return carry

    lax.fori_loop(1, WINDOW * GROUP, start_chunk, 0)
    arrived[0] = chunks[chip]

    slots = response.shape[0]

    def make_response(slot, carry):
        wave = wave_order[tile * slots + slot]
        doubled = jnp.where(wave == 0, 1.0, 2.0).astype(F32)
        for p in range(2):
            degree = wave + p + 2 * lax.broadcasted_iota(jnp.int32, (1, half), 1)
            growth = (degree * (degree + 1)).astype(F32) * (1.0 / (TRUNC * (TRUNC + 1)))
            value = doubled / (1.0 + damping[...] * growth)
            response[slot, p] = jnp.where(degree <= TRUNC, value, 0.0)
        return carry

    lax.fori_loop(0, slots, make_response, 0)

    drain(area_in.at[pl.ds(0, ZS - 1)], area_recv.at[0])
    for step in range(1, XS):
        area_x(step).start()

    strip = points
    longitude = lax.broadcasted_iota(jnp.int32, (strip, points), 1)
    norm = 1.0 / math.sqrt(lons)

    def make_rows(step, carry):
        at = pl.ds(pl.multiple_of(step * strip, strip), strip)
        code = wave_codes[:, at]
        code = down_rows(code // 64, points) * 64.0 + down_rows(code % 64, points)
        code = code.astype(jnp.int32)
        wave, part = code % 1024, code // 1024
        cos, sin = cos_sin(wrap(wave * longitude + part * (lons // 4), lons), lons)
        cos, sin = cos * norm, sin * norm
        turn_c, turn_s = cos_sin(wrap(wave * points, lons), lons)
        for block in range(per_row):
            table[at, block * points : (block + 1) * points] = cos.astype(BF)
            cos, sin = cos * turn_c - sin * turn_s, sin * turn_c + cos * turn_s
        return carry

    lax.fori_loop(0, table.shape[0] // strip, make_rows, 0)

    drain(area_in.at[pl.ds(0, CHIPS - ZS)], area_recv.at[1])
    area[lev, core] = jnp.dot(
        pack_rows[...], area_in[...].reshape(CHIPS * PAD_LAT, -1), preferred_element_type=F32
    ).astype(BF)
    area_core(lev).start()
    for step in range(1, LEVS):
        area_y(step).start()
    for way in range(2):
        give_tables(1, way).start()

    lat_index = lax.broadcasted_iota(jnp.int32, (lats, rows), 0)

    def add_group(group, first):
        ahead = group + WINDOW

        @pl.when(ahead < CHIPS // GROUP)
        def _():
            for j in range(GROUP):
                chunk_copy(ahead * GROUP + j).start()

        from_slot = pl.ds(1, GROUP - 1) if first else pl.ds(group * GROUP, GROUP)
        drain(code_in.at[from_slot], code_recv.at[group])
        drain(arrived.at[from_slot], chunk_recv.at[group])
        code = code_in[group * GROUP]
        for j in range(1, GROUP):
            code = code + code_in[group * GROUP + j]
        code_rows[group] = code
        code = code[:, :rows]
        one_hot = jnp.where(lat_index == code // 16384, 1.0, 0.0).astype(BF)
        values = arrived[pl.ds(group * GROUP, GROUP)].reshape(rows, points)
        where = down_rows(code % 16, points).astype(BF)
        for b in range(0, per_row, 2):
            spread = jnp.concatenate(
                [jnp.where(where == float(b + i), values, jnp.zeros_like(values)) for i in range(2)],
                axis=1,
            )
            term = jnp.dot(one_hot, spread, preferred_element_type=F32)
            at = slice(b * points, (b + 2) * points)
            if first:
                totals[:, at] = term
            else:
                totals[:, at] += term

    def later_group(group, carry):
        add_group(group, False)
        return carry

    add_group(0, True)
    lax.fori_loop(1, 4, later_group, 0)
    drain(area.at[pl.ds(0, LEVS - 1), core], area_recv.at[2])
    for step in range(1, LEVS):
        area_core((lev + step) % LEVS).start()
    lax.fori_loop(4, CHIPS // GROUP, later_group, 0)
    drain(area.at[:, core], area_recv.at[3])

    sign = (1 - 2 * core).astype(F32)
    quarters = LEVS
    width = lons // LEVS

    def weights(q, side):
        at = slice(side * (half // 2), (side + 1) * (half // 2))
        return jnp.concatenate([area[q, c ^ side, at].astype(F32) for c in range(2)], axis=0)

    def swap_copy(q):
        return remote(
            given.at[q], taken.at[q], swap_send.at[0], swap_recv.at[q], partner
        )

    for q in range(quarters):
        at = slice(q * width, (q + 1) * width)
        north = totals[:half, at] * weights(q, 0)
        south = totals[half:, at] * weights(q, 1) * sign
        totals[:half, at] = north + south
        given[q] = (north - south).astype(BF)
        swap_copy(q).start()
    for q in range(quarters):
        at = slice(q * width, (q + 1) * width)
        swap_copy(q).wait_recv()
        folded = (totals[:half, at] + taken[q].astype(F32)).astype(BF)
        turned[at, :] = lax.dot_general(
            folded, unmix[...], TN, preferred_element_type=F32
        ).astype(BF)

    share = fourier.shape[1]
    batch = 2 * ZS

    def fourier_copy(peer):
        return remote(
            fourier.at[peer],
            spectra.at[slot_of(tile)],
            fourier_send.at[0],
            fourier_recv.at[0],
            peer,
        )

    def transform(step, carry):
        first = ((x + step) % XS) * batch
        at = pl.ds(pl.multiple_of(first * share, batch * share), batch * share)
        part = jnp.dot(table[at, :], turned[...], preferred_element_type=F32)
        fourier[pl.ds(first, batch)] = part.astype(BF).reshape(batch, share, half)

        def start_one(j, carry):
            _, dz = offset(j // 2)
            peer = first + (z + dz + ZS) % ZS * 2 + (core + j) % 2

            @pl.when(peer != tile)
            def _():
                fourier_copy(peer).start()

            return carry

        lax.fori_loop(0, batch, start_one, 0)
        return carry

    lax.fori_loop(0, XS, transform, 0)
    spectra[slot_of(tile)] = fourier[tile]
    for way in range(2):
        drain(tables.at[pl.ds(0, own)], table_recv.at[way])
        pass_tables(way).start()

    drain(spectra.at[pl.ds(0, TILES - 1)], fourier_recv.at[0])

    def wave_copy(peer):
        return remote(
            parts.at[peer], returned.at[tile], wave_send.at[0], wave_recv.at[x], peer
        )

    mixed = 2 * CHIPS
    drain(tables.at[pl.ds(0, own)], table_recv.at[2])
    keep_tables.wait()
    for p in range(2):
        rows_in = spectra[p * CHIPS : (p + 1) * CHIPS].reshape(CHIPS * share, half)
        sorted_in[...] = jnp.dot(order[...], rows_in, preferred_element_type=F32).astype(BF)

        def one_slot(slot, carry):
            at = pl.ds(pl.multiple_of(slot * mixed, mixed), mixed)
            legendre_at = tables[2 * slot + p]
            coefficient = lax.dot_general(
                sorted_in[at, :], legendre_at, NT, preferred_element_type=F32
            )
            scale = response[slot, p]
            spectrum = jnp.concatenate(
                [coefficient[:CHIPS] * scale, coefficient[CHIPS:] * scale], axis=0
            ).astype(BF)
            sorted_out[at, :] = jnp.dot(
                spectrum, legendre_at, preferred_element_type=F32
            ).astype(BF)
            return carry

        lax.fori_loop(0, slots, one_slot, 0)

        def send_back(step, carry):
            first = ((x + step) % XS) * ZS
            at = pl.ds(pl.multiple_of(first * share, ZS * share), ZS * share)
            part = jnp.dot(back_order[at, :], sorted_out[...], preferred_element_type=F32)
            part = part.astype(BF).reshape(ZS, share, half)
            for j in range(ZS):
                parts[2 * (first + j) + p] = part[j]

            def start_one(j, carry):
                _, dz = offset(j)
                peer = 2 * (first + (z + dz + ZS) % ZS) + p

                @pl.when(peer != tile)
                def _():
                    wave_copy(peer).start()

                return carry

            lax.fori_loop(0, ZS, start_one, 0)
            return carry

        lax.fori_loop(0, XS, send_back, 0)
    returned[tile] = parts[tile]

    def inverse(step):
        there = (x + XS - step) % XS
        first = there * (2 * ZS)
        count = 2 * ZS - 1 if step == 0 else 2 * ZS
        drain(returned.at[pl.ds(0, count)], wave_recv.at[there])
        values = returned[pl.ds(first, 2 * ZS)].reshape(2 * ZS * share, half).T
        at = pl.ds(pl.multiple_of(first * share, 2 * ZS * share), 2 * ZS * share)
        for c in range(0, lons, 512):
            term = jnp.dot(values, table[at, c : c + 512], preferred_element_type=F32)
            if step == 0:
                wide[:, c : c + 512] = term
            else:
                wide[:, c : c + 512] += term

    for step in range(XS):
        inverse(step)

    def return_copy(q):
        return remote(
            sent_back.at[q], got_back.at[q], return_send.at[0], return_recv.at[q], partner
        )

    for q in range(quarters):
        sent_back[q] = wide[:, q * width : (q + 1) * width].astype(BF)
        return_copy(q).start()
    for q in range(quarters):
        at = slice(q * width, (q + 1) * width)
        return_copy(q).wait_recv()
        mine, theirs = wide[:, at], got_back[q].astype(F32)
        band[:half, at] = (mine + theirs).astype(BF)
        band[half:, at] = ((mine - theirs) * sign).astype(BF)

    def pair_copy(slot):
        dx, dz = offset(slot)
        there = chip_at(x - dx, z - dz)
        return remote(
            picked.at[slot],
            replies.at[chip],
            pair_send.at[0],
            pair_recv.at[0],
            2 * there + core,
        )

    lat_lane = lax.broadcasted_iota(jnp.int32, (rows, points), 1).astype(F32)

    def answer(group, carry):
        code = code_rows[group][:, :rows]
        lat = code // 16 % 1024
        lat = down_rows(lat // points, points) * points + down_rows(lat % points, points)
        one_hot = jnp.concatenate(
            [
                jnp.where(lat == lat_lane + float(c), 1.0, 0.0).astype(BF)
                for c in range(0, 2 * half, points)
            ],
            axis=1,
        )
        where = down_rows(code % 16, points).astype(BF)
        chosen = jnp.zeros((rows, points), BF)
        for b in range(0, per_row, 2):
            found = jnp.dot(
                one_hot, band[:, b * points : (b + 2) * points], preferred_element_type=F32
            ).astype(BF)
            for i in range(2):
                chosen = jnp.where(
                    where == float(b + i), found[:, i * points : (i + 1) * points], chosen
                )
        picked[pl.ds(group * GROUP, GROUP)] = chosen.reshape(GROUP, pairs, points)
        for j in range(GROUP):
            slot = group * GROUP + j

            @pl.when(slot != 0)
            def _():
                pair_copy(slot).start()

        return carry

    lax.fori_loop(0, CHIPS // GROUP, answer, 0)
    replies[chip] = picked[0]

    drain(replies.at[pl.ds(0, CHIPS - 1)], pair_recv.at[0])
    drain(picked.at[pl.ds(0, CHIPS - 1)], pair_send.at[0])
    drain(parts.at[pl.ds(0, TILES - 1)], wave_send.at[0])
    drain(sent_back, return_send.at[0])
    drain(fourier.at[pl.ds(0, TILES - 1)], fourier_send.at[0])
    drain(given, swap_send.at[0])
    drain(chunks.at[pl.ds(0, CHIPS - 1)], chunk_send.at[0])
    drain(code_in.at[pl.ds(0, CHIPS - 1)], code_send.at[0])
    drain(area_in.at[pl.ds(0, ZS - 1)], area_send.at[0])
    drain(area_in.at[pl.ds(0, CHIPS - ZS)], area_send.at[1])
    drain(area.at[pl.ds(0, LEVS - 1), core], area_send.at[2])
    drain(area.at[:, core], area_send.at[3])
    drain(tables.at[pl.ds(0, 3 * own)], table_send.at[0])


def regrid_call(chunks, codes, area_part, lat_dev, wave_codes, wave_order, damping, legendre):
    pairs, points = chunks.shape[1:]
    room, width = codes.shape[2], area_part.shape[1]
    lons, lats = LEVS * width, lat_dev * TILES
    half, share, groups = lats // 2, wave_codes.shape[1] // TILES, CHIPS // GROUP
    slots, mixed = share // 2, CHIPS * share
    order, back_order = slot_orders(slots)
    pack_rows, unmix = lat_orders(lat_dev)
    vmem = pl.BlockSpec(memory_space=pltpu.VMEM)
    smem = pl.BlockSpec(memory_space=pltpu.SMEM)
    anywhere = pl.BlockSpec(memory_space=pl.ANY)
    dma = pltpu.SemaphoreType.DMA
    return pl.pallas_call(
        regrid,
        out_shape=jax.ShapeDtypeStruct((CHIPS, pairs, points), BF),
        in_specs=[vmem] * 6 + [smem, vmem, anywhere, vmem, vmem],
        out_specs=vmem,
        scratch_shapes=[
            pltpu.VMEM((CHIPS, pairs, points), BF),
            pltpu.VMEM((CHIPS, 1, room), jnp.int32),
            pltpu.VMEM((groups, 1, room), jnp.int32),
            pltpu.VMEM((lats, lons), F32),
            pltpu.VMEM((CHIPS, PAD_LAT, width), BF),
            pltpu.VMEM((LEVS, 2, half, width), BF),
            pltpu.VMEM((TILES * share, lons), BF),
            pltpu.VMEM((2 * slots, half, half), BF),
            pltpu.VMEM((slots, 2, CHIPS, half), F32),
            pltpu.VMEM((LEVS, half, width), BF),
            pltpu.VMEM((LEVS, half, width), BF),
            pltpu.VMEM((lons, half), BF),
            pltpu.VMEM((TILES, share, half), BF),
            pltpu.VMEM((TILES, share, half), BF),
            pltpu.VMEM((mixed, half), BF),
            pltpu.VMEM((mixed, half), BF),
            pltpu.VMEM((TILES, share, half), BF),
            pltpu.VMEM((TILES, share, half), BF),
            pltpu.VMEM((half, lons), F32),
            pltpu.VMEM((LEVS, half, width), BF),
            pltpu.VMEM((LEVS, half, width), BF),
            pltpu.VMEM((lats, lons), BF),
            pltpu.VMEM((CHIPS, pairs, points), BF),
            dma((1,)),
            dma((groups,)),
            dma((1,)),
            dma((groups,)),
            dma((4,)),
            dma((4,)),
            dma((1,)),
            dma((3,)),
            dma((1,)),
            dma((LEVS,)),
            dma((1,)),
            dma((1,)),
            dma((1,)),
            dma((XS,)),
            dma((1,)),
            dma((LEVS,)),
            dma((1,)),
            dma((1,)),
            dma((1,)),
        ],
        compiler_params=pltpu.CompilerParams(
            collective_id=0, has_side_effects=True, vmem_limit_bytes=VMEM_LIMIT
        ),
    )(
        chunks,
        codes,
        area_part,
        pack_rows,
        unmix,
        wave_codes,
        wave_order,
        damping,
        legendre,
        order,
        back_order,
    )


def slot_orders(slots):
    chip, part, slot = np.meshgrid(
        np.arange(CHIPS), np.arange(2), np.arange(slots), indexing="ij"
    )
    source = ((chip * 2 + part) * slots + slot).reshape(-1)
    target = ((slot * 2 + part) * CHIPS + chip).reshape(-1)
    order = np.zeros((source.size, source.size), np.float32)
    order[target, source] = 1.0
    return jnp.asarray(order, BF), jnp.asarray(order.T.copy(), BF)


def mixed_row(lat, lat_dev):
    tile = lat // lat_dev
    return tile % 2 * (CHIPS // 2 * lat_dev) + tile // 2 * lat_dev + lat % lat_dev


def lat_orders(lat_dev):
    quarter = CHIPS // 2 * lat_dev
    pack = np.zeros((2 * quarter, CHIPS * PAD_LAT), np.float32)
    for chip in range(CHIPS):
        for i in range(lat_dev):
            row = chip * lat_dev + i
            if chip >= CHIPS // 2:
                row = quarter + (CHIPS - 1 - chip) * lat_dev + lat_dev - 1 - i
            pack[row, chip * PAD_LAT + i] = 1.0
    unmix = np.zeros((2 * quarter, 2 * quarter), np.float32)
    lats = np.arange(2 * quarter)
    unmix[mixed_row(lats, lat_dev), lats] = 1.0
    return jnp.asarray(pack, BF), jnp.asarray(unmix, BF)


def shards(
    cube_field,
    margin,
    pair_owner,
    pair_block,
    cube_area,
    band_area,
    wave_order,
    legendre,
    gauss_weight,
    diffusion,
):
    levs = lax.axis_size("lev")
    tile, x, z, core = place()
    lev = lax.axis_index("lev")
    fields, cell_count = cube_field.shape
    pairs, cells, points = margin.shape
    blocks = pairs // 2
    lat_dev, lons = band_area.shape
    per_row = lons // points
    lats = lat_dev * TILES
    half = lats // 2
    slots = wave_order.shape[0] // TILES
    width = lons // levs

    lat = pair_owner * lat_dev + pair_block // per_row
    south = jnp.where(lat < half, 0, half)
    north = jnp.where(lat < half, lat, lats - 1 - lat)
    code = (south + mixed_row(north, lat_dev)) * 1024 + south + north
    code = code * 16 + pair_block % per_row
    room = -(-GROUP * pairs // points) * points
    codes = jnp.stack(
        [jnp.pad(code, (j * pairs, room - (j + 1) * pairs))[None] for j in range(GROUP)]
    )

    own_lat = tile * lat_dev + jnp.arange(lat_dev, dtype=jnp.int32)
    own_weight = gauss_weight[jnp.where(own_lat < half, own_lat, lats - 1 - own_lat)]
    part = lax.dynamic_slice_in_dim(band_area, lev * width, width, axis=1)
    part = (own_weight[:, None] / part).astype(BF)
    area_part = jnp.pad(part, ((0, PAD_LAT - lat_dev), (0, 0)))
    margin_q = margin.reshape(blocks, 2, cells, points)
    chunks = jnp.einsum(
        "fbc,bkcg->fbkg",
        cube_field.reshape(fields, blocks, cells),
        margin_q,
        preferred_element_type=F32,
    )
    chunks = chunks.astype(BF).reshape(fields, pairs, points)

    part_codes = jnp.arange(2, dtype=jnp.int32)[None, :, None] * 1024
    wave_codes = (wave_order.reshape(TILES, 1, slots) + part_codes).reshape(1, -1)
    damping = lax.dynamic_slice_in_dim(diffusion, lev * fields, fields)[:, None]
    replies = regrid_call(
        chunks,
        codes,
        area_part,
        lat_dev,
        wave_codes,
        wave_order,
        damping,
        legendre.reshape(-1, half, half),
    )

    cube = jnp.einsum(
        "fbkg,bkcg->fbc",
        replies.reshape(fields, blocks, 2, points),
        margin_q,
        preferred_element_type=F32,
    )
    cube = cube / cube_area.reshape(blocks, cells)[None]
    return cube.astype(BF).reshape(fields, cell_count)


def solution(mesh):
    in_specs = (
        P("lev", "tile"),
        P("tile", None, None),
        P("tile"),
        P("tile"),
        P("tile"),
        P("tile", None),
        P(),
        P(("tile", "lev"), None, None, None),
        P(),
        P(),
    )
    out_specs = P("lev", "tile")
    return jax.shard_map(shards, mesh=mesh, in_specs=in_specs, out_specs=out_specs, check_vma=False)
```

```python
import functools
import math

import jax
import jax.numpy as jnp
import numpy as np
from jax import lax
from jax.experimental import pallas as pl
from jax.experimental.pallas import tpu as pltpu
from jax.sharding import PartitionSpec as P

TRUNC = 766
MESH = pl.DeviceIdType.MESH
BF = jnp.bfloat16
F32 = jnp.float32
GROUP = 4
WINDOW = 3
PAD_LAT = 16
VMEM_LIMIT = 56 * 2**20
NT = (((1,), (1,)), ((), ()))
TN = (((0,), (0,)), ((), ()))

XS, ZS, LEVS = 4, 8, 4
CHIPS = XS * ZS
TILES = 2 * CHIPS


def place():
    tile = lax.axis_index("tile")
    return tile, tile // (2 * ZS), (tile // 2) % ZS, tile % 2


def chip_at(x, z):
    return ((x + XS) % XS) * ZS + (z + ZS) % ZS


def greet():
    tile, _, _, _ = place()
    lev = lax.axis_index("lev")
    barrier = pltpu.get_barrier_semaphore()

    def one(step, carry):
        peer = (tile + step) % TILES
        pl.semaphore_signal(barrier, inc=1, device_id=(peer, lev), device_id_type=MESH)
        return carry

    lax.fori_loop(1, TILES, one, 0)
    for step in range(1, LEVS):
        peer = (tile, (lev + step) % LEVS)
        pl.semaphore_signal(barrier, inc=1, device_id=peer, device_id_type=MESH)
    pl.semaphore_wait(barrier, TILES - 1 + LEVS - 1)


def remote(src, dst, send, recv, peer, lev=None):
    return pltpu.make_async_remote_copy(
        src_ref=src,
        dst_ref=dst,
        send_sem=send,
        recv_sem=recv,
        device_id=(peer, lax.axis_index("lev") if lev is None else lev),
        device_id_type=MESH,
    )


def drain(ref, sem):
    pltpu.make_async_copy(ref, ref, sem).wait()


def offset(slot):
    k = slot % ZS
    return slot // ZS, (k + 1) // 2 * (2 * (k % 2) - 1)


def slot_of(tile):
    return (tile % 2) * CHIPS + tile // 2


def cos_sin(phase, turn):
    eighth = turn // 8
    octant = ((phase + eighth).astype(F32) * (4.0 / turn) + 0.5 / turn).astype(jnp.int32)
    angle = (phase - octant * (turn // 4)).astype(F32) * (2.0 * math.pi / turn)
    square = angle * angle
    cos = 1.0 + square * (
        -1 / 2 + square * (1 / 24 + square * (-1 / 720 + square * (1 / 40320)))
    )
    sin = angle * (
        1.0 + square * (-1 / 6 + square * (1 / 120 + square * (-1 / 5040 + square * (1 / 362880))))
    )
    odd = octant % 2 == 1
    base_c, base_s = jnp.where(odd, sin, cos), jnp.where(odd, cos, sin)
    flip_c = (octant == 1) | (octant == 2)
    flip_s = (octant == 2) | (octant == 3)
    return jnp.where(flip_c, -base_c, base_c), jnp.where(flip_s, -base_s, base_s)


def wrap(count, turn):
    return count - ((count.astype(F32) + 0.5) * (1.0 / turn)).astype(jnp.int32) * turn


def down_rows(row, width):
    first = lax.broadcasted_iota(jnp.int32, (16, row.shape[1]), 0) == 0
    spread = jnp.where(first, row.astype(F32), 0.0).astype(BF)
    return lax.dot_general(spread, jnp.ones((16, width), BF), TN, preferred_element_type=F32)


def regrid(
    chunks,
    codes,
    band_area,
    gauss_weight,
    pack_rows,
    unmix,
    wave_list,
    wave_order,
    diffusion,
    legendre,
    order,
    back_order,
    replies,
    arrived,
    code_in,
    code_rows,
    totals,
    area_stage,
    area_in,
    area,
    table,
    tables,
    response,
    given,
    taken,
    turned,
    fourier,
    spectra,
    sorted_in,
    sorted_out,
    parts,
    returned,
    wide,
    sent_back,
    got_back,
    band,
    picked,
    chunk_send,
    chunk_recv,
    code_send,
    code_recv,
    area_send,
    area_recv,
    table_send,
    table_recv,
    swap_send,
    swap_recv,
    fourier_send,
    fourier_recv,
    wave_send,
    wave_recv,
    return_send,
    return_recv,
    pair_send,
    pair_recv,
    local_sem,
):
    tile, x, z, core = place()
    lev = lax.axis_index("lev")
    chip = tile // 2
    partner = tile + 1 - 2 * core
    lats, lons = totals.shape
    half = lats // 2
    pairs, points = arrived.shape[1:]
    rows = GROUP * pairs
    per_row = lons // points
    greet()

    lat_dev, width = band_area.shape[0], lons // LEVS
    row = lax.broadcasted_iota(jnp.int32, (PAD_LAT, half), 0)
    own_lat = tile * lat_dev + row
    north_lat = jnp.where(own_lat < half, own_lat, lats - 1 - own_lat)
    found = lax.broadcasted_iota(jnp.int32, (PAD_LAT, half), 1) == north_lat
    weight = jnp.sum(jnp.where(found, gauss_weight[...].reshape(1, half), 0.0), axis=1, keepdims=True)
    area_stage[...] = jnp.ones_like(area_stage)
    area_stage[:lat_dev] = band_area[:, pl.ds(pl.multiple_of(lev * width, width), width)]
    real_row = lax.broadcasted_iota(jnp.int32, (PAD_LAT, width), 0) < lat_dev
    area_in[chip] = jnp.where(real_row, weight / area_stage[...], 0.0).astype(BF)

    def area_z(step):
        there = chip_at(x, z + step)
        here = area_in.at[chip]
        sems = area_send.at[0], area_recv.at[0]
        return remote(here, here, *sems, 2 * there + core)

    def area_x(step):
        there = chip_at(x + step, z)
        here = area_in.at[pl.ds(pl.multiple_of(x * ZS, ZS), ZS)]
        sems = area_send.at[1], area_recv.at[1]
        return remote(here, here, *sems, 2 * there + core)

    def area_y(step):
        here = area.at[lev, core]
        sems = area_send.at[2], area_recv.at[2]
        return remote(here, here, *sems, tile, (lev + step) % LEVS)

    def area_core(q):
        here = area.at[q, core]
        return remote(here, here, area_send.at[3], area_recv.at[3], partner)

    for step in range(1, ZS):
        area_z(step).start()

    own = legendre.shape[0]

    def own_tables(first, count):
        return tables.at[pl.ds(own * lev + first, count)]

    keep_tables = pltpu.make_async_copy(legendre, own_tables(0, own), local_sem.at[0])
    keep_tables.start()

    unit = own // 6
    give_order = (((0, 2), (2, 4)), ((3, 2), (5, 1), (0, 3)))

    def give_tables(piece, way):
        first, count = (unit * v for v in give_order[way][piece])
        return remote(
            legendre.at[pl.ds(first, count)],
            own_tables(first, count),
            table_send.at[0],
            table_recv.at[2 * way + min(piece, 1)],
            tile,
            (lev + (1, LEVS - 1)[way]) % LEVS,
        )

    def pass_tables(piece, way):
        from_lev = (lev + (LEVS - 1, 1)[way]) % LEVS
        first, count = ((0, 2), (2, 1))[piece]
        here = tables.at[pl.ds(own * from_lev + (3 * way + first) * unit, count * unit)]
        return remote(
            here,
            here,
            table_send.at[0],
            table_recv.at[4],
            tile,
            (lev + (1, LEVS - 1)[way]) % LEVS,
        )

    for way in range(2):
        give_tables(0, way).start()

    def code_copy(slot):
        dx, dz = offset(slot)
        there = chip_at(x + dx, z + dz)
        return remote(
            codes.at[slot % GROUP],
            code_in.at[slot],
            code_send.at[0],
            code_recv.at[slot // GROUP],
            2 * there + core,
        )

    def start_code(slot, carry):
        code_copy(slot).start()
        return carry

    lax.fori_loop(1, CHIPS, start_code, 0)
    code_in[0] = codes[0]

    def chunk_copy(slot):
        dx, dz = offset(slot)
        there = chip_at(x + dx, z + dz)
        return remote(
            chunks.at[there],
            arrived.at[slot],
            chunk_send.at[0],
            chunk_recv.at[slot // GROUP],
            2 * there + core,
        )

    def start_chunk(slot, carry):
        chunk_copy(slot).start()
        return carry

    lax.fori_loop(1, WINDOW * GROUP, start_chunk, 0)
    arrived[0] = chunks[chip]

    slots = response.shape[0]

    found = lax.broadcasted_iota(jnp.int32, (CHIPS, LEVS * CHIPS), 1) == (
        lax.broadcasted_iota(jnp.int32, (CHIPS, LEVS * CHIPS), 0) + CHIPS * lev
    )
    damping = diffusion[...].reshape(1, LEVS * CHIPS)
    damping = jnp.sum(jnp.where(found, damping, 0.0), axis=1, keepdims=True)

    def make_response(slot, carry):
        wave = wave_order[tile * slots + slot]
        doubled = jnp.where(wave == 0, 1.0, 2.0).astype(F32)
        for p in range(2):
            degree = wave + p + 2 * lax.broadcasted_iota(jnp.int32, (1, half), 1)
            growth = (degree * (degree + 1)).astype(F32) * (1.0 / (TRUNC * (TRUNC + 1)))
            value = doubled / (1.0 + damping * growth)
            response[slot, p] = jnp.where(degree <= TRUNC, value, 0.0)
        return carry

    lax.fori_loop(0, slots, make_response, 0)

    drain(area_in.at[pl.ds(0, ZS - 1)], area_recv.at[0])
    for step in range(1, XS):
        area_x(step).start()

    strip = points
    longitude = lax.broadcasted_iota(jnp.int32, (strip, points), 1)
    norm = 1.0 / math.sqrt(lons)
    waves = wave_list[...].reshape(1, TILES * slots).astype(F32)
    wave_at = lax.broadcasted_iota(jnp.int32, (strip, TILES * slots), 1)

    def make_rows(step, carry):
        at = pl.ds(pl.multiple_of(step * strip, strip), strip)
        row = step * strip + lax.broadcasted_iota(jnp.int32, (strip, 1), 0)
        part = row // slots % 2
        found = wave_at == row // (2 * slots) * slots + row % slots
        wave = jnp.sum(jnp.where(found, waves, 0.0), axis=1, keepdims=True).astype(jnp.int32)
        wave = jnp.broadcast_to(wave, (strip, points))
        cos, sin = cos_sin(wrap(wave * longitude + part * (lons // 4), lons), lons)
        cos, sin = cos * norm, sin * norm
        turn_c, turn_s = cos_sin(wrap(wave * points, lons), lons)
        for block in range(per_row):
            table[at, block * points : (block + 1) * points] = cos.astype(BF)
            cos, sin = cos * turn_c - sin * turn_s, sin * turn_c + cos * turn_s
        return carry

    lax.fori_loop(0, table.shape[0] // strip, make_rows, 0)

    drain(area_in.at[pl.ds(0, CHIPS - ZS)], area_recv.at[1])
    area[lev, core] = jnp.dot(
        pack_rows[...], area_in[...].reshape(CHIPS * PAD_LAT, -1), preferred_element_type=F32
    ).astype(BF)
    area_core(lev).start()
    for step in range(1, LEVS):
        area_y(step).start()
    for piece, way in ((1, 0), (1, 1), (2, 1)):
        give_tables(piece, way).start()

    lat_index = lax.broadcasted_iota(jnp.int32, (lats, rows), 0)

    def add_group(group, first):
        ahead = group + WINDOW

        @pl.when(ahead < CHIPS // GROUP)
        def _():
            for j in range(GROUP):
                chunk_copy(ahead * GROUP + j).start()

        from_slot = pl.ds(1, GROUP - 1) if first else pl.ds(group * GROUP, GROUP)
        drain(code_in.at[from_slot], code_recv.at[group])
        drain(arrived.at[from_slot], chunk_recv.at[group])
        code = code_in[group * GROUP]
        for j in range(1, GROUP):
            code = code + code_in[group * GROUP + j]
        code_rows[group] = code
        code = code[:, :rows]
        one_hot = jnp.where(lat_index == code // 16384, 1.0, 0.0).astype(BF)
        values = arrived[pl.ds(group * GROUP, GROUP)].reshape(rows, points)
        where = down_rows(code % 16, points).astype(BF)
        for b in range(0, per_row, 2):
            spread = jnp.concatenate(
                [jnp.where(where == float(b + i), values, jnp.zeros_like(values)) for i in range(2)],
                axis=1,
            )
            term = jnp.dot(one_hot, spread, preferred_element_type=F32)
            at = slice(b * points, (b + 2) * points)
            if first:
                totals[:, at] = term
            else:
                totals[:, at] += term

    def later_group(group, carry):
        add_group(group, False)
        return carry

    add_group(0, True)
    lax.fori_loop(1, 4, later_group, 0)
    drain(area.at[pl.ds(0, LEVS - 1), core], area_recv.at[2])
    for way in range(2):
        drain(tables.at[pl.ds(0, 2 * unit)], table_recv.at[2 * way])
        pass_tables(0, way).start()
    for step in range(1, LEVS):
        area_core((lev + step) % LEVS).start()
    lax.fori_loop(4, CHIPS // GROUP, later_group, 0)
    drain(area.at[:, core], area_recv.at[3])

    sign = (1 - 2 * core).astype(F32)
    quarters = LEVS

    def weights(q, side):
        at = slice(side * (half // 2), (side + 1) * (half // 2))
        return jnp.concatenate([area[q, c ^ side, at].astype(F32) for c in range(2)], axis=0)

    def swap_copy(q):
        return remote(
            given.at[q], taken.at[q], swap_send.at[0], swap_recv.at[q], partner
        )

    for q in range(quarters):
        at = slice(q * width, (q + 1) * width)
        north = totals[:half, at] * weights(q, 0)
        south = totals[half:, at] * weights(q, 1) * sign
        totals[:half, at] = north + south
        given[q] = (north - south).astype(BF)
        swap_copy(q).start()
    for q in range(quarters):
        at = slice(q * width, (q + 1) * width)
        swap_copy(q).wait_recv()
        folded = (totals[:half, at] + taken[q].astype(F32)).astype(BF)
        turned[at, :] = lax.dot_general(
            folded, unmix[...], TN, preferred_element_type=F32
        ).astype(BF)

    share = fourier.shape[1]
    batch = 2 * ZS

    def fourier_copy(peer):
        return remote(
            fourier.at[peer],
            spectra.at[slot_of(tile)],
            fourier_send.at[0],
            fourier_recv.at[0],
            peer,
        )

    def transform(step, carry):
        first = ((x + step) % XS) * batch
        at = pl.ds(pl.multiple_of(first * share, batch * share), batch * share)
        part = jnp.dot(table[at, :], turned[...], preferred_element_type=F32)
        fourier[pl.ds(first, batch)] = part.astype(BF).reshape(batch, share, half)

        def start_one(j, carry):
            _, dz = offset(j // 2)
            peer = first + (z + dz + ZS) % ZS * 2 + (core + j) % 2

            @pl.when(peer != tile)
            def _():
                fourier_copy(peer).start()

            return carry

        lax.fori_loop(0, batch, start_one, 0)
        return carry

    lax.fori_loop(0, XS, transform, 0)
    spectra[slot_of(tile)] = fourier[tile]
    for way in range(2):
        drain(tables.at[pl.ds(0, 4 * unit)], table_recv.at[2 * way + 1])
        pass_tables(1, way).start()

    drain(spectra.at[pl.ds(0, TILES - 1)], fourier_recv.at[0])

    def wave_copy(peer):
        return remote(
            parts.at[peer], returned.at[tile], wave_send.at[0], wave_recv.at[x], peer
        )

    mixed = 2 * CHIPS
    keep_tables.wait()
    own_slots = slots // LEVS
    for p in range(2):
        rows_in = spectra[p * CHIPS : (p + 1) * CHIPS].reshape(CHIPS * share, half)
        sorted_in[...] = jnp.dot(order[...], rows_in, preferred_element_type=F32).astype(BF)

        def one_slot(step, carry):
            there = step // own_slots
            there = (lev + there + there // 2 * (5 - 2 * there)) % LEVS
            slot = there * own_slots + step % own_slots
            at = pl.ds(pl.multiple_of(slot * mixed, mixed), mixed)
            legendre_at = tables[2 * slot + p]
            coefficient = lax.dot_general(
                sorted_in[at, :], legendre_at, NT, preferred_element_type=F32
            )
            scale = response[slot, p]
            spectrum = jnp.concatenate(
                [coefficient[:CHIPS] * scale, coefficient[CHIPS:] * scale], axis=0
            ).astype(BF)
            sorted_out[at, :] = jnp.dot(
                spectrum, legendre_at, preferred_element_type=F32
            ).astype(BF)
            return carry

        lax.fori_loop(0, slots - own_slots, one_slot, 0)
        if p == 0:
            drain(tables.at[pl.ds(0, own)], table_recv.at[4])
        lax.fori_loop(slots - own_slots, slots, one_slot, 0)

        def send_back(step, carry):
            first = ((x + step) % XS) * ZS
            at = pl.ds(pl.multiple_of(first * share, ZS * share), ZS * share)
            part = jnp.dot(back_order[at, :], sorted_out[...], preferred_element_type=F32)
            part = part.astype(BF).reshape(ZS, share, half)
            for j in range(ZS):
                parts[2 * (first + j) + p] = part[j]

            def start_one(j, carry):
                _, dz = offset(j)
                peer = 2 * (first + (z + dz + ZS) % ZS) + p

                @pl.when(peer != tile)
                def _():
                    wave_copy(peer).start()

                return carry

            lax.fori_loop(0, ZS, start_one, 0)
            return carry

        lax.fori_loop(0, XS, send_back, 0)
    returned[tile] = parts[tile]

    def inverse(step):
        there = (x + XS - step) % XS
        first = there * (2 * ZS)
        count = 2 * ZS - 1 if step == 0 else 2 * ZS
        drain(returned.at[pl.ds(0, count)], wave_recv.at[there])
        values = returned[pl.ds(first, 2 * ZS)].reshape(2 * ZS * share, half).T
        at = pl.ds(pl.multiple_of(first * share, 2 * ZS * share), 2 * ZS * share)
        for c in range(0, lons, 512):
            term = jnp.dot(values, table[at, c : c + 512], preferred_element_type=F32)
            if step == 0:
                wide[:, c : c + 512] = term
            else:
                wide[:, c : c + 512] += term

    for step in range(XS):
        inverse(step)

    def return_copy(q):
        return remote(
            sent_back.at[q], got_back.at[q], return_send.at[0], return_recv.at[q], partner
        )

    for q in range(quarters):
        sent_back[q] = wide[:, q * width : (q + 1) * width].astype(BF)
        return_copy(q).start()
    for q in range(quarters):
        at = slice(q * width, (q + 1) * width)
        return_copy(q).wait_recv()
        mine, theirs = wide[:, at], got_back[q].astype(F32)
        band[:half, at] = (mine + theirs).astype(BF)
        band[half:, at] = ((mine - theirs) * sign).astype(BF)

    def pair_copy(slot):
        dx, dz = offset(slot)
        there = chip_at(x - dx, z - dz)
        return remote(
            picked.at[slot],
            replies.at[chip],
            pair_send.at[0],
            pair_recv.at[0],
            2 * there + core,
        )

    lat_lane = lax.broadcasted_iota(jnp.int32, (rows, points), 1).astype(F32)

    def answer(group, carry):
        code = code_rows[group][:, :rows]
        lat = code // 16 % 1024
        lat = down_rows(lat // points, points) * points + down_rows(lat % points, points)
        one_hot = jnp.concatenate(
            [
                jnp.where(lat == lat_lane + float(c), 1.0, 0.0).astype(BF)
                for c in range(0, 2 * half, points)
            ],
            axis=1,
        )
        where = down_rows(code % 16, points).astype(BF)
        chosen = jnp.zeros((rows, points), BF)
        for b in range(0, per_row, 2):
            found = jnp.dot(
                one_hot, band[:, b * points : (b + 2) * points], preferred_element_type=F32
            ).astype(BF)
            for i in range(2):
                chosen = jnp.where(
                    where == float(b + i), found[:, i * points : (i + 1) * points], chosen
                )
        picked[pl.ds(group * GROUP, GROUP)] = chosen.reshape(GROUP, pairs, points)
        for j in range(GROUP):
            slot = group * GROUP + j

            @pl.when(slot != 0)
            def _():
                pair_copy(slot).start()

        return carry

    lax.fori_loop(0, CHIPS // GROUP, answer, 0)
    replies[chip] = picked[0]

    drain(replies.at[pl.ds(0, CHIPS - 1)], pair_recv.at[0])
    drain(picked.at[pl.ds(0, CHIPS - 1)], pair_send.at[0])
    drain(parts.at[pl.ds(0, TILES - 1)], wave_send.at[0])
    drain(sent_back, return_send.at[0])
    drain(fourier.at[pl.ds(0, TILES - 1)], fourier_send.at[0])
    drain(given, swap_send.at[0])
    drain(chunks.at[pl.ds(0, CHIPS - 1)], chunk_send.at[0])
    drain(code_in.at[pl.ds(0, CHIPS - 1)], code_send.at[0])
    drain(area_in.at[pl.ds(0, ZS - 1)], area_send.at[0])
    drain(area_in.at[pl.ds(0, CHIPS - ZS)], area_send.at[1])
    drain(area.at[pl.ds(0, LEVS - 1), core], area_send.at[2])
    drain(area.at[:, core], area_send.at[3])
    drain(tables.at[pl.ds(0, 3 * own)], table_send.at[0])


def regrid_call(chunks, codes, band_area, gauss_weight, wave_order, diffusion, legendre):
    pairs, points = chunks.shape[1:]
    room, (lat_dev, lons) = codes.shape[2], band_area.shape
    width, lats = lons // LEVS, lat_dev * TILES
    half, slots, groups = lats // 2, wave_order.shape[0] // TILES, CHIPS // GROUP
    share, mixed = 2 * slots, CHIPS * 2 * slots
    order, back_order = slot_orders(slots)
    pack_rows, unmix = lat_orders(lat_dev)
    vmem = pl.BlockSpec(memory_space=pltpu.VMEM)
    smem = pl.BlockSpec(memory_space=pltpu.SMEM)
    anywhere = pl.BlockSpec(memory_space=pl.ANY)
    dma = pltpu.SemaphoreType.DMA
    return pl.pallas_call(
        regrid,
        out_shape=jax.ShapeDtypeStruct((CHIPS, pairs, points), BF),
        in_specs=[vmem] * 7 + [smem, vmem, anywhere, vmem, vmem],
        out_specs=vmem,
        scratch_shapes=[
            pltpu.VMEM((CHIPS, pairs, points), BF),
            pltpu.VMEM((CHIPS, 1, room), jnp.int32),
            pltpu.VMEM((groups, 1, room), jnp.int32),
            pltpu.VMEM((lats, lons), F32),
            pltpu.VMEM((PAD_LAT, width), F32),
            pltpu.VMEM((CHIPS, PAD_LAT, width), BF),
            pltpu.VMEM((LEVS, 2, half, width), BF),
            pltpu.VMEM((TILES * share, lons), BF),
            pltpu.VMEM((2 * slots, half, half), BF),
            pltpu.VMEM((slots, 2, CHIPS, half), F32),
            pltpu.VMEM((LEVS, half, width), BF),
            pltpu.VMEM((LEVS, half, width), BF),
            pltpu.VMEM((lons, half), BF),
            pltpu.VMEM((TILES, share, half), BF),
            pltpu.VMEM((TILES, share, half), BF),
            pltpu.VMEM((mixed, half), BF),
            pltpu.VMEM((mixed, half), BF),
            pltpu.VMEM((TILES, share, half), BF),
            pltpu.VMEM((TILES, share, half), BF),
            pltpu.VMEM((half, lons), F32),
            pltpu.VMEM((LEVS, half, width), BF),
            pltpu.VMEM((LEVS, half, width), BF),
            pltpu.VMEM((lats, lons), BF),
            pltpu.VMEM((CHIPS, pairs, points), BF),
            dma((1,)),
            dma((groups,)),
            dma((1,)),
            dma((groups,)),
            dma((4,)),
            dma((4,)),
            dma((1,)),
            dma((5,)),
            dma((1,)),
            dma((LEVS,)),
            dma((1,)),
            dma((1,)),
            dma((1,)),
            dma((XS,)),
            dma((1,)),
            dma((LEVS,)),
            dma((1,)),
            dma((1,)),
            dma((1,)),
        ],
        compiler_params=pltpu.CompilerParams(
            collective_id=0, has_side_effects=True, vmem_limit_bytes=VMEM_LIMIT
        ),
    )(
        chunks,
        codes,
        band_area,
        gauss_weight,
        pack_rows,
        unmix,
        wave_order,
        wave_order,
        diffusion,
        legendre,
        order,
        back_order,
    )


def slot_orders(slots):
    chip, part, slot = np.meshgrid(
        np.arange(CHIPS), np.arange(2), np.arange(slots), indexing="ij"
    )
    source = ((chip * 2 + part) * slots + slot).reshape(-1)
    target = ((slot * 2 + part) * CHIPS + chip).reshape(-1)
    order = np.zeros((source.size, source.size), np.float32)
    order[target, source] = 1.0
    return jnp.asarray(order, BF), jnp.asarray(order.T.copy(), BF)


def mixed_row(lat, lat_dev):
    tile = lat // lat_dev
    return tile % 2 * (CHIPS // 2 * lat_dev) + tile // 2 * lat_dev + lat % lat_dev


def lat_orders(lat_dev):
    quarter = CHIPS // 2 * lat_dev
    pack = np.zeros((2 * quarter, CHIPS * PAD_LAT), np.float32)
    for chip in range(CHIPS):
        for i in range(lat_dev):
            row = chip * lat_dev + i
            if chip >= CHIPS // 2:
                row = quarter + (CHIPS - 1 - chip) * lat_dev + lat_dev - 1 - i
            pack[row, chip * PAD_LAT + i] = 1.0
    unmix = np.zeros((2 * quarter, 2 * quarter), np.float32)
    lats = np.arange(2 * quarter)
    unmix[mixed_row(lats, lat_dev), lats] = 1.0
    return jnp.asarray(pack, BF), jnp.asarray(unmix, BF)


def shards(
    cube_field,
    margin,
    pair_owner,
    pair_block,
    cube_area,
    band_area,
    wave_order,
    legendre,
    gauss_weight,
    diffusion,
):
    fields, cell_count = cube_field.shape
    pairs, cells, points = margin.shape
    blocks = pairs // 2
    lat_dev, lons = band_area.shape
    per_row = lons // points
    lats = lat_dev * TILES
    half = lats // 2

    lat = pair_owner * lat_dev + pair_block // per_row
    south = jnp.where(lat < half, 0, half)
    north = jnp.where(lat < half, lat, lats - 1 - lat)
    code = (south + mixed_row(north, lat_dev)) * 1024 + south + north
    code = code * 16 + pair_block % per_row
    room = -(-GROUP * pairs // points) * points
    codes = jnp.stack(
        [jnp.pad(code, (j * pairs, room - (j + 1) * pairs))[None] for j in range(GROUP)]
    )

    margin_q = margin.reshape(blocks, 2, cells, points)
    chunks = jnp.einsum(
        "fbc,bkcg->fbkg",
        cube_field.reshape(fields, blocks, cells),
        margin_q,
        preferred_element_type=F32,
    )
    chunks = chunks.astype(BF).reshape(fields, pairs, points)

    replies = regrid_call(
        chunks,
        codes,
        band_area,
        gauss_weight,
        wave_order,
        diffusion,
        legendre.reshape(-1, half, half),
    )

    cube = jnp.einsum(
        "fbkg,bkcg->fbc",
        replies.reshape(fields, blocks, 2, points),
        margin_q,
        preferred_element_type=F32,
    )
    cube = cube / cube_area.reshape(blocks, cells)[None]
    return cube.astype(BF).reshape(fields, cell_count)


def solution(mesh):
    in_specs = (
        P("lev", "tile"),
        P("tile", None, None),
        P("tile"),
        P("tile"),
        P("tile"),
        P("tile", None),
        P(),
        P(("tile", "lev"), None, None, None),
        P(),
        P(),
    )
    out_specs = P("lev", "tile")
    return jax.shard_map(shards, mesh=mesh, in_specs=in_specs, out_specs=out_specs, check_vma=False)
```

```python
import functools
import math

import jax
import jax.numpy as jnp
import numpy as np
from jax import lax
from jax.experimental import pallas as pl
from jax.experimental.pallas import tpu as pltpu
from jax.sharding import PartitionSpec as P

TRUNC = 766
MESH = pl.DeviceIdType.MESH
BF = jnp.bfloat16
F32 = jnp.float32
GROUP = 4
WINDOW = 3
PAD_LAT = 16
VMEM_LIMIT = 56 * 2**20
NT = (((1,), (1,)), ((), ()))
TN = (((0,), (0,)), ((), ()))

XS, ZS, LEVS = 4, 8, 4
CHIPS = XS * ZS
TILES = 2 * CHIPS


def place():
    tile = lax.axis_index("tile")
    return tile, tile // (2 * ZS), (tile // 2) % ZS, tile % 2


def chip_at(x, z):
    return ((x + XS) % XS) * ZS + (z + ZS) % ZS


def greet():
    tile, _, _, _ = place()
    lev = lax.axis_index("lev")
    barrier = pltpu.get_barrier_semaphore()

    def one(step, carry):
        peer = (tile + step) % TILES
        pl.semaphore_signal(barrier, inc=1, device_id=(peer, lev), device_id_type=MESH)
        return carry

    lax.fori_loop(1, TILES, one, 0)
    for step in range(1, LEVS):
        peer = (tile, (lev + step) % LEVS)
        pl.semaphore_signal(barrier, inc=1, device_id=peer, device_id_type=MESH)


def welcome():
    pl.semaphore_wait(pltpu.get_barrier_semaphore(), TILES - 1 + LEVS - 1)


def remote(src, dst, send, recv, peer, lev=None):
    return pltpu.make_async_remote_copy(
        src_ref=src,
        dst_ref=dst,
        send_sem=send,
        recv_sem=recv,
        device_id=(peer, lax.axis_index("lev") if lev is None else lev),
        device_id_type=MESH,
    )


def drain(ref, sem):
    pltpu.make_async_copy(ref, ref, sem).wait()


def offset(slot):
    k = slot % ZS
    return slot // ZS, (k + 1) // 2 * (2 * (k % 2) - 1)


def slot_of(tile):
    return (tile % 2) * CHIPS + tile // 2


def cos_sin(phase, turn):
    eighth = turn // 8
    octant = ((phase + eighth).astype(F32) * (4.0 / turn) + 0.5 / turn).astype(jnp.int32)
    angle = (phase - octant * (turn // 4)).astype(F32) * (2.0 * math.pi / turn)
    square = angle * angle
    cos = 1.0 + square * (
        -1 / 2 + square * (1 / 24 + square * (-1 / 720 + square * (1 / 40320)))
    )
    sin = angle * (
        1.0 + square * (-1 / 6 + square * (1 / 120 + square * (-1 / 5040 + square * (1 / 362880))))
    )
    odd = octant % 2 == 1
    base_c, base_s = jnp.where(odd, sin, cos), jnp.where(odd, cos, sin)
    flip_c = (octant == 1) | (octant == 2)
    flip_s = (octant == 2) | (octant == 3)
    return jnp.where(flip_c, -base_c, base_c), jnp.where(flip_s, -base_s, base_s)


def wrap(count, turn):
    return count - ((count.astype(F32) + 0.5) * (1.0 / turn)).astype(jnp.int32) * turn


def down_rows(row, width):
    first = lax.broadcasted_iota(jnp.int32, (16, row.shape[1]), 0) == 0
    spread = jnp.where(first, row.astype(F32), 0.0).astype(BF)
    return lax.dot_general(spread, jnp.ones((16, width), BF), TN, preferred_element_type=F32)


def regrid(
    cube_field,
    margin,
    pair_owner,
    pair_block,
    band_area,
    gauss_weight,
    pack_rows,
    unmix,
    wave_list,
    wave_order,
    diffusion,
    legendre,
    order_any,
    back_order_any,
    replies,
    chunks,
    codes,
    order,
    back_order,
    arrived,
    code_in,
    code_rows,
    totals,
    area_stage,
    area_in,
    area,
    table,
    tables,
    response,
    given,
    taken,
    turned,
    fourier,
    spectra,
    sorted_in,
    sorted_out,
    parts,
    returned,
    wide,
    sent_back,
    got_back,
    band,
    picked,
    chunk_send,
    chunk_recv,
    code_send,
    code_recv,
    area_send,
    area_recv,
    table_send,
    table_recv,
    swap_send,
    swap_recv,
    fourier_send,
    fourier_recv,
    wave_send,
    wave_recv,
    return_send,
    return_recv,
    pair_send,
    pair_recv,
    local_sem,
):
    tile, x, z, core = place()
    lev = lax.axis_index("lev")
    chip = tile // 2
    partner = tile + 1 - 2 * core
    lats, lons = totals.shape
    half = lats // 2
    pairs, points = arrived.shape[1:]
    rows = GROUP * pairs
    per_row = lons // points
    greet()
    orders = [
        pltpu.make_async_copy(order_any, order, local_sem.at[1]),
        pltpu.make_async_copy(back_order_any, back_order, local_sem.at[2]),
    ]
    for copy in orders:
        copy.start()

    lat_dev, width = band_area.shape[0], lons // LEVS
    owner, block = pair_owner[...].reshape(1, pairs), pair_block[...].reshape(1, pairs)
    lat = owner * lat_dev + block // per_row
    south_side = jnp.where(lat < half, 0, half)
    north_lat = jnp.where(lat < half, lat, lats - 1 - lat)
    code = (south_side + mixed_row(north_lat, lat_dev)) * 1024 + south_side + north_lat
    codes[...] = jnp.zeros_like(codes)
    codes[0, :, :pairs] = code * 16 + block % per_row
    code = jnp.broadcast_to(codes[0], (8, codes.shape[2]))
    for j in range(1, GROUP):
        codes[j] = pltpu.roll(code, j * pairs, 1)[:1]

    cells = margin.shape[2]
    span = 8 * cells
    pair_at = lax.broadcasted_iota(jnp.int32, (16, span), 0)
    block_at = lax.broadcasted_iota(jnp.int32, (16, span), 1) // cells
    masks = [jnp.where(2 * block_at + k == pair_at, 1.0, 0.0).astype(F32) for k in range(2)]

    def contribute(step, carry):
        field = cube_field[:, pl.ds(pl.multiple_of(step * span, span), span)].astype(F32)
        total = None
        for k in range(2):
            spread = (field[:, None, :] * masks[k][None]).reshape(CHIPS * 16, span).astype(BF)
            weights_k = margin[pl.ds(step * 8, 8), k].reshape(span, points)
            term = jnp.dot(spread, weights_k, preferred_element_type=F32)
            total = term if total is None else total + term
        at = pl.ds(pl.multiple_of(step * 16, 16), 16)
        chunks[:, at, :] = total.astype(BF).reshape(CHIPS, 16, points)
        return carry

    lax.fori_loop(0, pairs // 16, contribute, 0)

    row = lax.broadcasted_iota(jnp.int32, (PAD_LAT, half), 0)
    own_lat = tile * lat_dev + row
    north_lat = jnp.where(own_lat < half, own_lat, lats - 1 - own_lat)
    found = lax.broadcasted_iota(jnp.int32, (PAD_LAT, half), 1) == north_lat
    weight = jnp.sum(jnp.where(found, gauss_weight[...].reshape(1, half), 0.0), axis=1, keepdims=True)
    area_stage[...] = jnp.ones_like(area_stage)
    area_stage[:lat_dev] = band_area[:, pl.ds(pl.multiple_of(lev * width, width), width)]
    real_row = lax.broadcasted_iota(jnp.int32, (PAD_LAT, width), 0) < lat_dev
    area_in[chip] = jnp.where(real_row, weight / area_stage[...], 0.0).astype(BF)

    welcome()

    def area_z(step):
        there = chip_at(x, z + step)
        here = area_in.at[chip]
        sems = area_send.at[0], area_recv.at[0]
        return remote(here, here, *sems, 2 * there + core)

    def area_x(step):
        there = chip_at(x + step, z)
        here = area_in.at[pl.ds(pl.multiple_of(x * ZS, ZS), ZS)]
        sems = area_send.at[1], area_recv.at[1]
        return remote(here, here, *sems, 2 * there + core)

    def area_y(step):
        here = area.at[lev, core]
        sems = area_send.at[2], area_recv.at[2]
        return remote(here, here, *sems, tile, (lev + step) % LEVS)

    def area_core(q):
        here = area.at[q, core]
        return remote(here, here, area_send.at[3], area_recv.at[3], partner)

    for step in range(1, ZS):
        area_z(step).start()

    own = legendre.shape[0]

    def own_tables(first, count):
        return tables.at[pl.ds(own * lev + first, count)]

    keep_tables = pltpu.make_async_copy(legendre, own_tables(0, own), local_sem.at[0])
    keep_tables.start()

    unit = own // 6
    give_order = (((0, 2), (2, 4)), ((3, 2), (5, 1), (0, 3)))

    def give_tables(piece, way):
        first, count = (unit * v for v in give_order[way][piece])
        return remote(
            legendre.at[pl.ds(first, count)],
            own_tables(first, count),
            table_send.at[0],
            table_recv.at[2 * way + min(piece, 1)],
            tile,
            (lev + (1, LEVS - 1)[way]) % LEVS,
        )

    def pass_tables(piece, way):
        from_lev = (lev + (LEVS - 1, 1)[way]) % LEVS
        first, count = ((0, 2), (2, 1))[piece]
        here = tables.at[pl.ds(own * from_lev + (3 * way + first) * unit, count * unit)]
        return remote(
            here,
            here,
            table_send.at[0],
            table_recv.at[4],
            tile,
            (lev + (1, LEVS - 1)[way]) % LEVS,
        )

    for way in range(2):
        give_tables(0, way).start()

    def code_copy(slot):
        dx, dz = offset(slot)
        there = chip_at(x + dx, z + dz)
        return remote(
            codes.at[slot % GROUP],
            code_in.at[slot],
            code_send.at[0],
            code_recv.at[slot // GROUP],
            2 * there + core,
        )

    def start_code(slot, carry):
        code_copy(slot).start()
        return carry

    lax.fori_loop(1, CHIPS, start_code, 0)
    code_in[0] = codes[0]

    def chunk_copy(slot):
        dx, dz = offset(slot)
        there = chip_at(x + dx, z + dz)
        return remote(
            chunks.at[there],
            arrived.at[slot],
            chunk_send.at[0],
            chunk_recv.at[slot // GROUP],
            2 * there + core,
        )

    def start_chunk(slot, carry):
        chunk_copy(slot).start()
        return carry

    lax.fori_loop(1, WINDOW * GROUP, start_chunk, 0)
    arrived[0] = chunks[chip]

    slots = response.shape[0]

    found = lax.broadcasted_iota(jnp.int32, (CHIPS, LEVS * CHIPS), 1) == (
        lax.broadcasted_iota(jnp.int32, (CHIPS, LEVS * CHIPS), 0) + CHIPS * lev
    )
    damping = diffusion[...].reshape(1, LEVS * CHIPS)
    damping = jnp.sum(jnp.where(found, damping, 0.0), axis=1, keepdims=True)

    def make_response(slot, carry):
        wave = wave_order[tile * slots + slot]
        doubled = jnp.where(wave == 0, 1.0, 2.0).astype(F32)
        for p in range(2):
            degree = wave + p + 2 * lax.broadcasted_iota(jnp.int32, (1, half), 1)
            growth = (degree * (degree + 1)).astype(F32) * (1.0 / (TRUNC * (TRUNC + 1)))
            value = doubled / (1.0 + damping * growth)
            response[slot, p] = jnp.where(degree <= TRUNC, value, 0.0)
        return carry

    lax.fori_loop(0, slots, make_response, 0)

    drain(area_in.at[pl.ds(0, ZS - 1)], area_recv.at[0])
    for step in range(1, XS):
        area_x(step).start()

    strip = points
    longitude = lax.broadcasted_iota(jnp.int32, (strip, points), 1)
    norm = 1.0 / math.sqrt(lons)
    waves = wave_list[...].reshape(1, TILES * slots).astype(F32)
    wave_at = lax.broadcasted_iota(jnp.int32, (strip, TILES * slots), 1)

    def make_rows(step, carry):
        at = pl.ds(pl.multiple_of(step * strip, strip), strip)
        row = step * strip + lax.broadcasted_iota(jnp.int32, (strip, 1), 0)
        part = row // slots % 2
        found = wave_at == row // (2 * slots) * slots + row % slots
        wave = jnp.sum(jnp.where(found, waves, 0.0), axis=1, keepdims=True).astype(jnp.int32)
        wave = jnp.broadcast_to(wave, (strip, points))
        cos, sin = cos_sin(wrap(wave * longitude + part * (lons // 4), lons), lons)
        cos, sin = cos * norm, sin * norm
        turn_c, turn_s = cos_sin(wrap(wave * points, lons), lons)
        for block in range(per_row):
            table[at, block * points : (block + 1) * points] = cos.astype(BF)
            cos, sin = cos * turn_c - sin * turn_s, sin * turn_c + cos * turn_s
        return carry

    lax.fori_loop(0, table.shape[0] // strip, make_rows, 0)

    drain(area_in.at[pl.ds(0, CHIPS - ZS)], area_recv.at[1])
    area[lev, core] = jnp.dot(
        pack_rows[...], area_in[...].reshape(CHIPS * PAD_LAT, -1), preferred_element_type=F32
    ).astype(BF)
    area_core(lev).start()
    for step in range(1, LEVS):
        area_y(step).start()
    for piece, way in ((1, 0), (1, 1), (2, 1)):
        give_tables(piece, way).start()

    lat_index = lax.broadcasted_iota(jnp.int32, (lats, rows), 0)

    def add_group(group, first):
        ahead = group + WINDOW

        @pl.when(ahead < CHIPS // GROUP)
        def _():
            for j in range(GROUP):
                chunk_copy(ahead * GROUP + j).start()

        from_slot = pl.ds(1, GROUP - 1) if first else pl.ds(group * GROUP, GROUP)
        drain(code_in.at[from_slot], code_recv.at[group])
        drain(arrived.at[from_slot], chunk_recv.at[group])
        code = code_in[group * GROUP]
        for j in range(1, GROUP):
            code = code + code_in[group * GROUP + j]
        code_rows[group] = code
        code = code[:, :rows]
        one_hot = jnp.where(lat_index == code // 16384, 1.0, 0.0).astype(BF)
        values = arrived[pl.ds(group * GROUP, GROUP)].reshape(rows, points)
        where = down_rows(code % 16, points).astype(BF)
        for b in range(0, per_row, 2):
            spread = jnp.concatenate(
                [jnp.where(where == float(b + i), values, jnp.zeros_like(values)) for i in range(2)],
                axis=1,
            )
            term = jnp.dot(one_hot, spread, preferred_element_type=F32)
            at = slice(b * points, (b + 2) * points)
            if first:
                totals[:, at] = term
            else:
                totals[:, at] += term

    def later_group(group, carry):
        add_group(group, False)
        return carry

    add_group(0, True)
    lax.fori_loop(1, 4, later_group, 0)
    drain(area.at[pl.ds(0, LEVS - 1), core], area_recv.at[2])
    for way in range(2):
        drain(tables.at[pl.ds(0, 2 * unit)], table_recv.at[2 * way])
        pass_tables(0, way).start()
    for step in range(1, LEVS):
        area_core((lev + step) % LEVS).start()
    lax.fori_loop(4, CHIPS // GROUP, later_group, 0)
    drain(area.at[:, core], area_recv.at[3])

    sign = (1 - 2 * core).astype(F32)
    quarters = LEVS

    def weights(q, side):
        at = slice(side * (half // 2), (side + 1) * (half // 2))
        return jnp.concatenate([area[q, c ^ side, at].astype(F32) for c in range(2)], axis=0)

    def swap_copy(q):
        return remote(
            given.at[q], taken.at[q], swap_send.at[0], swap_recv.at[q], partner
        )

    for q in range(quarters):
        at = slice(q * width, (q + 1) * width)
        north = totals[:half, at] * weights(q, 0)
        south = totals[half:, at] * weights(q, 1) * sign
        totals[:half, at] = north + south
        given[q] = (north - south).astype(BF)
        swap_copy(q).start()
    for q in range(quarters):
        at = slice(q * width, (q + 1) * width)
        swap_copy(q).wait_recv()
        folded = (totals[:half, at] + taken[q].astype(F32)).astype(BF)
        turned[at, :] = lax.dot_general(
            folded, unmix[...], TN, preferred_element_type=F32
        ).astype(BF)

    share = fourier.shape[1]
    batch = 2 * ZS

    def fourier_copy(peer):
        return remote(
            fourier.at[peer],
            spectra.at[slot_of(tile)],
            fourier_send.at[0],
            fourier_recv.at[0],
            peer,
        )

    def transform(step, carry):
        first = ((x + step) % XS) * batch
        at = pl.ds(pl.multiple_of(first * share, batch * share), batch * share)
        part = jnp.dot(table[at, :], turned[...], preferred_element_type=F32)
        fourier[pl.ds(first, batch)] = part.astype(BF).reshape(batch, share, half)

        def start_one(j, carry):
            _, dz = offset(j // 2)
            peer = first + (z + dz + ZS) % ZS * 2 + (core + j) % 2

            @pl.when(peer != tile)
            def _():
                fourier_copy(peer).start()

            return carry

        lax.fori_loop(0, batch, start_one, 0)
        return carry

    lax.fori_loop(0, XS, transform, 0)
    spectra[slot_of(tile)] = fourier[tile]
    for way in range(2):
        drain(tables.at[pl.ds(0, 4 * unit)], table_recv.at[2 * way + 1])
        pass_tables(1, way).start()

    drain(spectra.at[pl.ds(0, TILES - 1)], fourier_recv.at[0])

    def wave_copy(peer):
        return remote(
            parts.at[peer], returned.at[tile], wave_send.at[0], wave_recv.at[x], peer
        )

    mixed = 2 * CHIPS
    keep_tables.wait()
    for copy in orders:
        copy.wait()
    own_slots = slots // LEVS
    for p in range(2):
        rows_in = spectra[p * CHIPS : (p + 1) * CHIPS].reshape(CHIPS * share, half)
        sorted_in[...] = jnp.dot(order[...], rows_in, preferred_element_type=F32).astype(BF)

        def one_slot(step, carry):
            there = step // own_slots
            there = (lev + there + there // 2 * (5 - 2 * there)) % LEVS
            slot = there * own_slots + step % own_slots
            at = pl.ds(pl.multiple_of(slot * mixed, mixed), mixed)
            legendre_at = tables[2 * slot + p]
            coefficient = lax.dot_general(
                sorted_in[at, :], legendre_at, NT, preferred_element_type=F32
            )
            scale = response[slot, p]
            spectrum = jnp.concatenate(
                [coefficient[:CHIPS] * scale, coefficient[CHIPS:] * scale], axis=0
            ).astype(BF)
            sorted_out[at, :] = jnp.dot(
                spectrum, legendre_at, preferred_element_type=F32
            ).astype(BF)
            return carry

        lax.fori_loop(0, slots - own_slots, one_slot, 0)
        if p == 0:
            drain(tables.at[pl.ds(0, own)], table_recv.at[4])
        lax.fori_loop(slots - own_slots, slots, one_slot, 0)

        def send_back(step, carry):
            first = ((x + step) % XS) * ZS
            at = pl.ds(pl.multiple_of(first * share, ZS * share), ZS * share)
            part = jnp.dot(back_order[at, :], sorted_out[...], preferred_element_type=F32)
            part = part.astype(BF).reshape(ZS, share, half)
            for j in range(ZS):
                parts[2 * (first + j) + p] = part[j]

            def start_one(j, carry):
                _, dz = offset(j)
                peer = 2 * (first + (z + dz + ZS) % ZS) + p

                @pl.when(peer != tile)
                def _():
                    wave_copy(peer).start()

                return carry

            lax.fori_loop(0, ZS, start_one, 0)
            return carry

        lax.fori_loop(0, XS, send_back, 0)
    returned[tile] = parts[tile]

    def inverse(step):
        there = (x + XS - step) % XS
        first = there * (2 * ZS)
        count = 2 * ZS - 1 if step == 0 else 2 * ZS
        drain(returned.at[pl.ds(0, count)], wave_recv.at[there])
        values = returned[pl.ds(first, 2 * ZS)].reshape(2 * ZS * share, half).T
        at = pl.ds(pl.multiple_of(first * share, 2 * ZS * share), 2 * ZS * share)
        for c in range(0, lons, 512):
            term = jnp.dot(values, table[at, c : c + 512], preferred_element_type=F32)
            if step == 0:
                wide[:, c : c + 512] = term
            else:
                wide[:, c : c + 512] += term

    for step in range(XS):
        inverse(step)

    def return_copy(q):
        return remote(
            sent_back.at[q], got_back.at[q], return_send.at[0], return_recv.at[q], partner
        )

    for q in range(quarters):
        sent_back[q] = wide[:, q * width : (q + 1) * width].astype(BF)
        return_copy(q).start()
    for q in range(quarters):
        at = slice(q * width, (q + 1) * width)
        return_copy(q).wait_recv()
        mine, theirs = wide[:, at], got_back[q].astype(F32)
        band[:half, at] = (mine + theirs).astype(BF)
        band[half:, at] = ((mine - theirs) * sign).astype(BF)

    def pair_copy(slot):
        dx, dz = offset(slot)
        there = chip_at(x - dx, z - dz)
        return remote(
            picked.at[slot],
            replies.at[chip],
            pair_send.at[0],
            pair_recv.at[0],
            2 * there + core,
        )

    lat_lane = lax.broadcasted_iota(jnp.int32, (rows, points), 1).astype(F32)

    def answer(group, carry):
        code = code_rows[group][:, :rows]
        lat = code // 16 % 1024
        lat = down_rows(lat // points, points) * points + down_rows(lat % points, points)
        one_hot = jnp.concatenate(
            [
                jnp.where(lat == lat_lane + float(c), 1.0, 0.0).astype(BF)
                for c in range(0, 2 * half, points)
            ],
            axis=1,
        )
        where = down_rows(code % 16, points).astype(BF)
        chosen = jnp.zeros((rows, points), BF)
        for b in range(0, per_row, 2):
            found = jnp.dot(
                one_hot, band[:, b * points : (b + 2) * points], preferred_element_type=F32
            ).astype(BF)
            for i in range(2):
                chosen = jnp.where(
                    where == float(b + i), found[:, i * points : (i + 1) * points], chosen
                )
        picked[pl.ds(group * GROUP, GROUP)] = chosen.reshape(GROUP, pairs, points)
        for j in range(GROUP):
            slot = group * GROUP + j

            @pl.when(slot != 0)
            def _():
                pair_copy(slot).start()

        return carry

    lax.fori_loop(0, CHIPS // GROUP, answer, 0)
    replies[chip] = picked[0]

    drain(replies.at[pl.ds(0, CHIPS - 1)], pair_recv.at[0])
    drain(picked.at[pl.ds(0, CHIPS - 1)], pair_send.at[0])
    drain(parts.at[pl.ds(0, TILES - 1)], wave_send.at[0])
    drain(sent_back, return_send.at[0])
    drain(fourier.at[pl.ds(0, TILES - 1)], fourier_send.at[0])
    drain(given, swap_send.at[0])
    drain(chunks.at[pl.ds(0, CHIPS - 1)], chunk_send.at[0])
    drain(code_in.at[pl.ds(0, CHIPS - 1)], code_send.at[0])
    drain(area_in.at[pl.ds(0, ZS - 1)], area_send.at[0])
    drain(area_in.at[pl.ds(0, CHIPS - ZS)], area_send.at[1])
    drain(area.at[pl.ds(0, LEVS - 1), core], area_send.at[2])
    drain(area.at[:, core], area_send.at[3])
    drain(tables.at[pl.ds(0, 3 * own)], table_send.at[0])


def regrid_call(
    cube_field,
    margin,
    pair_owner,
    pair_block,
    band_area,
    gauss_weight,
    wave_order,
    diffusion,
    legendre,
):
    pairs, points = pair_owner.shape[0], margin.shape[3]
    lat_dev, lons = band_area.shape
    room = -(-GROUP * pairs // points) * points
    width, lats = lons // LEVS, lat_dev * TILES
    half, slots, groups = lats // 2, wave_order.shape[0] // TILES, CHIPS // GROUP
    share, mixed = 2 * slots, CHIPS * 2 * slots
    order, back_order = slot_orders(slots)
    pack_rows, unmix = lat_orders(lat_dev)
    vmem = pl.BlockSpec(memory_space=pltpu.VMEM)
    smem = pl.BlockSpec(memory_space=pltpu.SMEM)
    anywhere = pl.BlockSpec(memory_space=pl.ANY)
    dma = pltpu.SemaphoreType.DMA
    return pl.pallas_call(
        regrid,
        out_shape=jax.ShapeDtypeStruct((CHIPS, pairs, points), BF),
        in_specs=[vmem] * 9 + [smem, vmem, anywhere, anywhere, anywhere],
        out_specs=vmem,
        scratch_shapes=[
            pltpu.VMEM((CHIPS, pairs, points), BF),
            pltpu.VMEM((GROUP, 1, room), jnp.int32),
            pltpu.VMEM((mixed, mixed), BF),
            pltpu.VMEM((mixed, mixed), BF),
            pltpu.VMEM((CHIPS, pairs, points), BF),
            pltpu.VMEM((CHIPS, 1, room), jnp.int32),
            pltpu.VMEM((groups, 1, room), jnp.int32),
            pltpu.VMEM((lats, lons), F32),
            pltpu.VMEM((PAD_LAT, width), F32),
            pltpu.VMEM((CHIPS, PAD_LAT, width), BF),
            pltpu.VMEM((LEVS, 2, half, width), BF),
            pltpu.VMEM((TILES * share, lons), BF),
            pltpu.VMEM((2 * slots, half, half), BF),
            pltpu.VMEM((slots, 2, CHIPS, half), F32),
            pltpu.VMEM((LEVS, half, width), BF),
            pltpu.VMEM((LEVS, half, width), BF),
            pltpu.VMEM((lons, half), BF),
            pltpu.VMEM((TILES, share, half), BF),
            pltpu.VMEM((TILES, share, half), BF),
            pltpu.VMEM((mixed, half), BF),
            pltpu.VMEM((mixed, half), BF),
            pltpu.VMEM((TILES, share, half), BF),
            pltpu.VMEM((TILES, share, half), BF),
            pltpu.VMEM((half, lons), F32),
            pltpu.VMEM((LEVS, half, width), BF),
            pltpu.VMEM((LEVS, half, width), BF),
            pltpu.VMEM((lats, lons), BF),
            pltpu.VMEM((CHIPS, pairs, points), BF),
            dma((1,)),
            dma((groups,)),
            dma((1,)),
            dma((groups,)),
            dma((4,)),
            dma((4,)),
            dma((1,)),
            dma((5,)),
            dma((1,)),
            dma((LEVS,)),
            dma((1,)),
            dma((1,)),
            dma((1,)),
            dma((XS,)),
            dma((1,)),
            dma((LEVS,)),
            dma((1,)),
            dma((1,)),
            dma((3,)),
        ],
        compiler_params=pltpu.CompilerParams(
            collective_id=0, has_side_effects=True, vmem_limit_bytes=VMEM_LIMIT
        ),
    )(
        cube_field,
        margin,
        pair_owner,
        pair_block,
        band_area,
        gauss_weight,
        pack_rows,
        unmix,
        wave_order,
        wave_order,
        diffusion,
        legendre,
        order,
        back_order,
    )


def slot_orders(slots):
    chip, part, slot = np.meshgrid(
        np.arange(CHIPS), np.arange(2), np.arange(slots), indexing="ij"
    )
    source = ((chip * 2 + part) * slots + slot).reshape(-1)
    target = ((slot * 2 + part) * CHIPS + chip).reshape(-1)
    order = np.zeros((source.size, source.size), np.float32)
    order[target, source] = 1.0
    return jnp.asarray(order, BF), jnp.asarray(order.T.copy(), BF)


def mixed_row(lat, lat_dev):
    tile = lat // lat_dev
    return tile % 2 * (CHIPS // 2 * lat_dev) + tile // 2 * lat_dev + lat % lat_dev


def lat_orders(lat_dev):
    quarter = CHIPS // 2 * lat_dev
    pack = np.zeros((2 * quarter, CHIPS * PAD_LAT), np.float32)
    for chip in range(CHIPS):
        for i in range(lat_dev):
            row = chip * lat_dev + i
            if chip >= CHIPS // 2:
                row = quarter + (CHIPS - 1 - chip) * lat_dev + lat_dev - 1 - i
            pack[row, chip * PAD_LAT + i] = 1.0
    unmix = np.zeros((2 * quarter, 2 * quarter), np.float32)
    lats = np.arange(2 * quarter)
    unmix[mixed_row(lats, lat_dev), lats] = 1.0
    return jnp.asarray(pack, BF), jnp.asarray(unmix, BF)


def shards(
    cube_field,
    margin,
    pair_owner,
    pair_block,
    cube_area,
    band_area,
    wave_order,
    legendre,
    gauss_weight,
    diffusion,
):
    fields, cell_count = cube_field.shape
    pairs, cells, points = margin.shape
    blocks = pairs // 2
    lat_dev, lons = band_area.shape
    per_row = lons // points
    lats = lat_dev * TILES
    half = lats // 2

    margin_q = margin.reshape(blocks, 2, cells, points)
    replies = regrid_call(
        cube_field,
        margin_q,
        pair_owner,
        pair_block,
        band_area,
        gauss_weight,
        wave_order,
        diffusion,
        legendre.reshape(-1, half, half),
    )

    cube = jnp.einsum(
        "fbkg,bkcg->fbc",
        replies.reshape(fields, blocks, 2, points),
        margin_q,
        preferred_element_type=F32,
    )
    cube = cube / cube_area.reshape(blocks, cells)[None]
    return cube.astype(BF).reshape(fields, cell_count)


def solution(mesh):
    in_specs = (
        P("lev", "tile"),
        P("tile", None, None),
        P("tile"),
        P("tile"),
        P("tile"),
        P("tile", None),
        P(),
        P(("tile", "lev"), None, None, None),
        P(),
        P(),
    )
    out_specs = P("lev", "tile")
    return jax.shard_map(shards, mesh=mesh, in_specs=in_specs, out_specs=out_specs, check_vma=False)
```

```python
import functools
import math

import jax
import jax.numpy as jnp
import numpy as np
from jax import lax
from jax.experimental import pallas as pl
from jax.experimental.pallas import tpu as pltpu
from jax.sharding import PartitionSpec as P

TRUNC = 766
MESH = pl.DeviceIdType.MESH
BF = jnp.bfloat16
F32 = jnp.float32
GROUP = 4
WINDOW = 3
PAD_LAT = 16
VMEM_LIMIT = 56 * 2**20
NT = (((1,), (1,)), ((), ()))
TN = (((0,), (0,)), ((), ()))

XS, ZS, LEVS = 4, 8, 4
CHIPS = XS * ZS
TILES = 2 * CHIPS


def place():
    tile = lax.axis_index("tile")
    return tile, tile // (2 * ZS), (tile // 2) % ZS, tile % 2


def chip_at(x, z):
    return ((x + XS) % XS) * ZS + (z + ZS) % ZS


def greet():
    tile, _, _, _ = place()
    lev = lax.axis_index("lev")
    barrier = pltpu.get_barrier_semaphore()

    def one(step, carry):
        peer = (tile + step) % TILES
        pl.semaphore_signal(barrier, inc=1, device_id=(peer, lev), device_id_type=MESH)
        return carry

    lax.fori_loop(1, TILES, one, 0)
    for step in range(1, LEVS):
        peer = (tile, (lev + step) % LEVS)
        pl.semaphore_signal(barrier, inc=1, device_id=peer, device_id_type=MESH)


def welcome():
    pl.semaphore_wait(pltpu.get_barrier_semaphore(), TILES - 1 + LEVS - 1)


def remote(src, dst, send, recv, peer, lev=None):
    return pltpu.make_async_remote_copy(
        src_ref=src,
        dst_ref=dst,
        send_sem=send,
        recv_sem=recv,
        device_id=(peer, lax.axis_index("lev") if lev is None else lev),
        device_id_type=MESH,
    )


def drain(ref, sem):
    pltpu.make_async_copy(ref, ref, sem).wait()


def offset(slot):
    k = slot % ZS
    return slot // ZS, (k + 1) // 2 * (2 * (k % 2) - 1)


def slot_of(tile):
    return (tile % 2) * CHIPS + tile // 2


def cos_sin(phase, turn):
    eighth = turn // 8
    octant = ((phase + eighth).astype(F32) * (4.0 / turn) + 0.5 / turn).astype(jnp.int32)
    angle = (phase - octant * (turn // 4)).astype(F32) * (2.0 * math.pi / turn)
    square = angle * angle
    cos = 1.0 + square * (
        -1 / 2 + square * (1 / 24 + square * (-1 / 720 + square * (1 / 40320)))
    )
    sin = angle * (
        1.0 + square * (-1 / 6 + square * (1 / 120 + square * (-1 / 5040 + square * (1 / 362880))))
    )
    odd = octant % 2 == 1
    base_c, base_s = jnp.where(odd, sin, cos), jnp.where(odd, cos, sin)
    flip_c = (octant == 1) | (octant == 2)
    flip_s = (octant == 2) | (octant == 3)
    return jnp.where(flip_c, -base_c, base_c), jnp.where(flip_s, -base_s, base_s)


def wrap(count, turn):
    return count - ((count.astype(F32) + 0.5) * (1.0 / turn)).astype(jnp.int32) * turn


def down_rows(row, width):
    first = lax.broadcasted_iota(jnp.int32, (16, row.shape[1]), 0) == 0
    spread = jnp.where(first, row.astype(F32), 0.0).astype(BF)
    return lax.dot_general(spread, jnp.ones((16, width), BF), TN, preferred_element_type=F32)


def regrid(
    cube_any,
    margin_any,
    pair_owner,
    pair_block,
    band_area,
    gauss_weight,
    pack_rows,
    unmix,
    wave_list,
    wave_order,
    diffusion,
    legendre,
    order_any,
    back_order_any,
    replies,
    cube_field,
    margin,
    chunks,
    codes,
    order,
    back_order,
    arrived,
    code_in,
    code_rows,
    totals,
    area_stage,
    area_in,
    area,
    table,
    tables,
    response,
    given,
    taken,
    turned,
    fourier,
    spectra,
    sorted_in,
    sorted_out,
    parts,
    returned,
    wide,
    sent_back,
    got_back,
    band,
    picked,
    chunk_send,
    chunk_recv,
    code_send,
    code_recv,
    area_send,
    area_recv,
    table_send,
    table_recv,
    swap_send,
    swap_recv,
    fourier_send,
    fourier_recv,
    wave_send,
    wave_recv,
    return_send,
    return_recv,
    pair_send,
    pair_recv,
    local_sem,
):
    tile, x, z, core = place()
    lev = lax.axis_index("lev")
    chip = tile // 2
    partner = tile + 1 - 2 * core
    lats, lons = totals.shape
    half = lats // 2
    pairs, points = arrived.shape[1:]
    rows = GROUP * pairs
    per_row = lons // points
    fields_in = [
        pltpu.make_async_copy(cube_any, cube_field, local_sem.at[3]),
        pltpu.make_async_copy(margin_any, margin, local_sem.at[4]),
    ]
    for copy in fields_in:
        copy.start()
    greet()
    orders = [
        pltpu.make_async_copy(order_any, order, local_sem.at[1]),
        pltpu.make_async_copy(back_order_any, back_order, local_sem.at[2]),
    ]
    for copy in orders:
        copy.start()

    lat_dev, width = band_area.shape[0], lons // LEVS
    owner, block = pair_owner[...].reshape(1, pairs), pair_block[...].reshape(1, pairs)
    lat = owner * lat_dev + block // per_row
    south_side = jnp.where(lat < half, 0, half)
    north_lat = jnp.where(lat < half, lat, lats - 1 - lat)
    code = (south_side + mixed_row(north_lat, lat_dev)) * 1024 + south_side + north_lat
    codes[...] = jnp.zeros_like(codes)
    codes[0, :, :pairs] = code * 16 + block % per_row
    code = jnp.broadcast_to(codes[0], (8, codes.shape[2]))
    for j in range(1, GROUP):
        codes[j] = pltpu.roll(code, j * pairs, 1)[:1]

    cells = margin.shape[2]
    span = 8 * cells
    pair_at = lax.broadcasted_iota(jnp.int32, (16, span), 0)
    block_at = lax.broadcasted_iota(jnp.int32, (16, span), 1) // cells
    masks = [jnp.where(2 * block_at + k == pair_at, 1.0, 0.0).astype(F32) for k in range(2)]

    def contribute(step, carry):
        field = cube_field[:, pl.ds(pl.multiple_of(step * span, span), span)].astype(F32)
        total = None
        for k in range(2):
            spread = (field[:, None, :] * masks[k][None]).reshape(CHIPS * 16, span).astype(BF)
            weights_k = margin[pl.ds(step * 8, 8), k].reshape(span, points)
            term = jnp.dot(spread, weights_k, preferred_element_type=F32)
            total = term if total is None else total + term
        at = pl.ds(pl.multiple_of(step * 16, 16), 16)
        chunks[:, at, :] = total.astype(BF).reshape(CHIPS, 16, points)
        return carry

    for copy in fields_in:
        copy.wait()
    lax.fori_loop(0, pairs // 16, contribute, 0)

    row = lax.broadcasted_iota(jnp.int32, (PAD_LAT, half), 0)
    own_lat = tile * lat_dev + row
    north_lat = jnp.where(own_lat < half, own_lat, lats - 1 - own_lat)
    found = lax.broadcasted_iota(jnp.int32, (PAD_LAT, half), 1) == north_lat
    weight = jnp.sum(jnp.where(found, gauss_weight[...].reshape(1, half), 0.0), axis=1, keepdims=True)
    area_stage[...] = jnp.ones_like(area_stage)
    area_stage[:lat_dev] = band_area[:, pl.ds(pl.multiple_of(lev * width, width), width)]
    real_row = lax.broadcasted_iota(jnp.int32, (PAD_LAT, width), 0) < lat_dev
    area_in[chip] = jnp.where(real_row, weight / area_stage[...], 0.0).astype(BF)

    welcome()

    def area_z(step):
        there = chip_at(x, z + step)
        here = area_in.at[chip]
        sems = area_send.at[0], area_recv.at[0]
        return remote(here, here, *sems, 2 * there + core)

    def area_x(step):
        there = chip_at(x + step, z)
        here = area_in.at[pl.ds(pl.multiple_of(x * ZS, ZS), ZS)]
        sems = area_send.at[1], area_recv.at[1]
        return remote(here, here, *sems, 2 * there + core)

    def area_y(step):
        here = area.at[lev, core]
        sems = area_send.at[2], area_recv.at[2]
        return remote(here, here, *sems, tile, (lev + step) % LEVS)

    def area_core(q):
        here = area.at[q, core]
        return remote(here, here, area_send.at[3], area_recv.at[3], partner)

    for step in range(1, ZS):
        area_z(step).start()

    own = legendre.shape[0]

    def own_tables(first, count):
        return tables.at[pl.ds(own * lev + first, count)]

    keep_tables = pltpu.make_async_copy(legendre, own_tables(0, own), local_sem.at[0])
    keep_tables.start()

    unit = own // 6
    give_order = (((0, 2), (2, 4)), ((3, 2), (5, 1), (0, 3)))

    def give_tables(piece, way):
        first, count = (unit * v for v in give_order[way][piece])
        return remote(
            legendre.at[pl.ds(first, count)],
            own_tables(first, count),
            table_send.at[0],
            table_recv.at[2 * way + min(piece, 1)],
            tile,
            (lev + (1, LEVS - 1)[way]) % LEVS,
        )

    def pass_tables(piece, way):
        from_lev = (lev + (LEVS - 1, 1)[way]) % LEVS
        first, count = ((0, 2), (2, 1))[piece]
        here = tables.at[pl.ds(own * from_lev + (3 * way + first) * unit, count * unit)]
        return remote(
            here,
            here,
            table_send.at[0],
            table_recv.at[4],
            tile,
            (lev + (1, LEVS - 1)[way]) % LEVS,
        )

    for way in range(2):
        give_tables(0, way).start()

    def code_copy(slot):
        dx, dz = offset(slot)
        there = chip_at(x + dx, z + dz)
        return remote(
            codes.at[slot % GROUP],
            code_in.at[slot],
            code_send.at[0],
            code_recv.at[slot // GROUP],
            2 * there + core,
        )

    def start_code(slot, carry):
        code_copy(slot).start()
        return carry

    lax.fori_loop(1, CHIPS, start_code, 0)
    code_in[0] = codes[0]

    def chunk_copy(slot):
        dx, dz = offset(slot)
        there = chip_at(x + dx, z + dz)
        return remote(
            chunks.at[there],
            arrived.at[slot],
            chunk_send.at[0],
            chunk_recv.at[slot // GROUP],
            2 * there + core,
        )

    def start_chunk(slot, carry):
        chunk_copy(slot).start()
        return carry

    lax.fori_loop(1, WINDOW * GROUP, start_chunk, 0)
    arrived[0] = chunks[chip]

    slots = response.shape[0]

    found = lax.broadcasted_iota(jnp.int32, (CHIPS, LEVS * CHIPS), 1) == (
        lax.broadcasted_iota(jnp.int32, (CHIPS, LEVS * CHIPS), 0) + CHIPS * lev
    )
    damping = diffusion[...].reshape(1, LEVS * CHIPS)
    damping = jnp.sum(jnp.where(found, damping, 0.0), axis=1, keepdims=True)

    def make_response(slot, carry):
        wave = wave_order[tile * slots + slot]
        doubled = jnp.where(wave == 0, 1.0, 2.0).astype(F32)
        for p in range(2):
            degree = wave + p + 2 * lax.broadcasted_iota(jnp.int32, (1, half), 1)
            growth = (degree * (degree + 1)).astype(F32) * (1.0 / (TRUNC * (TRUNC + 1)))
            value = doubled / (1.0 + damping * growth)
            response[slot, p] = jnp.where(degree <= TRUNC, value, 0.0)
        return carry

    lax.fori_loop(0, slots, make_response, 0)

    drain(area_in.at[pl.ds(0, ZS - 1)], area_recv.at[0])
    for step in range(1, XS):
        area_x(step).start()

    strip = points
    longitude = lax.broadcasted_iota(jnp.int32, (strip, points), 1)
    norm = 1.0 / math.sqrt(lons)
    waves = wave_list[...].reshape(1, TILES * slots).astype(F32)
    wave_at = lax.broadcasted_iota(jnp.int32, (strip, TILES * slots), 1)

    def make_rows(step, carry):
        at = pl.ds(pl.multiple_of(step * strip, strip), strip)
        row = step * strip + lax.broadcasted_iota(jnp.int32, (strip, 1), 0)
        part = row // slots % 2
        found = wave_at == row // (2 * slots) * slots + row % slots
        wave = jnp.sum(jnp.where(found, waves, 0.0), axis=1, keepdims=True).astype(jnp.int32)
        wave = jnp.broadcast_to(wave, (strip, points))
        cos, sin = cos_sin(wrap(wave * longitude + part * (lons // 4), lons), lons)
        cos, sin = cos * norm, sin * norm
        turn_c, turn_s = cos_sin(wrap(wave * points, lons), lons)
        for block in range(per_row):
            table[at, block * points : (block + 1) * points] = cos.astype(BF)
            cos, sin = cos * turn_c - sin * turn_s, sin * turn_c + cos * turn_s
        return carry

    lax.fori_loop(0, table.shape[0] // strip, make_rows, 0)

    drain(area_in.at[pl.ds(0, CHIPS - ZS)], area_recv.at[1])
    area[lev, core] = jnp.dot(
        pack_rows[...], area_in[...].reshape(CHIPS * PAD_LAT, -1), preferred_element_type=F32
    ).astype(BF)
    area_core(lev).start()
    for step in range(1, LEVS):
        area_y(step).start()
    for piece, way in ((1, 0), (1, 1), (2, 1)):
        give_tables(piece, way).start()

    lat_index = lax.broadcasted_iota(jnp.int32, (lats, rows), 0)

    def add_group(group, first):
        ahead = group + WINDOW

        @pl.when(ahead < CHIPS // GROUP)
        def _():
            for j in range(GROUP):
                chunk_copy(ahead * GROUP + j).start()

        from_slot = pl.ds(1, GROUP - 1) if first else pl.ds(group * GROUP, GROUP)
        drain(code_in.at[from_slot], code_recv.at[group])
        drain(arrived.at[from_slot], chunk_recv.at[group])
        code = code_in[group * GROUP]
        for j in range(1, GROUP):
            code = code + code_in[group * GROUP + j]
        code_rows[group] = code
        code = code[:, :rows]
        one_hot = jnp.where(lat_index == code // 16384, 1.0, 0.0).astype(BF)
        values = arrived[pl.ds(group * GROUP, GROUP)].reshape(rows, points)
        where = down_rows(code % 16, points).astype(BF)
        for b in range(0, per_row, 2):
            spread = jnp.concatenate(
                [jnp.where(where == float(b + i), values, jnp.zeros_like(values)) for i in range(2)],
                axis=1,
            )
            term = jnp.dot(one_hot, spread, preferred_element_type=F32)
            at = slice(b * points, (b + 2) * points)
            if first:
                totals[:, at] = term
            else:
                totals[:, at] += term

    def later_group(group, carry):
        add_group(group, False)
        return carry

    add_group(0, True)
    lax.fori_loop(1, 4, later_group, 0)
    drain(area.at[pl.ds(0, LEVS - 1), core], area_recv.at[2])
    for way in range(2):
        drain(tables.at[pl.ds(0, 2 * unit)], table_recv.at[2 * way])
        pass_tables(0, way).start()
    for step in range(1, LEVS):
        area_core((lev + step) % LEVS).start()
    lax.fori_loop(4, CHIPS // GROUP, later_group, 0)
    drain(area.at[:, core], area_recv.at[3])

    sign = (1 - 2 * core).astype(F32)
    quarters = LEVS

    def weights(q, side):
        at = slice(side * (half // 2), (side + 1) * (half // 2))
        return jnp.concatenate([area[q, c ^ side, at].astype(F32) for c in range(2)], axis=0)

    def swap_copy(q):
        return remote(
            given.at[q], taken.at[q], swap_send.at[0], swap_recv.at[q], partner
        )

    for q in range(quarters):
        at = slice(q * width, (q + 1) * width)
        north = totals[:half, at] * weights(q, 0)
        south = totals[half:, at] * weights(q, 1) * sign
        totals[:half, at] = north + south
        given[q] = (north - south).astype(BF)
        swap_copy(q).start()
    for q in range(quarters):
        at = slice(q * width, (q + 1) * width)
        swap_copy(q).wait_recv()
        folded = (totals[:half, at] + taken[q].astype(F32)).astype(BF)
        turned[at, :] = lax.dot_general(
            folded, unmix[...], TN, preferred_element_type=F32
        ).astype(BF)

    share = fourier.shape[1]
    batch = 2 * ZS

    def fourier_copy(peer):
        return remote(
            fourier.at[peer],
            spectra.at[slot_of(tile)],
            fourier_send.at[0],
            fourier_recv.at[0],
            peer,
        )

    def transform(step, carry):
        first = ((x + step) % XS) * batch
        at = pl.ds(pl.multiple_of(first * share, batch * share), batch * share)
        part = jnp.dot(table[at, :], turned[...], preferred_element_type=F32)
        fourier[pl.ds(first, batch)] = part.astype(BF).reshape(batch, share, half)

        def start_one(j, carry):
            _, dz = offset(j // 2)
            peer = first + (z + dz + ZS) % ZS * 2 + (core + j) % 2

            @pl.when(peer != tile)
            def _():
                fourier_copy(peer).start()

            return carry

        lax.fori_loop(0, batch, start_one, 0)
        return carry

    lax.fori_loop(0, XS, transform, 0)
    spectra[slot_of(tile)] = fourier[tile]
    for way in range(2):
        drain(tables.at[pl.ds(0, 4 * unit)], table_recv.at[2 * way + 1])
        pass_tables(1, way).start()

    drain(spectra.at[pl.ds(0, TILES - 1)], fourier_recv.at[0])

    def wave_copy(peer):
        return remote(
            parts.at[peer], returned.at[tile], wave_send.at[0], wave_recv.at[x], peer
        )

    mixed = 2 * CHIPS
    keep_tables.wait()
    for copy in orders:
        copy.wait()
    own_slots = slots // LEVS
    for p in range(2):
        rows_in = spectra[p * CHIPS : (p + 1) * CHIPS].reshape(CHIPS * share, half)
        sorted_in[...] = jnp.dot(order[...], rows_in, preferred_element_type=F32).astype(BF)

        def one_slot(step, carry):
            there = step // own_slots
            there = (lev + there + there // 2 * (5 - 2 * there)) % LEVS
            slot = there * own_slots + step % own_slots
            at = pl.ds(pl.multiple_of(slot * mixed, mixed), mixed)
            legendre_at = tables[2 * slot + p]
            coefficient = lax.dot_general(
                sorted_in[at, :], legendre_at, NT, preferred_element_type=F32
            )
            scale = response[slot, p]
            spectrum = jnp.concatenate(
                [coefficient[:CHIPS] * scale, coefficient[CHIPS:] * scale], axis=0
            ).astype(BF)
            sorted_out[at, :] = jnp.dot(
                spectrum, legendre_at, preferred_element_type=F32
            ).astype(BF)
            return carry

        lax.fori_loop(0, slots - own_slots, one_slot, 0, unroll=own_slots)
        if p == 0:
            drain(tables.at[pl.ds(0, own)], table_recv.at[4])
        lax.fori_loop(slots - own_slots, slots, one_slot, 0, unroll=own_slots)

        def send_back(step, carry):
            first = ((x + step) % XS) * ZS
            at = pl.ds(pl.multiple_of(first * share, ZS * share), ZS * share)
            part = jnp.dot(back_order[at, :], sorted_out[...], preferred_element_type=F32)
            part = part.astype(BF).reshape(ZS, share, half)
            for j in range(ZS):
                parts[2 * (first + j) + p] = part[j]

            def start_one(j, carry):
                _, dz = offset(j)
                peer = 2 * (first + (z + dz + ZS) % ZS) + p

                @pl.when(peer != tile)
                def _():
                    wave_copy(peer).start()

                return carry

            lax.fori_loop(0, ZS, start_one, 0)
            return carry

        lax.fori_loop(0, XS, send_back, 0)
    returned[tile] = parts[tile]

    def inverse(step):
        there = (x + XS - step) % XS
        first = there * (2 * ZS)
        count = 2 * ZS - 1 if step == 0 else 2 * ZS
        drain(returned.at[pl.ds(0, count)], wave_recv.at[there])
        values = returned[pl.ds(first, 2 * ZS)].reshape(2 * ZS * share, half).T
        at = pl.ds(pl.multiple_of(first * share, 2 * ZS * share), 2 * ZS * share)
        for c in range(0, lons, 512):
            term = jnp.dot(values, table[at, c : c + 512], preferred_element_type=F32)
            if step == 0:
                wide[:, c : c + 512] = term
            else:
                wide[:, c : c + 512] += term

    for step in range(XS):
        inverse(step)

    def return_copy(q):
        return remote(
            sent_back.at[q], got_back.at[q], return_send.at[0], return_recv.at[q], partner
        )

    for q in range(quarters):
        sent_back[q] = wide[:, q * width : (q + 1) * width].astype(BF)
        return_copy(q).start()
    for q in range(quarters):
        at = slice(q * width, (q + 1) * width)
        return_copy(q).wait_recv()
        mine, theirs = wide[:, at], got_back[q].astype(F32)
        band[:half, at] = (mine + theirs).astype(BF)
        band[half:, at] = ((mine - theirs) * sign).astype(BF)

    def pair_copy(slot):
        dx, dz = offset(slot)
        there = chip_at(x - dx, z - dz)
        return remote(
            picked.at[slot],
            replies.at[chip],
            pair_send.at[0],
            pair_recv.at[0],
            2 * there + core,
        )

    lat_lane = lax.broadcasted_iota(jnp.int32, (rows, points), 1).astype(F32)

    def answer(group, carry):
        code = code_rows[group][:, :rows]
        lat = code // 16 % 1024
        lat = down_rows(lat // points, points) * points + down_rows(lat % points, points)
        one_hot = jnp.concatenate(
            [
                jnp.where(lat == lat_lane + float(c), 1.0, 0.0).astype(BF)
                for c in range(0, 2 * half, points)
            ],
            axis=1,
        )
        where = down_rows(code % 16, points).astype(BF)
        chosen = jnp.zeros((rows, points), BF)
        for b in range(0, per_row, 2):
            found = jnp.dot(
                one_hot, band[:, b * points : (b + 2) * points], preferred_element_type=F32
            ).astype(BF)
            for i in range(2):
                chosen = jnp.where(
                    where == float(b + i), found[:, i * points : (i + 1) * points], chosen
                )
        picked[pl.ds(group * GROUP, GROUP)] = chosen.reshape(GROUP, pairs, points)
        for j in range(GROUP):
            slot = group * GROUP + j

            @pl.when(slot != 0)
            def _():
                pair_copy(slot).start()

        return carry

    lax.fori_loop(0, CHIPS // GROUP, answer, 0)
    replies[chip] = picked[0]

    drain(replies.at[pl.ds(0, CHIPS - 1)], pair_recv.at[0])
    drain(picked.at[pl.ds(0, CHIPS - 1)], pair_send.at[0])
    drain(parts.at[pl.ds(0, TILES - 1)], wave_send.at[0])
    drain(sent_back, return_send.at[0])
    drain(fourier.at[pl.ds(0, TILES - 1)], fourier_send.at[0])
    drain(given, swap_send.at[0])
    drain(chunks.at[pl.ds(0, CHIPS - 1)], chunk_send.at[0])
    drain(code_in.at[pl.ds(0, CHIPS - 1)], code_send.at[0])
    drain(area_in.at[pl.ds(0, ZS - 1)], area_send.at[0])
    drain(area_in.at[pl.ds(0, CHIPS - ZS)], area_send.at[1])
    drain(area.at[pl.ds(0, LEVS - 1), core], area_send.at[2])
    drain(area.at[:, core], area_send.at[3])
    drain(tables.at[pl.ds(0, 3 * own)], table_send.at[0])


def regrid_call(
    cube_field,
    margin,
    pair_owner,
    pair_block,
    band_area,
    gauss_weight,
    wave_order,
    diffusion,
    legendre,
):
    pairs, points = pair_owner.shape[0], margin.shape[3]
    lat_dev, lons = band_area.shape
    room = -(-GROUP * pairs // points) * points
    width, lats = lons // LEVS, lat_dev * TILES
    half, slots, groups = lats // 2, wave_order.shape[0] // TILES, CHIPS // GROUP
    share, mixed = 2 * slots, CHIPS * 2 * slots
    order, back_order = slot_orders(slots)
    pack_rows, unmix = lat_orders(lat_dev)
    vmem = pl.BlockSpec(memory_space=pltpu.VMEM)
    smem = pl.BlockSpec(memory_space=pltpu.SMEM)
    anywhere = pl.BlockSpec(memory_space=pl.ANY)
    dma = pltpu.SemaphoreType.DMA
    return pl.pallas_call(
        regrid,
        out_shape=jax.ShapeDtypeStruct((CHIPS, pairs, points), BF),
        in_specs=[anywhere] * 2 + [vmem] * 7 + [smem, vmem, anywhere, anywhere, anywhere],
        out_specs=vmem,
        scratch_shapes=[
            pltpu.VMEM(cube_field.shape, BF),
            pltpu.VMEM(margin.shape, BF),
            pltpu.VMEM((CHIPS, pairs, points), BF),
            pltpu.VMEM((GROUP, 1, room), jnp.int32),
            pltpu.VMEM((mixed, mixed), BF),
            pltpu.VMEM((mixed, mixed), BF),
            pltpu.VMEM((CHIPS, pairs, points), BF),
            pltpu.VMEM((CHIPS, 1, room), jnp.int32),
            pltpu.VMEM((groups, 1, room), jnp.int32),
            pltpu.VMEM((lats, lons), F32),
            pltpu.VMEM((PAD_LAT, width), F32),
            pltpu.VMEM((CHIPS, PAD_LAT, width), BF),
            pltpu.VMEM((LEVS, 2, half, width), BF),
            pltpu.VMEM((TILES * share, lons), BF),
            pltpu.VMEM((2 * slots, half, half), BF),
            pltpu.VMEM((slots, 2, CHIPS, half), F32),
            pltpu.VMEM((LEVS, half, width), BF),
            pltpu.VMEM((LEVS, half, width), BF),
            pltpu.VMEM((lons, half), BF),
            pltpu.VMEM((TILES, share, half), BF),
            pltpu.VMEM((TILES, share, half), BF),
            pltpu.VMEM((mixed, half), BF),
            pltpu.VMEM((mixed, half), BF),
            pltpu.VMEM((TILES, share, half), BF),
            pltpu.VMEM((TILES, share, half), BF),
            pltpu.VMEM((half, lons), F32),
            pltpu.VMEM((LEVS, half, width), BF),
            pltpu.VMEM((LEVS, half, width), BF),
            pltpu.VMEM((lats, lons), BF),
            pltpu.VMEM((CHIPS, pairs, points), BF),
            dma((1,)),
            dma((groups,)),
            dma((1,)),
            dma((groups,)),
            dma((4,)),
            dma((4,)),
            dma((1,)),
            dma((5,)),
            dma((1,)),
            dma((LEVS,)),
            dma((1,)),
            dma((1,)),
            dma((1,)),
            dma((XS,)),
            dma((1,)),
            dma((LEVS,)),
            dma((1,)),
            dma((1,)),
            dma((5,)),
        ],
        compiler_params=pltpu.CompilerParams(
            collective_id=0, has_side_effects=True, vmem_limit_bytes=VMEM_LIMIT
        ),
    )(
        cube_field,
        margin,
        pair_owner,
        pair_block,
        band_area,
        gauss_weight,
        pack_rows,
        unmix,
        wave_order,
        wave_order,
        diffusion,
        legendre,
        order,
        back_order,
    )


def slot_orders(slots):
    chip, part, slot = np.meshgrid(
        np.arange(CHIPS), np.arange(2), np.arange(slots), indexing="ij"
    )
    source = ((chip * 2 + part) * slots + slot).reshape(-1)
    target = ((slot * 2 + part) * CHIPS + chip).reshape(-1)
    order = np.zeros((source.size, source.size), np.float32)
    order[target, source] = 1.0
    return jnp.asarray(order, BF), jnp.asarray(order.T.copy(), BF)


def mixed_row(lat, lat_dev):
    tile = lat // lat_dev
    return tile % 2 * (CHIPS // 2 * lat_dev) + tile // 2 * lat_dev + lat % lat_dev


def lat_orders(lat_dev):
    quarter = CHIPS // 2 * lat_dev
    pack = np.zeros((2 * quarter, CHIPS * PAD_LAT), np.float32)
    for chip in range(CHIPS):
        for i in range(lat_dev):
            row = chip * lat_dev + i
            if chip >= CHIPS // 2:
                row = quarter + (CHIPS - 1 - chip) * lat_dev + lat_dev - 1 - i
            pack[row, chip * PAD_LAT + i] = 1.0
    unmix = np.zeros((2 * quarter, 2 * quarter), np.float32)
    lats = np.arange(2 * quarter)
    unmix[mixed_row(lats, lat_dev), lats] = 1.0
    return jnp.asarray(pack, BF), jnp.asarray(unmix, BF)


def shards(
    cube_field,
    margin,
    pair_owner,
    pair_block,
    cube_area,
    band_area,
    wave_order,
    legendre,
    gauss_weight,
    diffusion,
):
    fields, cell_count = cube_field.shape
    pairs, cells, points = margin.shape
    blocks = pairs // 2
    lat_dev, lons = band_area.shape
    per_row = lons // points
    lats = lat_dev * TILES
    half = lats // 2

    margin_q = margin.reshape(blocks, 2, cells, points)
    replies = regrid_call(
        cube_field,
        margin_q,
        pair_owner,
        pair_block,
        band_area,
        gauss_weight,
        wave_order,
        diffusion,
        legendre.reshape(-1, half, half),
    )

    cube = jnp.einsum(
        "fbkg,bkcg->fbc",
        replies.reshape(fields, blocks, 2, points),
        margin_q,
        preferred_element_type=F32,
    )
    cube = cube / cube_area.reshape(blocks, cells)[None]
    return cube.astype(BF).reshape(fields, cell_count)


def solution(mesh):
    in_specs = (
        P("lev", "tile"),
        P("tile", None, None),
        P("tile"),
        P("tile"),
        P("tile"),
        P("tile", None),
        P(),
        P(("tile", "lev"), None, None, None),
        P(),
        P(),
    )
    out_specs = P("lev", "tile")
    return jax.shard_map(shards, mesh=mesh, in_specs=in_specs, out_specs=out_specs, check_vma=False)
```

```python
import functools
import math

import jax
import jax.numpy as jnp
import numpy as np
from jax import lax
from jax.experimental import pallas as pl
from jax.experimental.pallas import tpu as pltpu
from jax.sharding import PartitionSpec as P

TRUNC = 766
MESH = pl.DeviceIdType.MESH
BF = jnp.bfloat16
F32 = jnp.float32
GROUP = 4
WINDOW = 3
PAD_LAT = 16
VMEM_LIMIT = 56 * 2**20
NT = (((1,), (1,)), ((), ()))
TN = (((0,), (0,)), ((), ()))

XS, ZS, LEVS = 4, 8, 4
CHIPS = XS * ZS
TILES = 2 * CHIPS


def place():
    tile = lax.axis_index("tile")
    return tile, tile // (2 * ZS), (tile // 2) % ZS, tile % 2


def chip_at(x, z):
    return ((x + XS) % XS) * ZS + (z + ZS) % ZS


def greet():
    tile, _, _, _ = place()
    lev = lax.axis_index("lev")
    barrier = pltpu.get_barrier_semaphore()

    def one(step, carry):
        peer = (tile + step) % TILES
        pl.semaphore_signal(barrier, inc=1, device_id=(peer, lev), device_id_type=MESH)
        return carry

    lax.fori_loop(1, TILES, one, 0)
    for step in range(1, LEVS):
        peer = (tile, (lev + step) % LEVS)
        pl.semaphore_signal(barrier, inc=1, device_id=peer, device_id_type=MESH)


def welcome():
    pl.semaphore_wait(pltpu.get_barrier_semaphore(), TILES - 1 + LEVS - 1)


def remote(src, dst, send, recv, peer, lev=None):
    return pltpu.make_async_remote_copy(
        src_ref=src,
        dst_ref=dst,
        send_sem=send,
        recv_sem=recv,
        device_id=(peer, lax.axis_index("lev") if lev is None else lev),
        device_id_type=MESH,
    )


def drain(ref, sem):
    pltpu.make_async_copy(ref, ref, sem).wait()


def offset(slot):
    k = slot % ZS
    return slot // ZS, (k + 1) // 2 * (2 * (k % 2) - 1)


def slot_of(tile):
    return (tile % 2) * CHIPS + tile // 2


def cos_sin(phase, turn):
    eighth = turn // 8
    octant = ((phase + eighth).astype(F32) * (4.0 / turn) + 0.5 / turn).astype(jnp.int32)
    angle = (phase - octant * (turn // 4)).astype(F32) * (2.0 * math.pi / turn)
    square = angle * angle
    cos = 1.0 + square * (
        -1 / 2 + square * (1 / 24 + square * (-1 / 720 + square * (1 / 40320)))
    )
    sin = angle * (
        1.0 + square * (-1 / 6 + square * (1 / 120 + square * (-1 / 5040 + square * (1 / 362880))))
    )
    odd = octant % 2 == 1
    base_c, base_s = jnp.where(odd, sin, cos), jnp.where(odd, cos, sin)
    flip_c = (octant == 1) | (octant == 2)
    flip_s = (octant == 2) | (octant == 3)
    return jnp.where(flip_c, -base_c, base_c), jnp.where(flip_s, -base_s, base_s)


def wrap(count, turn):
    return count - ((count.astype(F32) + 0.5) * (1.0 / turn)).astype(jnp.int32) * turn


def down_rows(row, width):
    first = lax.broadcasted_iota(jnp.int32, (16, row.shape[1]), 0) == 0
    spread = jnp.where(first, row.astype(F32), 0.0).astype(BF)
    return lax.dot_general(spread, jnp.ones((16, width), BF), TN, preferred_element_type=F32)


def regrid(
    cube_any,
    margin_any,
    pair_owner,
    pair_block,
    band_area,
    gauss_weight,
    pack_rows,
    unmix,
    wave_list,
    wave_order,
    diffusion,
    legendre,
    order_any,
    back_order_any,
    replies,
    cube_field,
    margin,
    chunks,
    codes,
    order,
    back_order,
    arrived,
    code_in,
    code_rows,
    totals,
    area_stage,
    area_in,
    area,
    table,
    tables,
    response,
    given,
    taken,
    turned,
    fourier,
    spectra,
    sorted_in,
    sorted_out,
    parts,
    returned,
    wide,
    sent_back,
    got_back,
    band,
    picked,
    chunk_send,
    chunk_recv,
    code_send,
    code_recv,
    area_send,
    area_recv,
    table_send,
    table_recv,
    swap_send,
    swap_recv,
    fourier_send,
    fourier_recv,
    wave_send,
    wave_recv,
    return_send,
    return_recv,
    pair_send,
    pair_recv,
    local_sem,
):
    tile, x, z, core = place()
    lev = lax.axis_index("lev")
    chip = tile // 2
    partner = tile + 1 - 2 * core
    lats, lons = totals.shape
    half = lats // 2
    pairs, points = arrived.shape[1:]
    rows = GROUP * pairs
    per_row = lons // points
    fields_in = [
        pltpu.make_async_copy(cube_any, cube_field, local_sem.at[3]),
        pltpu.make_async_copy(margin_any, margin, local_sem.at[4]),
    ]
    for copy in fields_in:
        copy.start()
    greet()
    orders = [
        pltpu.make_async_copy(order_any, order, local_sem.at[1]),
        pltpu.make_async_copy(back_order_any, back_order, local_sem.at[2]),
    ]
    for copy in orders:
        copy.start()

    lat_dev, width = band_area.shape[0], lons // LEVS
    owner, block = pair_owner[...].reshape(1, pairs), pair_block[...].reshape(1, pairs)
    lat = owner * lat_dev + block // per_row
    south_side = jnp.where(lat < half, 0, half)
    north_lat = jnp.where(lat < half, lat, lats - 1 - lat)
    code = (south_side + mixed_row(north_lat, lat_dev)) * 1024 + south_side + north_lat
    codes[...] = jnp.zeros_like(codes)
    codes[0, :, :pairs] = code * 16 + block % per_row
    code = jnp.broadcast_to(codes[0], (8, codes.shape[2]))
    for j in range(1, GROUP):
        codes[j] = pltpu.roll(code, j * pairs, 1)[:1]

    cells = margin.shape[2]
    span = 8 * cells
    pair_at = lax.broadcasted_iota(jnp.int32, (16, span), 0)
    block_at = lax.broadcasted_iota(jnp.int32, (16, span), 1) // cells
    masks = [jnp.where(2 * block_at + k == pair_at, 1.0, 0.0).astype(F32) for k in range(2)]

    def contribute(step, carry):
        field = cube_field[:, pl.ds(pl.multiple_of(step * span, span), span)].astype(F32)
        total = None
        for k in range(2):
            spread = (field[:, None, :] * masks[k][None]).reshape(CHIPS * 16, span).astype(BF)
            weights_k = margin[pl.ds(step * 8, 8), k].reshape(span, points)
            term = jnp.dot(spread, weights_k, preferred_element_type=F32)
            total = term if total is None else total + term
        at = pl.ds(pl.multiple_of(step * 16, 16), 16)
        chunks[:, at, :] = total.astype(BF).reshape(CHIPS, 16, points)
        return carry

    for copy in fields_in:
        copy.wait()
    lax.fori_loop(0, pairs // 16, contribute, 0, unroll=3)

    row = lax.broadcasted_iota(jnp.int32, (PAD_LAT, half), 0)
    own_lat = tile * lat_dev + row
    north_lat = jnp.where(own_lat < half, own_lat, lats - 1 - own_lat)
    found = lax.broadcasted_iota(jnp.int32, (PAD_LAT, half), 1) == north_lat
    weight = jnp.sum(jnp.where(found, gauss_weight[...].reshape(1, half), 0.0), axis=1, keepdims=True)
    area_stage[...] = jnp.ones_like(area_stage)
    area_stage[:lat_dev] = band_area[:, pl.ds(pl.multiple_of(lev * width, width), width)]
    real_row = lax.broadcasted_iota(jnp.int32, (PAD_LAT, width), 0) < lat_dev
    area_in[chip] = jnp.where(real_row, weight / area_stage[...], 0.0).astype(BF)

    welcome()

    def area_z(step):
        there = chip_at(x, z + step)
        here = area_in.at[chip]
        sems = area_send.at[0], area_recv.at[0]
        return remote(here, here, *sems, 2 * there + core)

    def area_x(step):
        there = chip_at(x + step, z)
        here = area_in.at[pl.ds(pl.multiple_of(x * ZS, ZS), ZS)]
        sems = area_send.at[1], area_recv.at[1]
        return remote(here, here, *sems, 2 * there + core)

    def area_y(step):
        here = area.at[lev, core]
        sems = area_send.at[2], area_recv.at[2]
        return remote(here, here, *sems, tile, (lev + step) % LEVS)

    def area_core(q):
        here = area.at[q, core]
        return remote(here, here, area_send.at[3], area_recv.at[3], partner)

    for step in range(1, ZS):
        area_z(step).start()

    own = legendre.shape[0]

    def own_tables(first, count):
        return tables.at[pl.ds(own * lev + first, count)]

    keep_tables = pltpu.make_async_copy(legendre, own_tables(0, own), local_sem.at[0])
    keep_tables.start()

    unit = own // 6
    give_order = (((0, 2), (2, 4)), ((3, 2), (5, 1), (0, 3)))

    def give_tables(piece, way):
        first, count = (unit * v for v in give_order[way][piece])
        return remote(
            legendre.at[pl.ds(first, count)],
            own_tables(first, count),
            table_send.at[0],
            table_recv.at[2 * way + min(piece, 1)],
            tile,
            (lev + (1, LEVS - 1)[way]) % LEVS,
        )

    def pass_tables(piece, way):
        from_lev = (lev + (LEVS - 1, 1)[way]) % LEVS
        first, count = ((0, 2), (2, 1))[piece]
        here = tables.at[pl.ds(own * from_lev + (3 * way + first) * unit, count * unit)]
        return remote(
            here,
            here,
            table_send.at[0],
            table_recv.at[4],
            tile,
            (lev + (1, LEVS - 1)[way]) % LEVS,
        )

    for way in range(2):
        give_tables(0, way).start()

    def code_copy(slot):
        dx, dz = offset(slot)
        there = chip_at(x + dx, z + dz)
        return remote(
            codes.at[slot % GROUP],
            code_in.at[slot],
            code_send.at[0],
            code_recv.at[slot // GROUP],
            2 * there + core,
        )

    def start_code(slot, carry):
        code_copy(slot).start()
        return carry

    lax.fori_loop(1, CHIPS, start_code, 0)
    code_in[0] = codes[0]

    def chunk_copy(slot):
        dx, dz = offset(slot)
        there = chip_at(x + dx, z + dz)
        return remote(
            chunks.at[there],
            arrived.at[slot],
            chunk_send.at[0],
            chunk_recv.at[slot // GROUP],
            2 * there + core,
        )

    def start_chunk(slot, carry):
        chunk_copy(slot).start()
        return carry

    lax.fori_loop(1, WINDOW * GROUP, start_chunk, 0)
    arrived[0] = chunks[chip]

    slots = response.shape[0]

    found = lax.broadcasted_iota(jnp.int32, (CHIPS, LEVS * CHIPS), 1) == (
        lax.broadcasted_iota(jnp.int32, (CHIPS, LEVS * CHIPS), 0) + CHIPS * lev
    )
    damping = diffusion[...].reshape(1, LEVS * CHIPS)
    damping = jnp.sum(jnp.where(found, damping, 0.0), axis=1, keepdims=True)

    def make_response(slot, carry):
        wave = wave_order[tile * slots + slot]
        doubled = jnp.where(wave == 0, 1.0, 2.0).astype(F32)
        for p in range(2):
            degree = wave + p + 2 * lax.broadcasted_iota(jnp.int32, (1, half), 1)
            growth = (degree * (degree + 1)).astype(F32) * (1.0 / (TRUNC * (TRUNC + 1)))
            value = doubled / (1.0 + damping * growth)
            response[slot, p] = jnp.where(degree <= TRUNC, value, 0.0)
        return carry

    lax.fori_loop(0, slots, make_response, 0, unroll=3)

    drain(area_in.at[pl.ds(0, ZS - 1)], area_recv.at[0])
    for step in range(1, XS):
        area_x(step).start()

    strip = points
    longitude = lax.broadcasted_iota(jnp.int32, (strip, points), 1)
    norm = 1.0 / math.sqrt(lons)
    waves = wave_list[...].reshape(1, TILES * slots).astype(F32)
    wave_at = lax.broadcasted_iota(jnp.int32, (strip, TILES * slots), 1)

    def make_rows(step, carry):
        at = pl.ds(pl.multiple_of(step * strip, strip), strip)
        row = step * strip + lax.broadcasted_iota(jnp.int32, (strip, 1), 0)
        part = row // slots % 2
        found = wave_at == row // (2 * slots) * slots + row % slots
        wave = jnp.sum(jnp.where(found, waves, 0.0), axis=1, keepdims=True).astype(jnp.int32)
        wave = jnp.broadcast_to(wave, (strip, points))
        cos, sin = cos_sin(wrap(wave * longitude + part * (lons // 4), lons), lons)
        cos, sin = cos * norm, sin * norm
        turn_c, turn_s = cos_sin(wrap(wave * points, lons), lons)
        for block in range(per_row):
            table[at, block * points : (block + 1) * points] = cos.astype(BF)
            cos, sin = cos * turn_c - sin * turn_s, sin * turn_c + cos * turn_s
        return carry

    lax.fori_loop(0, table.shape[0] // strip, make_rows, 0, unroll=3)

    drain(area_in.at[pl.ds(0, CHIPS - ZS)], area_recv.at[1])
    area[lev, core] = jnp.dot(
        pack_rows[...], area_in[...].reshape(CHIPS * PAD_LAT, -1), preferred_element_type=F32
    ).astype(BF)
    area_core(lev).start()
    for step in range(1, LEVS):
        area_y(step).start()
    for piece, way in ((1, 0), (1, 1), (2, 1)):
        give_tables(piece, way).start()

    lat_index = lax.broadcasted_iota(jnp.int32, (lats, rows), 0)

    def add_group(group, first):
        ahead = group + WINDOW

        @pl.when(ahead < CHIPS // GROUP)
        def _():
            for j in range(GROUP):
                chunk_copy(ahead * GROUP + j).start()

        from_slot = pl.ds(1, GROUP - 1) if first else pl.ds(group * GROUP, GROUP)
        drain(code_in.at[from_slot], code_recv.at[group])
        drain(arrived.at[from_slot], chunk_recv.at[group])
        code = code_in[group * GROUP]
        for j in range(1, GROUP):
            code = code + code_in[group * GROUP + j]
        code_rows[group] = code
        code = code[:, :rows]
        one_hot = jnp.where(lat_index == code // 16384, 1.0, 0.0).astype(BF)
        values = arrived[pl.ds(group * GROUP, GROUP)].reshape(rows, points)
        where = down_rows(code % 16, points).astype(BF)
        for b in range(0, per_row, 2):
            spread = jnp.concatenate(
                [jnp.where(where == float(b + i), values, jnp.zeros_like(values)) for i in range(2)],
                axis=1,
            )
            term = jnp.dot(one_hot, spread, preferred_element_type=F32)
            at = slice(b * points, (b + 2) * points)
            if first:
                totals[:, at] = term
            else:
                totals[:, at] += term

    def later_group(group, carry):
        add_group(group, False)
        return carry

    add_group(0, True)
    lax.fori_loop(1, 4, later_group, 0)
    drain(area.at[pl.ds(0, LEVS - 1), core], area_recv.at[2])
    for way in range(2):
        drain(tables.at[pl.ds(0, 2 * unit)], table_recv.at[2 * way])
        pass_tables(0, way).start()
    for step in range(1, LEVS):
        area_core((lev + step) % LEVS).start()
    lax.fori_loop(4, CHIPS // GROUP, later_group, 0)
    drain(area.at[:, core], area_recv.at[3])

    sign = (1 - 2 * core).astype(F32)
    quarters = LEVS

    def weights(q, side):
        at = slice(side * (half // 2), (side + 1) * (half // 2))
        return jnp.concatenate([area[q, c ^ side, at].astype(F32) for c in range(2)], axis=0)

    def swap_copy(q):
        return remote(
            given.at[q], taken.at[q], swap_send.at[0], swap_recv.at[q], partner
        )

    for q in range(quarters):
        at = slice(q * width, (q + 1) * width)
        north = totals[:half, at] * weights(q, 0)
        south = totals[half:, at] * weights(q, 1) * sign
        totals[:half, at] = north + south
        given[q] = (north - south).astype(BF)
        swap_copy(q).start()
    for q in range(quarters):
        at = slice(q * width, (q + 1) * width)
        swap_copy(q).wait_recv()
        folded = (totals[:half, at] + taken[q].astype(F32)).astype(BF)
        turned[at, :] = lax.dot_general(
            folded, unmix[...], TN, preferred_element_type=F32
        ).astype(BF)

    share = fourier.shape[1]
    batch = 2 * ZS

    def fourier_copy(peer):
        return remote(
            fourier.at[peer],
            spectra.at[slot_of(tile)],
            fourier_send.at[0],
            fourier_recv.at[0],
            peer,
        )

    def transform(step, carry):
        first = ((x + step) % XS) * batch
        at = pl.ds(pl.multiple_of(first * share, batch * share), batch * share)
        part = jnp.dot(table[at, :], turned[...], preferred_element_type=F32)
        fourier[pl.ds(first, batch)] = part.astype(BF).reshape(batch, share, half)

        def start_one(j, carry):
            _, dz = offset(j // 2)
            peer = first + (z + dz + ZS) % ZS * 2 + (core + j) % 2

            @pl.when(peer != tile)
            def _():
                fourier_copy(peer).start()

            return carry

        lax.fori_loop(0, batch, start_one, 0)
        return carry

    lax.fori_loop(0, XS, transform, 0)
    spectra[slot_of(tile)] = fourier[tile]
    for way in range(2):
        drain(tables.at[pl.ds(0, 4 * unit)], table_recv.at[2 * way + 1])
        pass_tables(1, way).start()

    drain(spectra.at[pl.ds(0, TILES - 1)], fourier_recv.at[0])

    def wave_copy(peer):
        return remote(
            parts.at[peer], returned.at[tile], wave_send.at[0], wave_recv.at[x], peer
        )

    mixed = 2 * CHIPS
    keep_tables.wait()
    for copy in orders:
        copy.wait()
    own_slots = slots // LEVS
    for p in range(2):
        rows_in = spectra[p * CHIPS : (p + 1) * CHIPS].reshape(CHIPS * share, half)
        sorted_in[...] = jnp.dot(order[...], rows_in, preferred_element_type=F32).astype(BF)

        def one_slot(step, carry):
            there = step // own_slots
            there = (lev + there + there // 2 * (5 - 2 * there)) % LEVS
            slot = there * own_slots + step % own_slots
            at = pl.ds(pl.multiple_of(slot * mixed, mixed), mixed)
            legendre_at = tables[2 * slot + p]
            coefficient = lax.dot_general(
                sorted_in[at, :], legendre_at, NT, preferred_element_type=F32
            )
            scale = response[slot, p]
            spectrum = jnp.concatenate(
                [coefficient[:CHIPS] * scale, coefficient[CHIPS:] * scale], axis=0
            ).astype(BF)
            sorted_out[at, :] = jnp.dot(
                spectrum, legendre_at, preferred_element_type=F32
            ).astype(BF)
            return carry

        lax.fori_loop(0, slots - own_slots, one_slot, 0, unroll=own_slots)
        if p == 0:
            drain(tables.at[pl.ds(0, own)], table_recv.at[4])
        lax.fori_loop(slots - own_slots, slots, one_slot, 0, unroll=own_slots)

        def send_back(step, carry):
            first = ((x + step) % XS) * ZS
            at = pl.ds(pl.multiple_of(first * share, ZS * share), ZS * share)
            part = jnp.dot(back_order[at, :], sorted_out[...], preferred_element_type=F32)
            part = part.astype(BF).reshape(ZS, share, half)
            for j in range(ZS):
                parts[2 * (first + j) + p] = part[j]

            def start_one(j, carry):
                _, dz = offset(j)
                peer = 2 * (first + (z + dz + ZS) % ZS) + p

                @pl.when(peer != tile)
                def _():
                    wave_copy(peer).start()

                return carry

            lax.fori_loop(0, ZS, start_one, 0)
            return carry

        lax.fori_loop(0, XS, send_back, 0)
    returned[tile] = parts[tile]

    def inverse(step):
        there = (x + XS - step) % XS
        first = there * (2 * ZS)
        count = 2 * ZS - 1 if step == 0 else 2 * ZS
        drain(returned.at[pl.ds(0, count)], wave_recv.at[there])
        values = returned[pl.ds(first, 2 * ZS)].reshape(2 * ZS * share, half).T
        at = pl.ds(pl.multiple_of(first * share, 2 * ZS * share), 2 * ZS * share)
        for c in range(0, lons, 512):
            term = jnp.dot(values, table[at, c : c + 512], preferred_element_type=F32)
            if step == 0:
                wide[:, c : c + 512] = term
            else:
                wide[:, c : c + 512] += term

    for step in range(XS):
        inverse(step)

    def return_copy(q):
        return remote(
            sent_back.at[q], got_back.at[q], return_send.at[0], return_recv.at[q], partner
        )

    for q in range(quarters):
        sent_back[q] = wide[:, q * width : (q + 1) * width].astype(BF)
        return_copy(q).start()
    for q in range(quarters):
        at = slice(q * width, (q + 1) * width)
        return_copy(q).wait_recv()
        mine, theirs = wide[:, at], got_back[q].astype(F32)
        band[:half, at] = (mine + theirs).astype(BF)
        band[half:, at] = ((mine - theirs) * sign).astype(BF)

    def pair_copy(slot):
        dx, dz = offset(slot)
        there = chip_at(x - dx, z - dz)
        return remote(
            picked.at[slot],
            replies.at[chip],
            pair_send.at[0],
            pair_recv.at[0],
            2 * there + core,
        )

    lat_lane = lax.broadcasted_iota(jnp.int32, (rows, points), 1).astype(F32)

    def answer(group, carry):
        code = code_rows[group][:, :rows]
        lat = code // 16 % 1024
        lat = down_rows(lat // points, points) * points + down_rows(lat % points, points)
        one_hot = jnp.concatenate(
            [
                jnp.where(lat == lat_lane + float(c), 1.0, 0.0).astype(BF)
                for c in range(0, 2 * half, points)
            ],
            axis=1,
        )
        where = down_rows(code % 16, points).astype(BF)
        chosen = jnp.zeros((rows, points), BF)
        for b in range(0, per_row, 2):
            found = jnp.dot(
                one_hot, band[:, b * points : (b + 2) * points], preferred_element_type=F32
            ).astype(BF)
            for i in range(2):
                chosen = jnp.where(
                    where == float(b + i), found[:, i * points : (i + 1) * points], chosen
                )
        picked[pl.ds(group * GROUP, GROUP)] = chosen.reshape(GROUP, pairs, points)
        for j in range(GROUP):
            slot = group * GROUP + j

            @pl.when(slot != 0)
            def _():
                pair_copy(slot).start()

        return carry

    lax.fori_loop(0, CHIPS // GROUP, answer, 0)
    replies[chip] = picked[0]

    drain(replies.at[pl.ds(0, CHIPS - 1)], pair_recv.at[0])
    drain(picked.at[pl.ds(0, CHIPS - 1)], pair_send.at[0])
    drain(parts.at[pl.ds(0, TILES - 1)], wave_send.at[0])
    drain(sent_back, return_send.at[0])
    drain(fourier.at[pl.ds(0, TILES - 1)], fourier_send.at[0])
    drain(given, swap_send.at[0])
    drain(chunks.at[pl.ds(0, CHIPS - 1)], chunk_send.at[0])
    drain(code_in.at[pl.ds(0, CHIPS - 1)], code_send.at[0])
    drain(area_in.at[pl.ds(0, ZS - 1)], area_send.at[0])
    drain(area_in.at[pl.ds(0, CHIPS - ZS)], area_send.at[1])
    drain(area.at[pl.ds(0, LEVS - 1), core], area_send.at[2])
    drain(area.at[:, core], area_send.at[3])
    drain(tables.at[pl.ds(0, 3 * own)], table_send.at[0])


def regrid_call(
    cube_field,
    margin,
    pair_owner,
    pair_block,
    band_area,
    gauss_weight,
    wave_order,
    diffusion,
    legendre,
):
    pairs, points = pair_owner.shape[0], margin.shape[3]
    lat_dev, lons = band_area.shape
    room = -(-GROUP * pairs // points) * points
    width, lats = lons // LEVS, lat_dev * TILES
    half, slots, groups = lats // 2, wave_order.shape[0] // TILES, CHIPS // GROUP
    share, mixed = 2 * slots, CHIPS * 2 * slots
    order, back_order = slot_orders(slots)
    pack_rows, unmix = lat_orders(lat_dev)
    vmem = pl.BlockSpec(memory_space=pltpu.VMEM)
    smem = pl.BlockSpec(memory_space=pltpu.SMEM)
    anywhere = pl.BlockSpec(memory_space=pl.ANY)
    dma = pltpu.SemaphoreType.DMA
    return pl.pallas_call(
        regrid,
        out_shape=jax.ShapeDtypeStruct((CHIPS, pairs, points), BF),
        in_specs=[anywhere] * 2 + [vmem] * 7 + [smem, vmem, anywhere, anywhere, anywhere],
        out_specs=vmem,
        scratch_shapes=[
            pltpu.VMEM(cube_field.shape, BF),
            pltpu.VMEM(margin.shape, BF),
            pltpu.VMEM((CHIPS, pairs, points), BF),
            pltpu.VMEM((GROUP, 1, room), jnp.int32),
            pltpu.VMEM((mixed, mixed), BF),
            pltpu.VMEM((mixed, mixed), BF),
            pltpu.VMEM((CHIPS, pairs, points), BF),
            pltpu.VMEM((CHIPS, 1, room), jnp.int32),
            pltpu.VMEM((groups, 1, room), jnp.int32),
            pltpu.VMEM((lats, lons), F32),
            pltpu.VMEM((PAD_LAT, width), F32),
            pltpu.VMEM((CHIPS, PAD_LAT, width), BF),
            pltpu.VMEM((LEVS, 2, half, width), BF),
            pltpu.VMEM((TILES * share, lons), BF),
            pltpu.VMEM((2 * slots, half, half), BF),
            pltpu.VMEM((slots, 2, CHIPS, half), F32),
            pltpu.VMEM((LEVS, half, width), BF),
            pltpu.VMEM((LEVS, half, width), BF),
            pltpu.VMEM((lons, half), BF),
            pltpu.VMEM((TILES, share, half), BF),
            pltpu.VMEM((TILES, share, half), BF),
            pltpu.VMEM((mixed, half), BF),
            pltpu.VMEM((mixed, half), BF),
            pltpu.VMEM((TILES, share, half), BF),
            pltpu.VMEM((TILES, share, half), BF),
            pltpu.VMEM((half, lons), F32),
            pltpu.VMEM((LEVS, half, width), BF),
            pltpu.VMEM((LEVS, half, width), BF),
            pltpu.VMEM((lats, lons), BF),
            pltpu.VMEM((CHIPS, pairs, points), BF),
            dma((1,)),
            dma((groups,)),
            dma((1,)),
            dma((groups,)),
            dma((4,)),
            dma((4,)),
            dma((1,)),
            dma((5,)),
            dma((1,)),
            dma((LEVS,)),
            dma((1,)),
            dma((1,)),
            dma((1,)),
            dma((XS,)),
            dma((1,)),
            dma((LEVS,)),
            dma((1,)),
            dma((1,)),
            dma((5,)),
        ],
        compiler_params=pltpu.CompilerParams(
            collective_id=0, has_side_effects=True, vmem_limit_bytes=VMEM_LIMIT
        ),
    )(
        cube_field,
        margin,
        pair_owner,
        pair_block,
        band_area,
        gauss_weight,
        pack_rows,
        unmix,
        wave_order,
        wave_order,
        diffusion,
        legendre,
        order,
        back_order,
    )


def slot_orders(slots):
    chip, part, slot = np.meshgrid(
        np.arange(CHIPS), np.arange(2), np.arange(slots), indexing="ij"
    )
    source = ((chip * 2 + part) * slots + slot).reshape(-1)
    target = ((slot * 2 + part) * CHIPS + chip).reshape(-1)
    order = np.zeros((source.size, source.size), np.float32)
    order[target, source] = 1.0
    return jnp.asarray(order, BF), jnp.asarray(order.T.copy(), BF)


def mixed_row(lat, lat_dev):
    tile = lat // lat_dev
    return tile % 2 * (CHIPS // 2 * lat_dev) + tile // 2 * lat_dev + lat % lat_dev


def lat_orders(lat_dev):
    quarter = CHIPS // 2 * lat_dev
    pack = np.zeros((2 * quarter, CHIPS * PAD_LAT), np.float32)
    for chip in range(CHIPS):
        for i in range(lat_dev):
            row = chip * lat_dev + i
            if chip >= CHIPS // 2:
                row = quarter + (CHIPS - 1 - chip) * lat_dev + lat_dev - 1 - i
            pack[row, chip * PAD_LAT + i] = 1.0
    unmix = np.zeros((2 * quarter, 2 * quarter), np.float32)
    lats = np.arange(2 * quarter)
    unmix[mixed_row(lats, lat_dev), lats] = 1.0
    return jnp.asarray(pack, BF), jnp.asarray(unmix, BF)


def shards(
    cube_field,
    margin,
    pair_owner,
    pair_block,
    cube_area,
    band_area,
    wave_order,
    legendre,
    gauss_weight,
    diffusion,
):
    fields, cell_count = cube_field.shape
    pairs, cells, points = margin.shape
    blocks = pairs // 2
    lat_dev, lons = band_area.shape
    per_row = lons // points
    lats = lat_dev * TILES
    half = lats // 2

    margin_q = margin.reshape(blocks, 2, cells, points)
    replies = regrid_call(
        cube_field,
        margin_q,
        pair_owner,
        pair_block,
        band_area,
        gauss_weight,
        wave_order,
        diffusion,
        legendre.reshape(-1, half, half),
    )

    cube = jnp.einsum(
        "fbkg,bkcg->fbc",
        replies.reshape(fields, blocks, 2, points),
        margin_q,
        preferred_element_type=F32,
    )
    cube = cube / cube_area.reshape(blocks, cells)[None]
    return cube.astype(BF).reshape(fields, cell_count)


def solution(mesh):
    in_specs = (
        P("lev", "tile"),
        P("tile", None, None),
        P("tile"),
        P("tile"),
        P("tile"),
        P("tile", None),
        P(),
        P(("tile", "lev"), None, None, None),
        P(),
        P(),
    )
    out_specs = P("lev", "tile")
    return jax.shard_map(shards, mesh=mesh, in_specs=in_specs, out_specs=out_specs, check_vma=False)
```
